32 devices in a mesh: fsdp: 16 (over z, y, core), tp: 2 (over x).
Axes of the slice: x: 2, y: 2, z: 4, core: 2. Of those that a mesh axis runs over, the one named last changes fastest.
Arguments:
- hidden: bfloat16 [16384, 1024], P(('fsdp', 'tp')), may hold values from -6 to 6
- norm_gain: bfloat16 [1024], P('fsdp'), may hold values from 0.5 to 1.5
- weight_gate: bfloat16 [1024, 2048], P('fsdp', 'tp'), may hold values from -0.1875 to 0.1875
- weight_inner: bfloat16 [1024, 2048], P('fsdp', 'tp'), may hold values from -0.1875 to 0.1875
- weight_shared: bfloat16 [1024, 256], P('fsdp'), may hold values from -0.1875 to 0.1875
- weight_step: bfloat16 [1024, 32], P('fsdp', 'tp'), may hold values from -0.1875 to 0.1875
- filter_inner: bfloat16 [4, 2048], P(None, 'tp'), may hold values from -0.5 to 0.5
- bias_inner: bfloat16 [2048], P('tp'), may hold values from -0.5 to 0.5
- filter_shared: bfloat16 [4, 256], replicated, may hold values from -0.5 to 0.5
- bias_shared: bfloat16 [256], replicated, may hold values from -0.5 to 0.5
- step_bias: bfloat16 [32], P('tp'), may hold values from -8 to -4
- log_rate: bfloat16 [32], P('tp'), may hold values from -1 to 2
- skip_gain: bfloat16 [32], P('tp'), may hold values from 0.5 to 1.5
- gate_gain: bfloat16 [2048], P('tp'), may hold values from 0.5 to 1.5
- weight_out: bfloat16 [1024, 2048], P('fsdp', 'tp'), may hold values from -0.125 to 0.125
- segments: int32 [16, 1024], P('fsdp'), may hold values from 0 to 6, as said below
- cotangent: bfloat16 [16384, 1024], P(('fsdp', 'tp')), may hold values from -6 to 6
Outputs:
- layer_out: bfloat16 [16384, 1024], P(('fsdp', 'tp'))
- grad_hidden: float32 [16384, 1024], P(('fsdp', 'tp'))
- grad_norm_gain: float32 [1024], P('fsdp')
- grad_weight_gate: float32 [1024, 2048], P('fsdp', 'tp')
- grad_weight_inner: float32 [1024, 2048], P('fsdp', 'tp')
- grad_weight_shared: float32 [1024, 256], P('fsdp')
- grad_weight_step: float32 [1024, 32], P('fsdp', 'tp')
- grad_filter_inner: float32 [4, 2048], P(None, 'tp')
- grad_bias_inner: float32 [2048], P('tp')
- grad_filter_shared: float32 [4, 256], replicated
- grad_bias_shared: float32 [256], replicated
- grad_step_bias: float32 [32], P('tp')
- grad_log_rate: float32 [32], P('tp')
- grad_skip_gain: float32 [32], P('tp')
- grad_gate_gain: float32 [2048], P('tp')
- grad_weight_out: float32 [1024, 2048], P('fsdp', 'tp')
The draws below stay inside these ranges and needn't reach their ends.
Inputs may be any that keep to these rules, and one draw needn't show every extreme that they name: `segments`: in each sequence the numbers start at 0, never fall, and rise by one where a new document begins; every document has 200 to 2000 positions, except the first and the last of a sequence, which the sequence's ends may cut.
All inputs are finite; a program needn't handle non-finite values.
Results may differ from the reference program's by a relative error of at most 0.014.
Values may be sent and summed in bfloat16 or wider, within the bound.
No kernel may reach another device: no remote copies, remote signals or barrier semaphores. Data moves between devices by JAX's collectives and lax.ppermute only.
A program may use at most 192 MiB of HBM per device.

```python
import jax
import jax.numpy as jnp
from jax import lax

D = 1024
INNER = 2048
NH = 32
NS = 128
KC = 4
BLOCK = 256
DOC_MIN = 200
DOC_MAX = 2000
LEN = 1024
NSEQ = 16
TOKENS = 16384


def draw_segments(key, part):
    key = jax.random.fold_in(key, 11)
    first_key, length_key, pick_key = jax.random.split(key, 3)
    count = LEN // DOC_MIN + 2
    firsts = jax.random.randint(first_key, (NSEQ, 1), 1, DOC_MAX + 1)
    spans = jax.random.randint(length_key, (NSEQ, count - 1), DOC_MIN, DOC_MAX + 1)
    picks = jax.random.permutation(pick_key, NSEQ)
    whole_row = picks[0]
    dense_row = picks[1]
    row_ids = jnp.arange(NSEQ)[:, None]
    firsts = jnp.where(row_ids == whole_row, LEN, jnp.where(row_ids == dense_row, 1, firsts))
    spans = jnp.where(row_ids == dense_row, DOC_MIN, spans)
    starts = jnp.concatenate([firsts, firsts + jnp.cumsum(spans, axis=1)], axis=1)
    places = jnp.arange(LEN)
    return jnp.sum((places[None, :, None] >= starts[:, None, :]).astype(jnp.int32), axis=2)


def shard_levels(own_key, dims, cuts, smallest, high):
    factor_of, own = 1.0, jax.random.fold_in(own_key, 6)
    for position, shards_of in cuts:
        draws = jnp.exp(jax.random.uniform(jax.random.fold_in(own, position), (shards_of,), jnp.float32, smallest / len(cuts), high / len(cuts)))
        factor_of = factor_of * jnp.repeat(draws, dims[position] // shards_of).reshape([-1 if axis == position else 1 for axis in range(len(dims))])
    return factor_of


def scatter_about(stream_key, shape, spread, limit, shards=(), held_as=jnp.bfloat16):
    values = jax.random.normal(stream_key, shape, jnp.float32) * spread
    if len(shards) > 0:
        values = shard_levels(stream_key, shape, shards, -0.22, 0.18) * values
    return jnp.clip(values, min=-limit, max=limit).astype(held_as)


def setup_inputs(seed: int = 0) -> dict:
    splits = jax.random.split(jax.random.key(seed), 18)
    return {
        "hidden": scatter_about(splits[0], (TOKENS, D), 1.0, 6.0, ((0, 32),)),
        "norm_gain": jnp.clip(1.0 + 0.1 * jax.random.normal(splits[1], (D,), jnp.float32), 0.5, 1.5).astype(jnp.bfloat16),
        "weight_gate": scatter_about(splits[2], (D, INNER), D ** -0.5, 0.1875, ((0, 16), (1, 2))),
        "weight_inner": scatter_about(splits[3], (D, INNER), D ** -0.5, 0.1875, ((0, 16), (1, 2))),
        "weight_shared": scatter_about(splits[4], (D, 2 * NS), D ** -0.5, 0.1875, ((0, 16),)),
        "weight_step": scatter_about(splits[5], (D, NH), D ** -0.5, 0.1875, ((0, 16), (1, 2))),
        "filter_inner": jnp.clip(jax.random.uniform(splits[6], (KC, INNER), jnp.float32, -0.5, 0.5) * shard_levels(splits[6], (KC, INNER), ((1, 2),), -0.4, 0.0), -0.5, 0.5).astype(jnp.bfloat16),
        "bias_inner": jnp.clip(jax.random.uniform(splits[7], (INNER,), jnp.float32, -0.5, 0.5) * shard_levels(splits[7], (INNER,), ((0, 2),), -0.4, 0.0), -0.5, 0.5).astype(jnp.bfloat16),
        "filter_shared": jnp.clip(jax.random.uniform(splits[8], (KC, 2 * NS), jnp.float32, -0.5, 0.5), -0.5, 0.5).astype(jnp.bfloat16),
        "bias_shared": jnp.clip(jax.random.uniform(splits[9], (2 * NS,), jnp.float32, -0.5, 0.5), -0.5, 0.5).astype(jnp.bfloat16),
        "step_bias": jnp.clip(-8.0 + 4.0 * jax.random.uniform(splits[10], (NH,), jnp.float32) ** shard_levels(splits[10], (NH,), ((0, 2),), -0.2, 0.2), -8.0, -4.0).astype(jnp.bfloat16),
        "log_rate": jnp.clip(-1.0 + 3.0 * jax.random.uniform(splits[11], (NH,), jnp.float32) ** shard_levels(splits[11], (NH,), ((0, 2),), -0.2, 0.2), -1.0, 2.0).astype(jnp.bfloat16),
        "skip_gain": jnp.clip(0.5 + 1.0 * jax.random.uniform(splits[12], (NH,), jnp.float32) ** shard_levels(splits[12], (NH,), ((0, 2),), -0.2, 0.2), 0.5, 1.5).astype(jnp.bfloat16),
        "gate_gain": jnp.clip(1.0 + 0.1 * jax.random.normal(splits[13], (INNER,), jnp.float32), 0.5, 1.5).astype(jnp.bfloat16),
        "weight_out": scatter_about(splits[14], (D, INNER), INNER ** -0.5, 0.125, ((0, 16), (1, 2))),
        "segments": draw_segments(jax.random.fold_in(splits[17], 71), 0),
        "cotangent": scatter_about(splits[16], (TOKENS, D), 1.0, 6.0, ((0, 32),)),
    }


EPSILON = 1e-05
HIGH = lax.Precision.HIGHEST

@jax.custom_vjp
def low(v):
    return lax.optimization_barrier(v.astype(jnp.bfloat16)).astype(jnp.float32)

@jax.custom_vjp
def low_back(v):
    return v

def low_keep(v):
    return (low(v), None)

def low_pass(kept, grad):
    return (grad,)

def back_keep(v):
    return (v, None)

def back_low(kept, grad):
    return (low(grad),)
low.defvjp(low_keep, low_pass)
low_back.defvjp(back_keep, back_low)

def rounded(value):
    return low(low_back(value))

def block_scan(inner_x, step_val, log_step, shared_b, shared_c, seg_line):
    length, num_heads, head_size = inner_x.shape
    nblocks = length // BLOCK

    def split(array):
        return array.reshape((nblocks, BLOCK) + array.shape[1:])

    def block_step(carried, block_in):
        state_now, last_doc = carried
        x_blk, dt_blk, la_blk, b_blk, c_blk, seg_blk = block_in
        cumulative = jnp.cumsum(la_blk, axis=0)
        order = jnp.arange(BLOCK)
        visible = (seg_blk[:, None] == seg_blk[None, :]) & (order[:, None] >= order[None, :])
        log_gap = cumulative[:, None, :] - cumulative[None, :, :]
        decays = jnp.exp(jnp.where(visible[:, :, None], log_gap, -jnp.inf))
        inner_cb = jnp.dot(c_blk, b_blk.T, precision=HIGH)
        mixing_w = inner_cb[:, :, None] * decays * dt_blk[None, :, :]
        y_block = jnp.einsum('tsh,shp->thp', mixing_w, x_blk, precision=HIGH)
        keep_state = (seg_blk == last_doc).astype(jnp.float32)
        carried_in = jnp.einsum('tn,hpn->thp', c_blk, state_now, precision=HIGH)
        y_block = y_block + carried_in * (jnp.exp(cumulative) * keep_state[:, None])[:, :, None]
        end_doc = seg_blk[BLOCK - 1]
        tail_w = jnp.exp(cumulative[BLOCK - 1][None, :] - cumulative) * (seg_blk == end_doc).astype(jnp.float32)[:, None] * dt_blk
        next_state = jnp.einsum('sh,shp,sn->hpn', tail_w, x_blk, b_blk, precision=HIGH)
        carry_on = jnp.exp(cumulative[BLOCK - 1]) * (last_doc == end_doc).astype(jnp.float32)
        next_state = next_state + state_now * carry_on[:, None, None]
        return ((next_state, end_doc), y_block)
    initial = (jnp.zeros((num_heads, head_size, shared_b.shape[1]), jnp.float32), jnp.array(-1, jnp.int32))
    blocks_in = (split(inner_x), split(step_val), split(log_step), split(shared_b), split(shared_c), split(seg_line))
    unused, y_blocks = lax.scan(jax.checkpoint(block_step), initial, blocks_in)
    return y_blocks.reshape(inner_x.shape)

def mixing(gate_val, inner_val, shared_val, step_raw, filters, biases, step_bias, log_rate, skip_gain, seg_line):
    length, width_in = inner_val.shape
    num_heads = step_raw.shape[1]
    head_size = width_in // num_heads
    joined = jnp.concatenate([inner_val, shared_val], axis=1)
    taps = filters.shape[0]
    conv_sum = biases[None, :] + filters[taps - 1][None, :] * joined
    for shift in range(1, taps):
        shifted = jnp.pad(joined, ((shift, 0), (0, 0)))[:length]
        prior_seg = jnp.pad(seg_line, (shift, 0), constant_values=-1)[:length]
        same_doc = (prior_seg == seg_line).astype(jnp.float32)
        conv_sum = conv_sum + filters[taps - 1 - shift][None, :] * shifted * same_doc[:, None]
    activated = jax.nn.silu(conv_sum)
    inner_x = activated[:, :width_in].reshape(length, num_heads, head_size)
    shared_b = activated[:, width_in:width_in + NS]
    shared_c = activated[:, width_in + NS:]
    step_val = jax.nn.softplus(step_raw + step_bias[None, :])
    log_step = -step_val * jnp.exp(log_rate)[None, :]
    y_heads = block_scan(inner_x, step_val, log_step, shared_b, shared_c, seg_line)
    y_heads = y_heads + skip_gain[None, :, None] * inner_x
    return y_heads.reshape(length, width_in) * jax.nn.silu(gate_val)

def forward(hidden_f, norm_gain, weight_gate, weight_inner, weight_shared, weight_step, filter_inner, bias_inner, filter_shared, bias_shared, step_bias, log_rate, skip_gain, gate_gain, weight_out, segments):
    inv_rms = lax.rsqrt(lax.optimization_barrier(jnp.mean(hidden_f * hidden_f, axis=1, keepdims=True)) + EPSILON)
    normed = low(hidden_f * inv_rms * norm_gain[None, :])
    gate_z = rounded(jnp.dot(normed, weight_gate, precision=HIGH))
    inner_x = rounded(jnp.dot(normed, weight_inner, precision=HIGH))
    shared_bc = rounded(jnp.dot(normed, weight_shared, precision=HIGH))
    step_raw = rounded(jnp.dot(normed, weight_step, precision=HIGH))
    filters = jnp.concatenate([filter_inner, filter_shared], axis=1)
    biases = jnp.concatenate([bias_inner, bias_shared], axis=0)

    def per_sequence(pieces):
        gate_s, inner_s, shared_s, step_s, seg_s = pieces
        mixed = mixing(gate_s, inner_s, shared_s, step_s, filters, biases, step_bias, log_rate, skip_gain, seg_s)
        inv_gate = lax.rsqrt(lax.optimization_barrier(jnp.mean(mixed * mixed, axis=1, keepdims=True)) + EPSILON)
        return mixed * inv_gate * gate_gain[None, :]

    def lines(array):
        return array.reshape((NSEQ, LEN) + array.shape[1:])
    gated = lax.map(jax.checkpoint(per_sequence), (lines(gate_z), lines(inner_x), lines(shared_bc), lines(step_raw), segments))
    gated = low(gated.reshape(TOKENS, INNER))
    return hidden_f + jnp.dot(gated, weight_out.T, precision=HIGH)

def reference(hidden, norm_gain, weight_gate, weight_inner, weight_shared, weight_step, filter_inner, bias_inner, filter_shared, bias_shared, step_bias, log_rate, skip_gain, gate_gain, weight_out, segments, cotangent):
    floats = [array.astype(jnp.float32) for array in (hidden, norm_gain, weight_gate, weight_inner, weight_shared, weight_step, filter_inner, bias_inner, filter_shared, bias_shared, step_bias, log_rate, skip_gain, gate_gain, weight_out)]

    def closed(*values):
        return forward(*values, segments)
    result, pullback = jax.vjp(closed, *floats)
    grads = pullback(cotangent.astype(jnp.float32))
    return (result.astype(jnp.bfloat16), grads[0], grads[1], grads[2], grads[3], grads[4], grads[5], grads[6], grads[7], grads[8], grads[9], grads[10], grads[11], grads[12], grads[13], grads[14])
```

```python
import jax
import jax.numpy as jnp
from jax import lax
from jax.experimental import pallas as pl
from jax.experimental.pallas import tpu as pltpu
from jax.sharding import PartitionSpec as P

INNER = 2048
NS = 128
HEAD = 64
Q = 128
LOG2E = 1.4426950408889634
FAR = -1e30
EPSILON = 1e-05

F32 = jnp.float32
BF16 = jnp.bfloat16
HIGH = lax.Precision.HIGHEST


def mm(a, b):
    return jnp.dot(a, b, preferred_element_type=F32)


def mm_t(a, b):
    return lax.dot_general(a, b, (((1,), (1,)), ((), ())), preferred_element_type=F32)


def weight_grad(a, b):
    return lax.dot_general(a, b, (((0,), (0,)), ((), ())), preferred_element_type=F32)


def iota(shape, dim):
    return lax.broadcasted_iota(jnp.int32, shape, dim)


def softplus(v):
    return jnp.maximum(v, 0.0) + jnp.log1p(jnp.exp(-jnp.abs(v)))


def steps_of(step_ref, heads_ref):
    raw = step_ref[...].astype(F32) + heads_ref[0:1, :]
    dt = softplus(raw)
    lower = (iota((Q, Q), 0) >= iota((Q, Q), 1)).astype(F32)
    cum = jnp.dot(
        lower, dt * (heads_ref[1:2, :] * LOG2E), precision=HIGH, preferred_element_type=F32
    )
    return raw, dt, cum


def wide(column):
    return jnp.broadcast_to(column, (Q, 128))


def pair_of(first, array, pair):
    return jnp.where(
        first, wide(array[:, 2 * pair : 2 * pair + 1]), wide(array[:, 2 * pair + 1 : 2 * pair + 2])
    )


def stacked(first, block):
    nil = jnp.zeros_like(block)
    return jnp.concatenate([jnp.where(first, block, nil), jnp.where(first, nil, block)], axis=0)


def forward_kernel(
    turn_ref, u_ref, s_ref, step_ref, aux_ref, seg_ref, inner_ref, shared_ref, heads_ref,
    y_ref, conv_ref, convs_ref, states_ref,
    ubuf, sbuf, state,
):
    width = u_ref.shape[1]
    chunk = pl.program_id(0)

    @pl.when(chunk == 0)
    def _():
        ubuf[0:8, :] = jnp.zeros((8, width), F32)
        sbuf[0:8, :] = jnp.zeros((8, 2 * NS), F32)
        state[...] = jnp.zeros_like(state)

    @pl.when(chunk > 0)
    def _():
        ubuf[0:8, :] = ubuf[Q : Q + 8, :]
        sbuf[0:8, :] = sbuf[Q : Q + 8, :]

    ubuf[8 : Q + 8, :] = u_ref[...].astype(F32)
    sbuf[8 : Q + 8, :] = s_ref[...].astype(F32)
    aux = aux_ref[...]
    same = [wide(aux[:, k : k + 1]) for k in range(3)]
    keep = wide(aux[:, 6:7])
    tail_in = wide(aux[:, 7:8])

    def conv_of(buf, weights, cols):
        total = weights[4:5, cols] + weights[3:4, cols] * buf[8 : Q + 8, cols]
        for shift in range(1, 4):
            total = total + weights[3 - shift : 4 - shift, cols] * (
                buf[8 - shift : Q + 8 - shift, cols] * same[shift - 1]
            )
        return total

    def silu(v):
        return v * (0.5 + 0.5 * jnp.tanh(0.5 * v))

    conv_b = conv_of(sbuf, shared_ref, slice(0, NS))
    conv_c = conv_of(sbuf, shared_ref, slice(NS, 2 * NS))
    convs_ref[:, 0:NS] = conv_b
    convs_ref[:, NS : 2 * NS] = conv_c
    b_f = silu(conv_b)
    b_low = b_f.astype(BF16)
    b_turn = b_f.T.astype(BF16)
    c_low = silu(conv_c).astype(BF16)
    inner_cb = mm_t(c_low, b_low)
    visible = (wide(aux[:, 8:9]) == seg_ref[0]) & (iota((Q, Q), 0) >= iota((Q, Q), 1))
    bias = jnp.where(visible, 0.0, FAR)
    raw, dt, cum = steps_of(step_ref, heads_ref)
    cum_t = cum.T
    first = iota((Q, 128), 1) < HEAD
    for pair in range(width // 128):
        cols = slice(128 * pair, 128 * pair + 128)
        conv = conv_of(ubuf, inner_ref, cols)
        conv_ref[:, cols] = conv
        x = silu(conv)
        cum_1 = wide(cum[:, 2 * pair : 2 * pair + 1])
        cum_2 = wide(cum[:, 2 * pair + 1 : 2 * pair + 2])
        m_1 = inner_cb * jnp.exp2(cum_1 - cum_t[2 * pair : 2 * pair + 1, :] + bias)
        m_2 = inner_cb * jnp.exp2(cum_2 - cum_t[2 * pair + 1 : 2 * pair + 2, :] + bias)
        xd = x * pair_of(first, dt, pair)
        mixers = jnp.concatenate([m_1.astype(BF16), m_2.astype(BF16)], axis=1)
        y = mm(mixers, stacked(first, xd.astype(BF16)))
        cum_p = jnp.where(first, cum_1, cum_2)
        last = cum_p[Q - 1 : Q, :]
        old = state[:, cols]
        old_low = old.astype(BF16)
        states_ref[0, :, cols] = old_low
        y = y + mm(c_low, old_low) * (jnp.exp2(cum_p) * keep)
        y_ref[:, cols] = y + inner_ref[5:6, cols] * x
        tail = jnp.exp2(last - cum_p) * tail_in
        carry = jnp.exp2(last) * keep[Q - 1 : Q, :]
        state[:, cols] = old * carry + mm(b_turn, (xd * tail).astype(BF16))


def backward_kernel(
    turn_ref, u_ref, s_ref, conv_ref, convs_ref, step_ref, aux_ref, seg_ref, grad_ref, states_ref,
    inner_ref, shared_ref, heads_ref,
    low_ref, inner_sum, shared_sum, heads_sum,
    dbuf, dsbuf, dstate, dcum_t, red, wgrad, xtail,
):
    width = u_ref.shape[1]
    chunk = pl.program_id(0)

    @pl.when(chunk == 0)
    def _():
        dbuf[Q : Q + 8, :] = jnp.zeros((8, width), F32)
        dsbuf[Q : Q + 8, :] = jnp.zeros((8, 2 * NS), F32)
        dstate[...] = jnp.zeros_like(dstate)
        dcum_t[...] = jnp.zeros_like(dcum_t)
        inner_sum[...] = jnp.zeros_like(inner_sum)
        shared_sum[...] = jnp.zeros_like(shared_sum)
        heads_sum[...] = jnp.zeros_like(heads_sum)

    @pl.when(chunk > 0)
    def _():
        dbuf[Q : Q + 8, :] = dbuf[0:8, :]
        dsbuf[Q : Q + 8, :] = dsbuf[0:8, :]

    aux = aux_ref[...]
    same = [wide(aux[:, 3 + k : 4 + k]) for k in range(3)]
    keep = wide(aux[:, 6:7])
    tail_in = wide(aux[:, 7:8])

    def silu_and_slope(v):
        sig = 0.5 + 0.5 * jnp.tanh(0.5 * v)
        act = v * sig
        return act, sig + act * (1.0 - sig)

    b_f, b_slope = silu_and_slope(convs_ref[:, 0:NS])
    c_f, c_slope = silu_and_slope(convs_ref[:, NS : 2 * NS])
    b_low = b_f.astype(BF16)
    c_low = c_f.astype(BF16)
    c_turn = c_f.T.astype(BF16)
    inner_bc = mm_t(b_low, c_low)
    row, column = iota((Q, Q), 0), iota((Q, Q), 1)
    visible = (wide(aux[:, 8:9]) == seg_ref[0]) & (row <= column)
    bias = jnp.where(visible, 0.0, FAR)
    lower_low = (row >= column).astype(BF16)
    strict = row < column
    raw, dt, cum = steps_of(step_ref, heads_ref)
    cum_t = cum.T
    first = iota((Q, 128), 1) < HEAD
    dinner = jnp.zeros((Q, Q), F32)
    for pair in range(width // 128):
        cols = slice(128 * pair, 128 * pair + 128)
        cum_1 = wide(cum[:, 2 * pair : 2 * pair + 1])
        cum_2 = wide(cum[:, 2 * pair + 1 : 2 * pair + 2])
        decay_1 = jnp.exp2(cum_t[2 * pair : 2 * pair + 1, :] - cum_1 + bias)
        decay_2 = jnp.exp2(cum_t[2 * pair + 1 : 2 * pair + 2, :] - cum_2 + bias)
        m_1 = inner_bc * decay_1
        m_2 = inner_bc * decay_2
        x, slope = silu_and_slope(conv_ref[:, cols])
        dt_p = pair_of(first, dt, pair)
        xd = x * dt_p
        grad = grad_ref[:, cols].astype(F32)
        grad_low = grad.astype(BF16)
        dm = mm_t(stacked(first, xd.astype(BF16)), grad_low)
        dm_1, dm_2 = dm[0:Q, :], dm[Q : 2 * Q, :]
        dinner = dinner + dm_1 * decay_1 + dm_2 * decay_2
        gaps = jnp.concatenate([(dm_1 * m_1).astype(BF16), (dm_2 * m_2).astype(BF16)], axis=0)
        spans = mm(gaps, lower_low)
        dcum_t[2 * pair : 2 * pair + 1, :] = jnp.sum(
            jnp.where(strict, spans[0:Q, :], 0.0), axis=0, keepdims=True
        )
        dcum_t[2 * pair + 1 : 2 * pair + 2, :] = jnp.sum(
            jnp.where(strict, spans[Q : 2 * Q, :], 0.0), axis=0, keepdims=True
        )
        mixers = jnp.concatenate([m_1.astype(BF16), m_2.astype(BF16)], axis=1)
        dxd = mm(mixers, stacked(first, grad_low))
        cum_p = jnp.where(first, cum_1, cum_2)
        last = cum_p[Q - 1 : Q, :]
        tail = jnp.exp2(last - cum_p) * tail_in
        later = dstate[:, cols]
        old_low = states_ref[0, :, cols]
        xt = xd * tail
        from_end = mm(b_low, later.astype(BF16))
        dxd = dxd + tail * from_end
        weight = jnp.exp2(cum_p) * keep
        wg = grad * weight
        from_start = mm(c_low, old_low)
        carry = jnp.exp2(last) * keep[Q - 1 : Q, :]
        carried = jnp.sum(later * old_low.astype(F32), axis=0, keepdims=True) * carry
        red[0:Q, cols] = (dxd * x).astype(BF16)
        red[Q : 2 * Q, cols] = (xt * from_end).astype(BF16)
        red[2 * Q : 3 * Q, cols] = (wg * from_start).astype(BF16)
        red[3 * Q : 3 * Q + 16, cols] = jnp.broadcast_to(carried, (16, 128)).astype(BF16)
        wg_low = wg.astype(BF16)
        wgrad[:, cols] = wg_low
        xtail[:, cols] = xt.astype(BF16)
        dx = dxd * dt_p + inner_ref[5:6, cols] * grad
        dbuf[0:Q, cols] = dx * slope
        inner_sum[5:6, cols] += jnp.sum(grad * x, axis=0, keepdims=True)

    to_head = (iota((width, 128), 0) // HEAD == iota((width, 128), 1)).astype(BF16)
    sums = mm(red[...], to_head)
    lower = (row >= column).astype(F32)
    upper = (row <= column).astype(F32)
    strict_lower = (row > column).astype(F32)
    dla = (
        dcum_t[...].T
        + jnp.dot(strict_lower, sums[Q : 2 * Q, :], precision=HIGH, preferred_element_type=F32)
        + jnp.dot(upper, sums[2 * Q : 3 * Q, :], precision=HIGH, preferred_element_type=F32)
        + sums[3 * Q : 3 * Q + 1, :]
    )
    rate = heads_ref[1:2, :]
    ddt = sums[0:Q, :] + rate * dla
    dstep = ddt * (0.5 + 0.5 * jnp.tanh(0.5 * raw))
    low_ref[:, width + 2 * NS : width + 2 * NS + 128] = dstep.astype(BF16)
    heads_sum[0:1, :] += jnp.sum(dstep, axis=0, keepdims=True)
    heads_sum[1:2, :] += jnp.sum(dla * dt * rate, axis=0, keepdims=True)

    dinner_low = dinner.astype(BF16)
    later_low = dstate[...].astype(BF16)
    db = mm(dinner_low, c_low) + mm_t(xtail[...], later_low)
    dc = mm(dinner.T.astype(BF16), b_low) + mm_t(wgrad[...], states_ref[0])
    dsbuf[0:Q, 0:NS] = db * b_slope
    dsbuf[0:Q, NS : 2 * NS] = dc * c_slope

    def conv_back(u, buf, weights, sums_ref, cols):
        d = buf[0:Q, cols]
        du = weights[3:4, cols] * d
        sums_ref[3:4, cols] += jnp.sum(d * u, axis=0, keepdims=True)
        sums_ref[4:5, cols] += jnp.sum(d, axis=0, keepdims=True)
        for shift in range(1, 4):
            d = buf[shift : Q + shift, cols] * same[shift - 1]
            du = du + weights[3 - shift : 4 - shift, cols] * d
            sums_ref[3 - shift : 4 - shift, cols] += jnp.sum(d * u, axis=0, keepdims=True)
        return du

    for part in range(2):
        cols = slice(NS * part, NS * part + NS)
        low_ref[:, width + NS * part : width + NS * part + NS] = conv_back(
            s_ref[:, cols].astype(F32), dsbuf, shared_ref, shared_sum, cols
        ).astype(BF16)
    new = mm(c_turn, wgrad[...])
    for pair in range(width // 128):
        cols = slice(128 * pair, 128 * pair + 128)
        low_ref[:, cols] = conv_back(
            u_ref[:, cols].astype(F32), dbuf, inner_ref, inner_sum, cols
        ).astype(BF16)
        cum_p = jnp.where(
            first[0:1, :],
            jnp.broadcast_to(cum[Q - 1 : Q, 2 * pair : 2 * pair + 1], (1, 128)),
            jnp.broadcast_to(cum[Q - 1 : Q, 2 * pair + 1 : 2 * pair + 2], (1, 128)),
        )
        carry = jnp.exp2(cum_p) * keep[Q - 1 : Q, :]
        dstate[:, cols] = dstate[:, cols] * carry + new[:, cols]


VMEM_LIMIT = 48 * 1024 * 1024


def forward_mix(turn, proj, aux, seg_rows, inner_p, shared_p, heads_p):
    length = proj.shape[0]
    width = inner_p.shape[1]
    chunks = length // Q

    def rows(n, at=0):
        return pl.BlockSpec((Q, n), lambda c, turn: (lax.rem(c + turn[0], chunks), at))

    def plain(n):
        return pl.BlockSpec((Q, n), lambda c, turn: (c, 0))

    def whole(n):
        return pl.BlockSpec((8, n), lambda c, turn: (0, 0))

    line = pl.BlockSpec((1, 1, Q), lambda c, turn: (c, 0, 0))
    kept = pl.BlockSpec((1, NS, width), lambda c, turn: (c, 0, 0))
    return pl.pallas_call(
        forward_kernel,
        grid_spec=pltpu.PrefetchScalarGridSpec(
            num_scalar_prefetch=1,
            grid=(chunks,),
            in_specs=[
                rows(width), rows(2 * NS, width // (2 * NS)), rows(128, (width + 2 * NS) // 128),
                plain(16), line, whole(width), whole(2 * NS), whole(128),
            ],
            out_specs=[rows(width), plain(width), plain(2 * NS), kept],
            scratch_shapes=[
                pltpu.VMEM((Q + 8, width), F32),
                pltpu.VMEM((Q + 8, 2 * NS), F32),
                pltpu.VMEM((NS, width), F32),
            ],
        ),
        out_shape=[
            jax.ShapeDtypeStruct((length, width), F32),
            jax.ShapeDtypeStruct((length, width), F32),
            jax.ShapeDtypeStruct((length, 2 * NS), F32),
            jax.ShapeDtypeStruct((chunks, NS, width), BF16),
        ],
        compiler_params=pltpu.CompilerParams(vmem_limit_bytes=VMEM_LIMIT),
        cost_estimate=pl.CostEstimate(
            flops=32 * length * 128 * width, bytes_accessed=12 * length * width, transcendentals=0
        ),
        name="mix_forward",
    )(turn, proj, proj, proj, aux, seg_rows, inner_p, shared_p, heads_p)


def backward_mix(turn, proj, conv, convs, aux, seg_rows, grad, states, inner_p, shared_p, heads_p):
    length = proj.shape[0]
    width = inner_p.shape[1]
    chunks = length // Q

    def rows(n, at=0):
        return pl.BlockSpec(
            (Q, n), lambda c, turn: (lax.rem(chunks - 1 - c + turn[0], chunks), at)
        )

    def plain(n):
        return pl.BlockSpec((Q, n), lambda c, turn: (chunks - 1 - c, 0))

    def whole(n):
        return pl.BlockSpec((8, n), lambda c, turn: (0, 0))

    line = pl.BlockSpec((1, 1, Q), lambda c, turn: (chunks - 1 - c, 0, 0))
    kept = pl.BlockSpec((1, NS, width), lambda c, turn: (chunks - 1 - c, 0, 0))
    return pl.pallas_call(
        backward_kernel,
        grid_spec=pltpu.PrefetchScalarGridSpec(
            num_scalar_prefetch=1,
            grid=(chunks,),
            in_specs=[
                rows(width), rows(2 * NS, width // (2 * NS)), plain(width), plain(2 * NS),
                rows(128, (width + 2 * NS) // 128), plain(16), line, rows(width), kept,
                whole(width), whole(2 * NS), whole(128),
            ],
            out_specs=[rows(width + 2 * NS + 128), whole(width), whole(2 * NS), whole(128)],
            scratch_shapes=[
                pltpu.VMEM((Q + 8, width), F32),
                pltpu.VMEM((Q + 8, 2 * NS), F32),
                pltpu.VMEM((NS, width), F32),
                pltpu.VMEM((128, Q), F32),
                pltpu.VMEM((3 * Q + 16, width), BF16),
                pltpu.VMEM((Q, width), BF16),
                pltpu.VMEM((Q, width), BF16),
            ],
        ),
        out_shape=[
            jax.ShapeDtypeStruct((length, width + 2 * NS + 128), BF16),
            jax.ShapeDtypeStruct((8, width), F32),
            jax.ShapeDtypeStruct((8, 2 * NS), F32),
            jax.ShapeDtypeStruct((8, 128), F32),
        ],
        compiler_params=pltpu.CompilerParams(vmem_limit_bytes=VMEM_LIMIT),
        cost_estimate=pl.CostEstimate(
            flops=70 * length * 128 * width, bytes_accessed=20 * length * width, transcendentals=0
        ),
        name="mix_backward",
    )(turn, proj, proj, conv, convs, proj, aux, seg_rows, grad, states, inner_p, shared_p, heads_p)


def aux_of(seg_line):
    length = seg_line.shape[0]
    ends = seg_line.reshape(-1, Q)[:, Q - 1]
    prior = jnp.concatenate([jnp.full((1,), -1, seg_line.dtype), ends[:-1]])
    place = jnp.arange(length)
    columns = []
    for shift in range(1, 4):
        columns.append((jnp.roll(seg_line, shift) == seg_line) & (place >= shift))
    for shift in range(1, 4):
        columns.append((jnp.roll(seg_line, -shift) == seg_line) & (place < length - shift))
    columns.append(seg_line == jnp.repeat(prior, Q))
    columns.append(seg_line == jnp.repeat(ends, Q))
    columns = [column.astype(F32) for column in columns] + [seg_line.astype(F32)]
    columns += [jnp.zeros((length,), F32)] * (16 - len(columns))
    rows = seg_line.astype(F32).reshape(-1, 1, Q)
    return jnp.stack(columns, axis=1), rows


def silu_of(v):
    return v * jax.nn.sigmoid(v)


def program(sizes, args):
    (
        hidden, norm_gain, weight_gate, weight_inner, weight_shared, weight_step,
        filter_inner, bias_inner, filter_shared, bias_shared, step_bias, log_rate, skip_gain,
        gate_gain, weight_out, segments, cotangent,
    ) = args
    n_fsdp, n_tp = sizes
    width = weight_gate.shape[1]
    heads = weight_step.shape[1]
    own_rows = hidden.shape[0]
    length = segments.shape[1]
    tp_place = lax.axis_index("tp")
    paired = n_tp == 2

    def tp_rows(own):
        if paired:
            return jnp.concatenate([own, lax.ppermute(own, "tp", [(0, 1), (1, 0)])], axis=0)
        return lax.all_gather(own, "tp", axis=0, tiled=True)

    def tp_scatter(part):
        if paired:
            away = lax.ppermute(part[own_rows:].astype(BF16), "tp", [(0, 1), (1, 0)])
            return part[:own_rows] + away.astype(F32)
        return lax.psum_scatter(part, "tp", scatter_dimension=0, tiled=True)

    def gather(shard):
        return lax.all_gather(shard, "fsdp", axis=0, tiled=True)

    def scatter(total):
        return lax.psum_scatter(total, "fsdp", scatter_dimension=0, tiled=True).astype(F32)

    def butterfly(value):
        reach = 1
        while reach < n_fsdp:
            value = value + lax.ppermute(
                value, "fsdp", [(i, i ^ reach) for i in range(n_fsdp)]
            )
            reach *= 2
        return value

    pad = jnp.zeros((weight_step.shape[0], 128 - heads - 1), BF16)
    shard_a = jnp.concatenate(
        [weight_inner, weight_shared, weight_step, norm_gain[:, None], pad], axis=1
    )
    shard_b = jnp.concatenate([weight_gate, weight_out], axis=1)
    hidden_all = tp_rows(hidden)
    weights_a = gather(shard_a)
    cot_all = tp_rows(cotangent)
    weights_b = gather(shard_b)
    gate_all, out_all = weights_b[:, :width], weights_b[:, width:]
    gain_row = weights_a[:, width + 2 * NS + heads].astype(F32)[None, :]

    hidden_f = hidden_all.astype(F32)
    inv_rms = lax.rsqrt(jnp.mean(hidden_f * hidden_f, axis=1, keepdims=True) + EPSILON)
    normed = (hidden_f * inv_rms * gain_row).astype(BF16)
    proj = mm(normed, weights_a).astype(BF16)

    turn = (tp_place * (own_rows // Q) if paired else jnp.zeros((), jnp.int32)).reshape(1)
    turn = turn.astype(jnp.int32)
    aux, seg_rows = aux_of(segments[0])
    skip_lanes = jnp.repeat(skip_gain.astype(F32), HEAD)
    inner_p = jnp.concatenate(
        [filter_inner.astype(F32), bias_inner.astype(F32)[None], skip_lanes[None],
         jnp.zeros((2, width), F32)], axis=0)
    shared_p = jnp.concatenate(
        [filter_shared.astype(F32), bias_shared.astype(F32)[None], jnp.zeros((3, 2 * NS), F32)],
        axis=0,
    )
    heads_p = jnp.pad(
        jnp.stack([step_bias.astype(F32), -jnp.exp(log_rate.astype(F32))]),
        ((0, 6), (0, 128 - heads)),
    )
    y, conv, convs, states = forward_mix(turn, proj, aux, seg_rows, inner_p, shared_p, heads_p)

    gate_z = mm(normed, gate_all).astype(BF16).astype(F32)
    grad_gated = mm(cot_all, out_all)
    gain_gate = gate_gain.astype(F32)[None, :]
    sig = jax.nn.sigmoid(gate_z)
    act = gate_z * sig
    mixed = y * act
    scaled = grad_gated * gain_gate
    sums = jnp.stack([jnp.sum(mixed * mixed, axis=1), jnp.sum(mixed * scaled, axis=1)], axis=1)
    if paired:
        half = jnp.concatenate([sums[own_rows:], sums[:own_rows]], axis=0)
        sums = sums + lax.ppermute(half, "tp", [(0, 1), (1, 0)])
    else:
        sums = lax.psum(sums, "tp")
    inv_gate = lax.rsqrt(sums[:, 0:1] / INNER + EPSILON)
    gated = (mixed * inv_gate * gain_gate).astype(BF16)
    grad_mixed = inv_gate * scaled - mixed * (inv_gate * inv_gate * inv_gate) * (
        sums[:, 1:2] / INNER
    )
    grad_y = grad_mixed * act
    low_z = (grad_mixed * y * (sig + act * (1.0 - sig))).astype(BF16)
    grad_gain_gate = jnp.sum(grad_gated * mixed * inv_gate, axis=0)
    grads_b = jnp.concatenate(
        [weight_grad(normed, low_z), weight_grad(cot_all, gated)], axis=1
    ).astype(BF16)
    owned_b = scatter(grads_b)
    out_own = tp_scatter(mm_t(gated, out_all))
    layer_out = (hidden.astype(F32) + out_own).astype(BF16)

    low, inner_sum, shared_sum, heads_sum = backward_mix(
        turn, proj, conv, convs, aux, seg_rows, grad_y, states, inner_p, shared_p, heads_p
    )
    grads_a = weight_grad(normed, low).astype(BF16)
    owned_a = scatter(grads_a)
    small = butterfly(
        jnp.concatenate(
            [jnp.concatenate([inner_sum[:6], grad_gain_gate[None], inner_sum[7:]], axis=0),
             shared_sum, heads_sum], axis=1)
    )
    grad_normed = tp_scatter(mm_t(low_z, gate_all) + mm_t(low, weights_a))
    x_hat = hidden.astype(F32) * inv_rms[:own_rows] if paired else None
    inv_own = inv_rms[:own_rows]
    if not paired:
        inv_own = lax.dynamic_slice_in_dim(inv_rms, tp_place * own_rows, own_rows, 0)
        x_hat = hidden.astype(F32) * inv_own
    scaled_in = grad_normed * gain_row
    grad_hidden = cotangent.astype(F32) + inv_own * (
        scaled_in - x_hat * jnp.mean(scaled_in * x_hat, axis=1, keepdims=True)
    )

    grad_gate, grad_out = owned_b[:, :width], owned_b[:, width:]
    grad_inner = owned_a[:, :width]
    grad_shared = owned_a[:, width : width + 2 * NS]
    grad_step = owned_a[:, width + 2 * NS : width + 2 * NS + heads]
    gain_own = (
        jnp.sum(weight_gate.astype(F32) * grad_gate, axis=1)
        + jnp.sum(weight_inner.astype(F32) * grad_inner, axis=1)
        + jnp.sum(weight_shared.astype(F32) * grad_shared, axis=1)
        + jnp.sum(weight_step.astype(F32) * grad_step, axis=1)
    )
    shared_part = small[:, width : width + 2 * NS]
    grad_shared, gain_own, shared_part = lax.psum((grad_shared, gain_own, shared_part), "tp")
    grad_norm_gain = gain_own / norm_gain.astype(F32)
    head_part = small[:, width + 2 * NS :]
    return (
        layer_out,
        grad_hidden,
        grad_norm_gain,
        grad_gate,
        grad_inner,
        grad_shared,
        grad_step,
        small[0:4, :width],
        small[4, :width],
        shared_part[0:4],
        shared_part[4],
        head_part[0, :heads],
        head_part[1, :heads],
        jnp.sum(small[5, :width].reshape(heads, HEAD), axis=1),
        small[6, :width],
        grad_out,
    )


def solution(mesh):
    sizes = (mesh.shape["fsdp"], mesh.shape["tp"])

    def per_device(*args):
        return program(sizes, args)

    return jax.shard_map(
        per_device,
        mesh=mesh,
        in_specs=(
            P(("fsdp", "tp"), None),
            P("fsdp"),
            P("fsdp", "tp"),
            P("fsdp", "tp"),
            P("fsdp", None),
            P("fsdp", "tp"),
            P(None, "tp"),
            P("tp"),
            P(),
            P(),
            P("tp"),
            P("tp"),
            P("tp"),
            P("tp"),
            P("fsdp", "tp"),
            P("fsdp", None),
            P(("fsdp", "tp"), None),
        ),
        out_specs=(
            P(("fsdp", "tp"), None),
            P(("fsdp", "tp"), None),
            P("fsdp"),
            P("fsdp", "tp"),
            P("fsdp", "tp"),
            P("fsdp", None),
            P("fsdp", "tp"),
            P(None, "tp"),
            P("tp"),
            P(),
            P(),
            P("tp"),
            P("tp"),
            P("tp"),
            P("tp"),
            P("fsdp", "tp"),
        ),
        check_vma=False,
    )
```

```python
import jax
import jax.numpy as jnp
from jax import lax
from jax.experimental import pallas as pl
from jax.experimental.pallas import tpu as pltpu
from jax.sharding import PartitionSpec as P

INNER = 2048
NS = 128
HEAD = 64
Q = 128
LOG2E = 1.4426950408889634
FAR = -1e30
EPSILON = 1e-05

F32 = jnp.float32
BF16 = jnp.bfloat16
HIGH = lax.Precision.HIGHEST


def mm(a, b):
    return jnp.dot(a, b, preferred_element_type=F32)


def mm_t(a, b):
    return lax.dot_general(a, b, (((1,), (1,)), ((), ())), preferred_element_type=F32)


def weight_grad(a, b):
    return lax.dot_general(a, b, (((0,), (0,)), ((), ())), preferred_element_type=F32)


def iota(shape, dim):
    return lax.broadcasted_iota(jnp.int32, shape, dim)


def softplus(v):
    return jnp.maximum(v, 0.0) + jnp.log1p(jnp.exp(-jnp.abs(v)))


def steps_of(step_ref, heads_ref):
    raw = step_ref[...].astype(F32) + heads_ref[0:1, :]
    dt = softplus(raw)
    lower = (iota((Q, Q), 0) >= iota((Q, Q), 1)).astype(F32)
    cum = jnp.dot(
        lower, dt * (heads_ref[1:2, :] * LOG2E), precision=HIGH, preferred_element_type=F32
    )
    return raw, dt, cum


def wide(column):
    return jnp.broadcast_to(column, (Q, 128))


def pair_of(first, array, pair):
    return jnp.where(
        first, wide(array[:, 2 * pair : 2 * pair + 1]), wide(array[:, 2 * pair + 1 : 2 * pair + 2])
    )


def stacked(first, block):
    nil = jnp.zeros_like(block)
    return jnp.concatenate([jnp.where(first, block, nil), jnp.where(first, nil, block)], axis=0)


def forward_kernel(
    turn_ref, u_ref, s_ref, step_ref, aux_ref, seg_ref, inner_ref, shared_ref, heads_ref,
    y_ref, conv_ref, convs_ref, states_ref,
    ubuf, sbuf, state,
):
    width = u_ref.shape[1]
    chunk = pl.program_id(0)

    @pl.when(chunk == 0)
    def _():
        ubuf[0:8, :] = jnp.zeros((8, width), F32)
        sbuf[0:8, :] = jnp.zeros((8, 2 * NS), F32)
        state[...] = jnp.zeros_like(state)

    @pl.when(chunk > 0)
    def _():
        ubuf[0:8, :] = ubuf[Q : Q + 8, :]
        sbuf[0:8, :] = sbuf[Q : Q + 8, :]

    ubuf[8 : Q + 8, :] = u_ref[...].astype(F32)
    sbuf[8 : Q + 8, :] = s_ref[...].astype(F32)
    aux = aux_ref[...]
    same = [wide(aux[:, k : k + 1]) for k in range(3)]
    keep = wide(aux[:, 6:7])
    tail_in = wide(aux[:, 7:8])

    def conv_of(buf, weights, cols):
        total = weights[4:5, cols] + weights[3:4, cols] * buf[8 : Q + 8, cols]
        for shift in range(1, 4):
            total = total + weights[3 - shift : 4 - shift, cols] * (
                buf[8 - shift : Q + 8 - shift, cols] * same[shift - 1]
            )
        return total

    def silu(v):
        return v * (0.5 + 0.5 * jnp.tanh(0.5 * v))

    conv_b = conv_of(sbuf, shared_ref, slice(0, NS))
    conv_c = conv_of(sbuf, shared_ref, slice(NS, 2 * NS))
    convs_ref[:, 0:NS] = conv_b
    convs_ref[:, NS : 2 * NS] = conv_c
    b_f = silu(conv_b)
    b_low = b_f.astype(BF16)
    b_turn = b_f.T.astype(BF16)
    c_low = silu(conv_c).astype(BF16)
    inner_cb = mm_t(c_low, b_low)
    visible = (wide(aux[:, 8:9]) == seg_ref[0]) & (iota((Q, Q), 0) >= iota((Q, Q), 1))
    bias = jnp.where(visible, 0.0, FAR)
    raw, dt, cum = steps_of(step_ref, heads_ref)
    cum_t = cum.T
    first = iota((Q, 128), 1) < HEAD
    for pair in range(width // 128):
        cols = slice(128 * pair, 128 * pair + 128)
        conv = conv_of(ubuf, inner_ref, cols)
        conv_ref[:, cols] = conv
        x = silu(conv)
        cum_1 = wide(cum[:, 2 * pair : 2 * pair + 1])
        cum_2 = wide(cum[:, 2 * pair + 1 : 2 * pair + 2])
        m_1 = inner_cb * jnp.exp2(cum_1 - cum_t[2 * pair : 2 * pair + 1, :] + bias)
        m_2 = inner_cb * jnp.exp2(cum_2 - cum_t[2 * pair + 1 : 2 * pair + 2, :] + bias)
        xd = x * pair_of(first, dt, pair)
        mixers = jnp.concatenate([m_1.astype(BF16), m_2.astype(BF16)], axis=1)
        y = mm(mixers, stacked(first, xd.astype(BF16)))
        cum_p = jnp.where(first, cum_1, cum_2)
        last = cum_p[Q - 1 : Q, :]
        old = state[:, cols]
        old_low = old.astype(BF16)
        states_ref[0, :, cols] = old_low
        y = y + mm(c_low, old_low) * (jnp.exp2(cum_p) * keep)
        y_ref[:, cols] = y + inner_ref[5:6, cols] * x
        tail = jnp.exp2(last - cum_p) * tail_in
        carry = jnp.exp2(last) * keep[Q - 1 : Q, :]
        state[:, cols] = old * carry + mm(b_turn, (xd * tail).astype(BF16))


def backward_kernel(
    turn_ref, u_ref, s_ref, conv_ref, convs_ref, step_ref, aux_ref, seg_ref, grad_ref, states_ref,
    inner_ref, shared_ref, heads_ref,
    low_ref, inner_sum, shared_sum, heads_sum,
    dbuf, dsbuf, dstate, dcum_t, red, wgrad, xtail,
):
    width = u_ref.shape[1]
    chunk = pl.program_id(0)

    @pl.when(chunk == 0)
    def _():
        dbuf[Q : Q + 8, :] = jnp.zeros((8, width), F32)
        dsbuf[Q : Q + 8, :] = jnp.zeros((8, 2 * NS), F32)
        dstate[...] = jnp.zeros_like(dstate)
        dcum_t[...] = jnp.zeros_like(dcum_t)
        inner_sum[...] = jnp.zeros_like(inner_sum)
        shared_sum[...] = jnp.zeros_like(shared_sum)
        heads_sum[...] = jnp.zeros_like(heads_sum)

    @pl.when(chunk > 0)
    def _():
        dbuf[Q : Q + 8, :] = dbuf[0:8, :]
        dsbuf[Q : Q + 8, :] = dsbuf[0:8, :]

    aux = aux_ref[...]
    same = [wide(aux[:, 3 + k : 4 + k]) for k in range(3)]
    keep = wide(aux[:, 6:7])
    tail_in = wide(aux[:, 7:8])

    def silu_and_slope(v):
        sig = 0.5 + 0.5 * jnp.tanh(0.5 * v)
        act = v * sig
        return act, sig + act * (1.0 - sig)

    b_f, b_slope = silu_and_slope(convs_ref[:, 0:NS])
    c_f, c_slope = silu_and_slope(convs_ref[:, NS : 2 * NS])
    b_low = b_f.astype(BF16)
    c_low = c_f.astype(BF16)
    c_turn = c_f.T.astype(BF16)
    inner_bc = mm_t(b_low, c_low)
    row, column = iota((Q, Q), 0), iota((Q, Q), 1)
    visible = (wide(aux[:, 8:9]) == seg_ref[0]) & (row <= column)
    bias = jnp.where(visible, 0.0, FAR)
    lower_low = (row >= column).astype(BF16)
    strict = row < column
    raw, dt, cum = steps_of(step_ref, heads_ref)
    cum_t = cum.T
    first = iota((Q, 128), 1) < HEAD
    dinner = jnp.zeros((Q, Q), F32)
    for pair in range(width // 128):
        cols = slice(128 * pair, 128 * pair + 128)
        cum_1 = wide(cum[:, 2 * pair : 2 * pair + 1])
        cum_2 = wide(cum[:, 2 * pair + 1 : 2 * pair + 2])
        decay_1 = jnp.exp2(cum_t[2 * pair : 2 * pair + 1, :] - cum_1 + bias)
        decay_2 = jnp.exp2(cum_t[2 * pair + 1 : 2 * pair + 2, :] - cum_2 + bias)
        m_1 = inner_bc * decay_1
        m_2 = inner_bc * decay_2
        x, slope = silu_and_slope(conv_ref[:, cols])
        dt_p = pair_of(first, dt, pair)
        xd = x * dt_p
        grad = grad_ref[:, cols].astype(F32)
        grad_low = grad.astype(BF16)
        dm = mm_t(stacked(first, xd.astype(BF16)), grad_low)
        dm_1, dm_2 = dm[0:Q, :], dm[Q : 2 * Q, :]
        dinner = dinner + dm_1 * decay_1 + dm_2 * decay_2
        gaps = jnp.concatenate([(dm_1 * m_1).astype(BF16), (dm_2 * m_2).astype(BF16)], axis=0)
        spans = mm(gaps, lower_low)
        dcum_t[2 * pair : 2 * pair + 1, :] = jnp.sum(
            jnp.where(strict, spans[0:Q, :], 0.0), axis=0, keepdims=True
        )
        dcum_t[2 * pair + 1 : 2 * pair + 2, :] = jnp.sum(
            jnp.where(strict, spans[Q : 2 * Q, :], 0.0), axis=0, keepdims=True
        )
        mixers = jnp.concatenate([m_1.astype(BF16), m_2.astype(BF16)], axis=1)
        dxd = mm(mixers, stacked(first, grad_low))
        cum_p = jnp.where(first, cum_1, cum_2)
        last = cum_p[Q - 1 : Q, :]
        tail = jnp.exp2(last - cum_p) * tail_in
        later = dstate[:, cols]
        old_low = states_ref[0, :, cols]
        xt = xd * tail
        from_end = mm(b_low, later.astype(BF16))
        dxd = dxd + tail * from_end
        weight = jnp.exp2(cum_p) * keep
        wg = grad * weight
        from_start = mm(c_low, old_low)
        carry = jnp.exp2(last) * keep[Q - 1 : Q, :]
        carried = jnp.sum(later * old_low.astype(F32), axis=0, keepdims=True) * carry
        red[0:Q, cols] = (dxd * x).astype(BF16)
        red[Q : 2 * Q, cols] = (xt * from_end).astype(BF16)
        red[2 * Q : 3 * Q, cols] = (wg * from_start).astype(BF16)
        red[3 * Q : 3 * Q + 16, cols] = jnp.broadcast_to(carried, (16, 128)).astype(BF16)
        wg_low = wg.astype(BF16)
        wgrad[:, cols] = wg_low
        xtail[:, cols] = xt.astype(BF16)
        dx = dxd * dt_p + inner_ref[5:6, cols] * grad
        dbuf[0:Q, cols] = dx * slope
        inner_sum[5:6, cols] += jnp.sum(grad * x, axis=0, keepdims=True)

    to_head = (iota((width, 128), 0) // HEAD == iota((width, 128), 1)).astype(BF16)
    sums = mm(red[...], to_head)
    lower = (row >= column).astype(F32)
    upper = (row <= column).astype(F32)
    strict_lower = (row > column).astype(F32)
    dla = (
        dcum_t[...].T
        + jnp.dot(strict_lower, sums[Q : 2 * Q, :], precision=HIGH, preferred_element_type=F32)
        + jnp.dot(upper, sums[2 * Q : 3 * Q, :], precision=HIGH, preferred_element_type=F32)
        + sums[3 * Q : 3 * Q + 1, :]
    )
    rate = heads_ref[1:2, :]
    ddt = sums[0:Q, :] + rate * dla
    dstep = ddt * (0.5 + 0.5 * jnp.tanh(0.5 * raw))
    low_ref[:, width + 2 * NS : width + 2 * NS + 128] = dstep.astype(BF16)
    heads_sum[0:1, :] += jnp.sum(dstep, axis=0, keepdims=True)
    heads_sum[1:2, :] += jnp.sum(dla * dt * rate, axis=0, keepdims=True)

    dinner_low = dinner.astype(BF16)
    later_low = dstate[...].astype(BF16)
    db = mm(dinner_low, c_low) + mm_t(xtail[...], later_low)
    dc = mm(dinner.T.astype(BF16), b_low) + mm_t(wgrad[...], states_ref[0])
    dsbuf[0:Q, 0:NS] = db * b_slope
    dsbuf[0:Q, NS : 2 * NS] = dc * c_slope

    def conv_back(u, buf, weights, sums_ref, cols):
        d = buf[0:Q, cols]
        du = weights[3:4, cols] * d
        sums_ref[3:4, cols] += jnp.sum(d * u, axis=0, keepdims=True)
        sums_ref[4:5, cols] += jnp.sum(d, axis=0, keepdims=True)
        for shift in range(1, 4):
            d = buf[shift : Q + shift, cols] * same[shift - 1]
            du = du + weights[3 - shift : 4 - shift, cols] * d
            sums_ref[3 - shift : 4 - shift, cols] += jnp.sum(d * u, axis=0, keepdims=True)
        return du

    for part in range(2):
        cols = slice(NS * part, NS * part + NS)
        low_ref[:, width + NS * part : width + NS * part + NS] = conv_back(
            s_ref[:, cols].astype(F32), dsbuf, shared_ref, shared_sum, cols
        ).astype(BF16)
    new = mm(c_turn, wgrad[...])
    for pair in range(width // 128):
        cols = slice(128 * pair, 128 * pair + 128)
        low_ref[:, cols] = conv_back(
            u_ref[:, cols].astype(F32), dbuf, inner_ref, inner_sum, cols
        ).astype(BF16)
        cum_p = jnp.where(
            first[0:1, :],
            jnp.broadcast_to(cum[Q - 1 : Q, 2 * pair : 2 * pair + 1], (1, 128)),
            jnp.broadcast_to(cum[Q - 1 : Q, 2 * pair + 1 : 2 * pair + 2], (1, 128)),
        )
        carry = jnp.exp2(cum_p) * keep[Q - 1 : Q, :]
        dstate[:, cols] = dstate[:, cols] * carry + new[:, cols]


VMEM_LIMIT = 48 * 1024 * 1024


def forward_mix(turn, proj, aux, seg_rows, inner_p, shared_p, heads_p):
    length = proj.shape[0]
    width = inner_p.shape[1]
    chunks = length // Q

    def rows(n, at=0):
        return pl.BlockSpec((Q, n), lambda c, turn: (lax.rem(c + turn[0], chunks), at))

    def plain(n):
        return pl.BlockSpec((Q, n), lambda c, turn: (c, 0))

    def whole(n):
        return pl.BlockSpec((8, n), lambda c, turn: (0, 0))

    line = pl.BlockSpec((1, 1, Q), lambda c, turn: (c, 0, 0))
    kept = pl.BlockSpec((1, NS, width), lambda c, turn: (c, 0, 0))
    return pl.pallas_call(
        forward_kernel,
        grid_spec=pltpu.PrefetchScalarGridSpec(
            num_scalar_prefetch=1,
            grid=(chunks,),
            in_specs=[
                rows(width), rows(2 * NS, width // (2 * NS)), rows(128, (width + 2 * NS) // 128),
                plain(16), line, whole(width), whole(2 * NS), whole(128),
            ],
            out_specs=[rows(width), plain(width), plain(2 * NS), kept],
            scratch_shapes=[
                pltpu.VMEM((Q + 8, width), F32),
                pltpu.VMEM((Q + 8, 2 * NS), F32),
                pltpu.VMEM((NS, width), F32),
            ],
        ),
        out_shape=[
            jax.ShapeDtypeStruct((length, width), F32),
            jax.ShapeDtypeStruct((length, width), F32),
            jax.ShapeDtypeStruct((length, 2 * NS), F32),
            jax.ShapeDtypeStruct((chunks, NS, width), BF16),
        ],
        compiler_params=pltpu.CompilerParams(vmem_limit_bytes=VMEM_LIMIT),
        cost_estimate=pl.CostEstimate(
            flops=32 * length * 128 * width, bytes_accessed=12 * length * width, transcendentals=0
        ),
        name="mix_forward",
    )(turn, proj, proj, proj, aux, seg_rows, inner_p, shared_p, heads_p)


def backward_mix(turn, proj, conv, convs, aux, seg_rows, grad, states, inner_p, shared_p, heads_p):
    length = proj.shape[0]
    width = inner_p.shape[1]
    chunks = length // Q

    def rows(n, at=0):
        return pl.BlockSpec(
            (Q, n), lambda c, turn: (lax.rem(chunks - 1 - c + turn[0], chunks), at)
        )

    def plain(n):
        return pl.BlockSpec((Q, n), lambda c, turn: (chunks - 1 - c, 0))

    def whole(n):
        return pl.BlockSpec((8, n), lambda c, turn: (0, 0))

    line = pl.BlockSpec((1, 1, Q), lambda c, turn: (chunks - 1 - c, 0, 0))
    kept = pl.BlockSpec((1, NS, width), lambda c, turn: (chunks - 1 - c, 0, 0))
    return pl.pallas_call(
        backward_kernel,
        grid_spec=pltpu.PrefetchScalarGridSpec(
            num_scalar_prefetch=1,
            grid=(chunks,),
            in_specs=[
                rows(width), rows(2 * NS, width // (2 * NS)), plain(width), plain(2 * NS),
                rows(128, (width + 2 * NS) // 128), plain(16), line, rows(width), kept,
                whole(width), whole(2 * NS), whole(128),
            ],
            out_specs=[rows(width + 2 * NS + 128), whole(width), whole(2 * NS), whole(128)],
            scratch_shapes=[
                pltpu.VMEM((Q + 8, width), F32),
                pltpu.VMEM((Q + 8, 2 * NS), F32),
                pltpu.VMEM((NS, width), F32),
                pltpu.VMEM((128, Q), F32),
                pltpu.VMEM((3 * Q + 16, width), BF16),
                pltpu.VMEM((Q, width), BF16),
                pltpu.VMEM((Q, width), BF16),
            ],
        ),
        out_shape=[
            jax.ShapeDtypeStruct((length, width + 2 * NS + 128), BF16),
            jax.ShapeDtypeStruct((8, width), F32),
            jax.ShapeDtypeStruct((8, 2 * NS), F32),
            jax.ShapeDtypeStruct((8, 128), F32),
        ],
        compiler_params=pltpu.CompilerParams(vmem_limit_bytes=VMEM_LIMIT),
        cost_estimate=pl.CostEstimate(
            flops=70 * length * 128 * width, bytes_accessed=20 * length * width, transcendentals=0
        ),
        name="mix_backward",
    )(turn, proj, proj, conv, convs, proj, aux, seg_rows, grad, states, inner_p, shared_p, heads_p)


def aux_of(seg_line):
    length = seg_line.shape[0]
    ends = seg_line.reshape(-1, Q)[:, Q - 1]
    prior = jnp.concatenate([jnp.full((1,), -1, seg_line.dtype), ends[:-1]])
    place = jnp.arange(length)
    columns = []
    for shift in range(1, 4):
        columns.append((jnp.roll(seg_line, shift) == seg_line) & (place >= shift))
    for shift in range(1, 4):
        columns.append((jnp.roll(seg_line, -shift) == seg_line) & (place < length - shift))
    columns.append(seg_line == jnp.repeat(prior, Q))
    columns.append(seg_line == jnp.repeat(ends, Q))
    columns = [column.astype(F32) for column in columns] + [seg_line.astype(F32)]
    columns += [jnp.zeros((length,), F32)] * (16 - len(columns))
    rows = seg_line.astype(F32).reshape(-1, 1, Q)
    return jnp.stack(columns, axis=1), rows


def silu_of(v):
    return v * jax.nn.sigmoid(v)


def program(sizes, args):
    (
        hidden, norm_gain, weight_gate, weight_inner, weight_shared, weight_step,
        filter_inner, bias_inner, filter_shared, bias_shared, step_bias, log_rate, skip_gain,
        gate_gain, weight_out, segments, cotangent,
    ) = args
    n_fsdp, n_tp = sizes
    width = weight_gate.shape[1]
    heads = weight_step.shape[1]
    own_rows = hidden.shape[0]
    length = segments.shape[1]
    tp_place = lax.axis_index("tp")
    paired = n_tp == 2

    def tp_rows(own):
        if paired:
            return jnp.concatenate([own, lax.ppermute(own, "tp", [(0, 1), (1, 0)])], axis=0)
        return lax.all_gather(own, "tp", axis=0, tiled=True)

    def tp_scatter(part):
        if paired:
            away = lax.ppermute(part[own_rows:].astype(BF16), "tp", [(0, 1), (1, 0)])
            return part[:own_rows] + away.astype(F32)
        return lax.psum_scatter(part, "tp", scatter_dimension=0, tiled=True)

    def gather(shard):
        return lax.all_gather(shard, "fsdp", axis=0, tiled=True)

    fsdp_place = lax.axis_index("fsdp")
    outer = n_fsdp // 2
    digits = [(4, n_fsdp // 4), (outer // 4, 2), (2, 1)] if outer % 4 == 0 else [(outer, 2), (2, 1)]

    def line_gather(shard):
        blocks = shard
        for axis, (size, stride) in enumerate(digits):
            place = lax.rem(fsdp_place // stride, size)
            parts = [blocks]
            for step in range(1, size):
                moves = []
                for i in range(n_fsdp):
                    at = (i // stride) % size
                    moves.append((i, i + ((at + step) % size - at) * stride))
                parts.append(lax.ppermute(blocks, "fsdp", moves))
            if size == 2:
                own, away = parts
                blocks = jnp.where(
                    place == 0,
                    jnp.stack([own, away], axis=axis),
                    jnp.stack([away, own], axis=axis),
                )
            elif size > 2:
                ring = jnp.stack(parts[::-1] + parts[::-1], axis=axis)
                blocks = lax.dynamic_slice_in_dim(ring, size - 1 - place, size, axis)
            else:
                blocks = jnp.expand_dims(blocks, axis)
        return blocks.reshape(n_fsdp * shard.shape[0], shard.shape[1])

    def core_sum(total):
        rows = total.shape[0] // n_fsdp
        blocks = total.reshape(outer, 2, rows, total.shape[1])
        even = lax.rem(fsdp_place, 2) == 0
        mine = jnp.where(even, blocks[:, 0], blocks[:, 1])
        away = jnp.where(even, blocks[:, 1], blocks[:, 0])
        got = lax.ppermute(away, "fsdp", [(i, i ^ 1) for i in range(n_fsdp)])
        return (mine.astype(F32) + got.astype(F32)).astype(BF16).reshape(outer * rows, -1)

    def chip_swap(half):
        groups = [[i for i in range(n_fsdp) if i % 2 == core] for core in range(2)]
        return lax.all_to_all(half, "fsdp", 0, 0, axis_index_groups=groups, tiled=True)

    def chip_sum(swapped):
        return jnp.sum(swapped.reshape(outer, -1, swapped.shape[1]).astype(F32), axis=0)

    def butterfly(value):
        reach = 1
        while reach < n_fsdp:
            value = value + lax.ppermute(
                value, "fsdp", [(i, i ^ reach) for i in range(n_fsdp)]
            )
            reach *= 2
        return value

    pad = jnp.zeros((weight_step.shape[0], 128 - heads - 1), BF16)
    shard_a = jnp.concatenate(
        [weight_inner, weight_shared, weight_step, norm_gain[:, None], pad], axis=1
    )
    hidden_all = tp_rows(hidden)
    weights_a = line_gather(shard_a)
    weights_b = gather(jnp.concatenate([weight_gate, weight_out], axis=1))
    gate_all, out_all = weights_b[:, :width], weights_b[:, width:]
    cot_all = tp_rows(cotangent)
    gain_row = weights_a[:, width + 2 * NS + heads].astype(F32)[None, :]

    hidden_f = hidden_all.astype(F32)
    inv_rms = lax.rsqrt(jnp.mean(hidden_f * hidden_f, axis=1, keepdims=True) + EPSILON)
    normed = (hidden_f * inv_rms * gain_row).astype(BF16)
    proj = mm(normed, weights_a).astype(BF16)

    turn = (tp_place * (own_rows // Q) if paired else jnp.zeros((), jnp.int32)).reshape(1)
    turn = turn.astype(jnp.int32)
    aux, seg_rows = aux_of(segments[0])
    skip_lanes = jnp.repeat(skip_gain.astype(F32), HEAD)
    inner_p = jnp.concatenate(
        [filter_inner.astype(F32), bias_inner.astype(F32)[None], skip_lanes[None],
         jnp.zeros((2, width), F32)], axis=0)
    shared_p = jnp.concatenate(
        [filter_shared.astype(F32), bias_shared.astype(F32)[None], jnp.zeros((3, 2 * NS), F32)],
        axis=0,
    )
    heads_p = jnp.pad(
        jnp.stack([step_bias.astype(F32), -jnp.exp(log_rate.astype(F32))]),
        ((0, 6), (0, 128 - heads)),
    )
    y, conv, convs, states = forward_mix(turn, proj, aux, seg_rows, inner_p, shared_p, heads_p)

    y, gate_all, out_all, cot_all = lax.optimization_barrier((y, gate_all, out_all, cot_all))
    gate_z = mm(normed, gate_all).astype(BF16).astype(F32)
    grad_gated = mm(cot_all, out_all)
    gain_gate = gate_gain.astype(F32)[None, :]
    sig = jax.nn.sigmoid(gate_z)
    act = gate_z * sig
    mixed = y * act
    scaled = grad_gated * gain_gate
    sums = jnp.stack([jnp.sum(mixed * mixed, axis=1), jnp.sum(mixed * scaled, axis=1)], axis=1)
    if paired:
        half = jnp.concatenate([sums[own_rows:], sums[:own_rows]], axis=0)
        sums = sums + lax.ppermute(half, "tp", [(0, 1), (1, 0)])
    else:
        sums = lax.psum(sums, "tp")
    inv_gate = lax.rsqrt(sums[:, 0:1] / INNER + EPSILON)
    gated = (mixed * inv_gate * gain_gate).astype(BF16)
    grad_mixed = inv_gate * scaled - mixed * (inv_gate * inv_gate * inv_gate) * (
        sums[:, 1:2] / INNER
    )
    grad_y = grad_mixed * act
    low_z = (grad_mixed * y * (sig + act * (1.0 - sig))).astype(BF16)
    grad_gain_gate = jnp.sum(grad_gated * mixed * inv_gate, axis=0)
    grads_b = jnp.concatenate(
        [weight_grad(normed, low_z), weight_grad(cot_all, gated)], axis=1
    ).astype(BF16)
    out_part = mm_t(gated, out_all)
    half_b = core_sum(grads_b)
    half_b, grad_y, out_part = lax.optimization_barrier((half_b, grad_y, out_part))
    swap_b = chip_swap(half_b)
    out_own = tp_scatter(out_part)
    layer_out = (hidden.astype(F32) + out_own).astype(BF16)

    low, inner_sum, shared_sum, heads_sum = backward_mix(
        turn, proj, conv, convs, aux, seg_rows, grad_y, states, inner_p, shared_p, heads_p
    )
    grads_a = weight_grad(normed, low).astype(BF16)
    half_a = core_sum(grads_a)
    small = butterfly(
        jnp.concatenate(
            [jnp.concatenate([inner_sum[:6], grad_gain_gate[None], inner_sum[7:]], axis=0),
             shared_sum, heads_sum], axis=1)
    )
    input_part = mm_t(low_z, gate_all) + mm_t(low, weights_a)
    half_a, input_part = lax.optimization_barrier((half_a, input_part))
    swap_a = chip_swap(half_a)
    grad_normed = tp_scatter(input_part)
    x_hat = hidden.astype(F32) * inv_rms[:own_rows] if paired else None
    inv_own = inv_rms[:own_rows]
    if not paired:
        inv_own = lax.dynamic_slice_in_dim(inv_rms, tp_place * own_rows, own_rows, 0)
        x_hat = hidden.astype(F32) * inv_own
    scaled_in = grad_normed * gain_row
    grad_hidden = cotangent.astype(F32) + inv_own * (
        scaled_in - x_hat * jnp.mean(scaled_in * x_hat, axis=1, keepdims=True)
    )

    swap_a, grad_hidden, small = lax.optimization_barrier((swap_a, grad_hidden, small))
    owned_a, owned_b = chip_sum(swap_a), chip_sum(swap_b)
    grad_gate, grad_out = owned_b[:, :width], owned_b[:, width:]
    grad_inner = owned_a[:, :width]
    grad_shared = owned_a[:, width : width + 2 * NS]
    grad_step = owned_a[:, width + 2 * NS : width + 2 * NS + heads]
    gain_own = (
        jnp.sum(weight_gate.astype(F32) * grad_gate, axis=1)
        + jnp.sum(weight_inner.astype(F32) * grad_inner, axis=1)
        + jnp.sum(weight_shared.astype(F32) * grad_shared, axis=1)
        + jnp.sum(weight_step.astype(F32) * grad_step, axis=1)
    )
    shared_part = small[:, width : width + 2 * NS]
    packed = jnp.concatenate(
        [grad_shared, shared_part, jnp.pad(
            gain_own[None], ((0, 7), (0, 2 * NS - gain_own.shape[0])))], axis=0)
    if paired:
        packed = packed + lax.ppermute(packed, "tp", [(0, 1), (1, 0)])
    else:
        packed = lax.psum(packed, "tp")
    owned = grad_shared.shape[0]
    grad_shared, shared_part = packed[:owned], packed[owned : owned + 8]
    gain_own = packed[owned + 8, : gain_own.shape[0]]
    grad_norm_gain = gain_own / norm_gain.astype(F32)
    head_part = small[:, width + 2 * NS :]
    return (
        layer_out,
        grad_hidden,
        grad_norm_gain,
        grad_gate,
        grad_inner,
        grad_shared,
        grad_step,
        small[0:4, :width],
        small[4, :width],
        shared_part[0:4],
        shared_part[4],
        head_part[0, :heads],
        head_part[1, :heads],
        jnp.sum(small[5, :width].reshape(heads, HEAD), axis=1),
        small[6, :width],
        grad_out,
    )


def solution(mesh):
    sizes = (mesh.shape["fsdp"], mesh.shape["tp"])

    def per_device(*args):
        return program(sizes, args)

    return jax.shard_map(
        per_device,
        mesh=mesh,
        in_specs=(
            P(("fsdp", "tp"), None),
            P("fsdp"),
            P("fsdp", "tp"),
            P("fsdp", "tp"),
            P("fsdp", None),
            P("fsdp", "tp"),
            P(None, "tp"),
            P("tp"),
            P(),
            P(),
            P("tp"),
            P("tp"),
            P("tp"),
            P("tp"),
            P("fsdp", "tp"),
            P("fsdp", None),
            P(("fsdp", "tp"), None),
        ),
        out_specs=(
            P(("fsdp", "tp"), None),
            P(("fsdp", "tp"), None),
            P("fsdp"),
            P("fsdp", "tp"),
            P("fsdp", "tp"),
            P("fsdp", None),
            P("fsdp", "tp"),
            P(None, "tp"),
            P("tp"),
            P(),
            P(),
            P("tp"),
            P("tp"),
            P("tp"),
            P("tp"),
            P("fsdp", "tp"),
        ),
        check_vma=False,
    )
```

```python
import jax
import jax.numpy as jnp
from jax import lax
from jax.experimental import pallas as pl
from jax.experimental.pallas import tpu as pltpu
from jax.sharding import PartitionSpec as P

INNER = 2048
NS = 128
HEAD = 64
Q = 128
LOG2E = 1.4426950408889634
FAR = -1e30
EPSILON = 1e-05

F32 = jnp.float32
BF16 = jnp.bfloat16
HIGH = lax.Precision.HIGHEST


def mm(a, b):
    return jnp.dot(a, b, preferred_element_type=F32)


def mm_t(a, b):
    return lax.dot_general(a, b, (((1,), (1,)), ((), ())), preferred_element_type=F32)


def weight_grad(a, b):
    return lax.dot_general(a, b, (((0,), (0,)), ((), ())), preferred_element_type=F32)


def iota(shape, dim):
    return lax.broadcasted_iota(jnp.int32, shape, dim)


def softplus(v):
    return jnp.maximum(v, 0.0) + jnp.log1p(jnp.exp(-jnp.abs(v)))


def wide(column):
    return jnp.broadcast_to(column, (Q, 128))


def pair_of(first, array, pair):
    return jnp.where(
        first, wide(array[:, 2 * pair : 2 * pair + 1]), wide(array[:, 2 * pair + 1 : 2 * pair + 2])
    )


def skip_of(first, heads_ref, pair):
    line = heads_ref[2:3, :]
    return jnp.where(
        first,
        jnp.broadcast_to(line[:, 2 * pair : 2 * pair + 1], (1, 128)),
        jnp.broadcast_to(line[:, 2 * pair + 1 : 2 * pair + 2], (1, 128)),
    )


def folded(block):
    return jnp.sum(block.reshape(Q // 8, 8, 128), axis=0)


def stacked(first, block):
    nil = jnp.zeros_like(block)
    return jnp.concatenate([jnp.where(first, block, nil), jnp.where(first, nil, block)], axis=0)


def forward_kernel(
    turn_ref, u_ref, s_ref, step_ref, aux_ref, seg_ref,
    inner_ref, inner_bias_ref, shared_ref, shared_bias_ref, heads_ref,
    y_ref, conv_ref, convs_ref, states_ref, steps_ref,
    ubuf, sbuf, state, xtail,
):
    width = u_ref.shape[1]
    chunk = pl.program_id(0)

    @pl.when(chunk == 0)
    def _():
        ubuf[0:8, :] = jnp.zeros((8, width), F32)
        sbuf[0:8, :] = jnp.zeros((8, 2 * NS), F32)
        state[...] = jnp.zeros_like(state)

    @pl.when(chunk > 0)
    def _():
        ubuf[0:8, :] = ubuf[Q : Q + 8, :]
        sbuf[0:8, :] = sbuf[Q : Q + 8, :]

    ubuf[8 : Q + 8, :] = u_ref[...].astype(F32)
    sbuf[8 : Q + 8, :] = s_ref[...].astype(F32)
    aux = aux_ref[...]
    same = [wide(aux[:, k : k + 1]) for k in range(3)]
    keep = wide(aux[:, 6:7])
    tail_in = wide(aux[:, 7:8])

    def conv_of(buf, taps_ref, bias_ref, cols):
        weights = taps_ref[:, cols].astype(F32)
        total = bias_ref[:, cols].astype(F32) + weights[3:4] * buf[8 : Q + 8, cols]
        for shift in range(1, 4):
            total = total + weights[3 - shift : 4 - shift] * (
                buf[8 - shift : Q + 8 - shift, cols] * same[shift - 1]
            )
        return total

    def silu(v):
        return v * (0.5 + 0.5 * jnp.tanh(0.5 * v))

    conv_b = conv_of(sbuf, shared_ref, shared_bias_ref, slice(0, NS))
    conv_c = conv_of(sbuf, shared_ref, shared_bias_ref, slice(NS, 2 * NS))
    convs_ref[:, 0:NS] = conv_b
    convs_ref[:, NS : 2 * NS] = conv_c
    b_f = silu(conv_b)
    b_low = b_f.astype(BF16)
    b_turn = b_f.T.astype(BF16)
    c_low = silu(conv_c).astype(BF16)
    inner_cb = mm_t(c_low, b_low)
    visible = (wide(aux[:, 8:9]) == seg_ref[0]) & (iota((Q, Q), 0) >= iota((Q, Q), 1))
    bias = jnp.where(visible, 0.0, FAR)
    dt = softplus(step_ref[...].astype(F32) + heads_ref[0:1, :])
    lower = (iota((Q, Q), 0) >= iota((Q, Q), 1)).astype(BF16)
    rest = dt * (heads_ref[1:2, :] * LOG2E)
    cum = jnp.zeros((Q, 128), F32)
    for _ in range(3):
        piece = rest.astype(BF16)
        cum = cum + mm(lower, piece)
        rest = rest - piece.astype(F32)
    cum_t = cum.T
    steps_ref[0, 0] = dt
    steps_ref[0, 1] = cum
    steps_ref[0, 2] = cum_t
    first = iota((Q, 128), 1) < HEAD
    state_low = state[...].astype(BF16)
    states_ref[0] = state_low
    carried = mm(c_low, state_low)
    for pair in range(width // 128):
        cols = slice(128 * pair, 128 * pair + 128)
        conv = conv_of(ubuf, inner_ref, inner_bias_ref, cols)
        conv_ref[:, cols] = conv
        x = silu(conv)
        cum_1 = wide(cum[:, 2 * pair : 2 * pair + 1])
        cum_2 = wide(cum[:, 2 * pair + 1 : 2 * pair + 2])
        m_1 = inner_cb * jnp.exp2(cum_1 - cum_t[2 * pair : 2 * pair + 1, :] + bias)
        m_2 = inner_cb * jnp.exp2(cum_2 - cum_t[2 * pair + 1 : 2 * pair + 2, :] + bias)
        xd = x * pair_of(first, dt, pair)
        mixers = jnp.concatenate([m_1.astype(BF16), m_2.astype(BF16)], axis=1)
        y = mm(mixers, stacked(first, xd.astype(BF16)))
        cum_p = jnp.where(first, cum_1, cum_2)
        last = cum_p[Q - 1 : Q, :]
        y = y + carried[:, cols] * (jnp.exp2(cum_p) * keep)
        y_ref[:, cols] = (y + skip_of(first[0:1], heads_ref, pair) * x).astype(BF16)
        tail = jnp.exp2(last - cum_p) * tail_in
        xtail[:, cols] = (xd * tail).astype(BF16)
        state[:, cols] = state[:, cols] * (jnp.exp2(last) * keep[Q - 1 : Q, :])
    state[...] += mm(b_turn, xtail[...])


def backward_kernel(
    turn_ref, u_ref, s_ref, conv_ref, convs_ref, step_ref, steps_ref, aux_ref, seg_ref, grad_ref, states_ref,
    inner_ref, shared_ref, heads_ref,
    low_ref, inner_sum, shared_sum, heads_sum,
    dbuf, dsbuf, dstate, dcum_t, red, wgrad, xtail, to_head, lower_low, inner_acc, shared_acc,
):
    width = u_ref.shape[1]
    chunk = pl.program_id(0)

    @pl.when(chunk == 0)
    def _():
        dbuf[Q : Q + 8, :] = jnp.zeros((8, width), F32)
        dsbuf[Q : Q + 8, :] = jnp.zeros((8, 2 * NS), F32)
        dstate[...] = jnp.zeros_like(dstate)
        dcum_t[...] = jnp.zeros_like(dcum_t)
        inner_acc[...] = jnp.zeros_like(inner_acc)
        shared_acc[...] = jnp.zeros_like(shared_acc)
        heads_sum[...] = jnp.zeros_like(heads_sum)
        to_head[...] = (
            iota((width, 128), 0) // HEAD == iota((width, 128), 1)
        ).astype(BF16)
        row_2, column_2 = iota((2 * Q, 2 * Q), 0), iota((2 * Q, 2 * Q), 1)
        lower_low[...] = ((row_2 // Q == column_2 // Q) & (row_2 >= column_2)).astype(BF16)

    @pl.when(chunk > 0)
    def _():
        dbuf[Q : Q + 8, :] = dbuf[0:8, :]
        dsbuf[Q : Q + 8, :] = dsbuf[0:8, :]

    aux = aux_ref[...]
    same = [wide(aux[:, 3 + k : 4 + k]) for k in range(3)]
    keep = wide(aux[:, 6:7])
    tail_in = wide(aux[:, 7:8])

    def silu_and_slope(v):
        sig = 0.5 + 0.5 * jnp.tanh(0.5 * v)
        act = v * sig
        return act, sig + act * (1.0 - sig)

    b_f, b_slope = silu_and_slope(convs_ref[:, 0:NS])
    c_f, c_slope = silu_and_slope(convs_ref[:, NS : 2 * NS])
    b_low = b_f.astype(BF16)
    c_low = c_f.astype(BF16)
    c_turn = c_f.T.astype(BF16)
    inner_bc = mm_t(b_low, c_low)
    row, column = iota((Q, Q), 0), iota((Q, Q), 1)
    visible = (wide(aux[:, 8:9]) == seg_ref[0]) & (row <= column)
    bias = jnp.where(visible, 0.0, FAR)
    strict = jnp.concatenate([row < column, row < column], axis=1)
    inner_2 = jnp.concatenate([inner_bc, inner_bc], axis=1)
    bias_2 = jnp.concatenate([bias, bias], axis=1)
    raw = step_ref[...].astype(F32) + heads_ref[0:1, :]
    dt, cum, cum_t = steps_ref[0, 0], steps_ref[0, 1], steps_ref[0, 2]
    first = iota((Q, 128), 1) < HEAD
    dinner = jnp.zeros((Q, 2 * Q), F32)
    later_low = dstate[...].astype(BF16)
    end_all = mm(b_low, later_low)
    start_all = mm(c_low, states_ref[0])
    for pair in range(width // 128):
        cols = slice(128 * pair, 128 * pair + 128)
        cum_1 = wide(cum[:, 2 * pair : 2 * pair + 1])
        cum_2 = wide(cum[:, 2 * pair + 1 : 2 * pair + 2])
        ahead = jnp.concatenate(
            [cum_t[2 * pair : 2 * pair + 1, :], cum_t[2 * pair + 1 : 2 * pair + 2, :]], axis=1
        )
        decay = jnp.exp2(ahead - jnp.concatenate([cum_1, cum_2], axis=1) + bias_2)
        m = inner_2 * decay
        x, slope = silu_and_slope(conv_ref[:, cols])
        dt_p = pair_of(first, dt, pair)
        xd = x * dt_p
        grad = grad_ref[:, cols].astype(F32)
        grad_two = stacked(first, grad_ref[:, cols].astype(BF16))
        dm = mm_t(xd.astype(BF16), grad_two)
        dinner = dinner + dm * decay
        spans = mm((dm * m).astype(BF16), lower_low[...])
        gaps = jnp.sum(jnp.where(strict, spans, 0.0), axis=0, keepdims=True)
        dcum_t[2 * pair : 2 * pair + 1, :] = gaps[:, 0:Q]
        dcum_t[2 * pair + 1 : 2 * pair + 2, :] = gaps[:, Q : 2 * Q]
        dxd = mm(m.astype(BF16), grad_two)
        cum_p = jnp.where(first, cum_1, cum_2)
        last = cum_p[Q - 1 : Q, :]
        tail = jnp.exp2(last - cum_p) * tail_in
        later = dstate[:, cols]
        old_low = states_ref[0, :, cols]
        xt = xd * tail
        from_end = end_all[:, cols]
        dxd = dxd + tail * from_end
        weight = jnp.exp2(cum_p) * keep
        wg = grad * weight
        from_start = start_all[:, cols]
        carry = jnp.exp2(last) * keep[Q - 1 : Q, :]
        carried = jnp.sum(later * old_low.astype(F32), axis=0, keepdims=True) * carry
        red[0:Q, cols] = (dxd * x).astype(BF16)
        red[Q : 2 * Q, cols] = (xt * from_end).astype(BF16)
        red[2 * Q : 3 * Q, cols] = (wg * from_start).astype(BF16)
        red[3 * Q : 3 * Q + 16, cols] = jnp.broadcast_to(carried, (16, 128)).astype(BF16)
        wg_low = wg.astype(BF16)
        wgrad[:, cols] = wg_low
        xtail[:, cols] = xt.astype(BF16)
        dx = dxd * dt_p + skip_of(first[0:1], heads_ref, pair) * grad
        dbuf[0:Q, cols] = dx * slope
        inner_acc[40:48, cols] += folded(grad * x)

    sums = mm(red[...], to_head[...])
    spread = jnp.concatenate([(row > column).astype(BF16), (row <= column).astype(BF16)], axis=1)
    dla = dcum_t[...].T + mm(spread, sums[Q : 3 * Q, :].astype(BF16)) + sums[3 * Q : 3 * Q + 1, :]
    rate = heads_ref[1:2, :]
    ddt = sums[0:Q, :] + rate * dla
    dstep = ddt * (0.5 + 0.5 * jnp.tanh(0.5 * raw))
    low_ref[:, width + 2 * NS : width + 2 * NS + 128] = dstep.astype(BF16)
    heads_sum[0:1, :] += jnp.sum(dstep, axis=0, keepdims=True)
    heads_sum[1:2, :] += jnp.sum(dla * dt * rate, axis=0, keepdims=True)

    dinner = dinner[:, 0:Q] + dinner[:, Q : 2 * Q]
    dinner_low = dinner.astype(BF16)
    db = mm(dinner_low, c_low) + mm_t(xtail[...], later_low)
    dc = mm(dinner.T.astype(BF16), b_low) + mm_t(wgrad[...], states_ref[0])
    dsbuf[0:Q, 0:NS] = db * b_slope
    dsbuf[0:Q, NS : 2 * NS] = dc * c_slope

    def conv_back(u, buf, taps_ref, acc, cols):
        weights = taps_ref[:, cols].astype(F32)
        d = buf[0:Q, cols]
        du = weights[3:4] * d
        acc[24:32, cols] += folded(d * u)
        acc[32:40, cols] += folded(d)
        for shift in range(1, 4):
            d = buf[shift : Q + shift, cols] * same[shift - 1]
            du = du + weights[3 - shift : 4 - shift] * d
            acc[24 - 8 * shift : 32 - 8 * shift, cols] += folded(d * u)
        return du

    for part in range(2):
        cols = slice(NS * part, NS * part + NS)
        low_ref[:, width + NS * part : width + NS * part + NS] = conv_back(
            s_ref[:, cols].astype(F32), dsbuf, shared_ref, shared_acc, cols
        ).astype(BF16)
    new = mm(c_turn, wgrad[...])
    for pair in range(width // 128):
        cols = slice(128 * pair, 128 * pair + 128)
        low_ref[:, cols] = conv_back(
            u_ref[:, cols].astype(F32), dbuf, inner_ref, inner_acc, cols
        ).astype(BF16)
        cum_p = jnp.where(
            first[0:1, :],
            jnp.broadcast_to(cum[Q - 1 : Q, 2 * pair : 2 * pair + 1], (1, 128)),
            jnp.broadcast_to(cum[Q - 1 : Q, 2 * pair + 1 : 2 * pair + 2], (1, 128)),
        )
        carry = jnp.exp2(cum_p) * keep[Q - 1 : Q, :]
        dstate[:, cols] = dstate[:, cols] * carry + new[:, cols]

    @pl.when(chunk == pl.num_programs(0) - 1)
    def _():
        for out, acc, count in ((inner_sum, inner_acc, 6), (shared_sum, shared_acc, 5)):
            out[...] = jnp.zeros_like(out)
            for k in range(count):
                out[k : k + 1, :] = jnp.sum(acc[8 * k : 8 * k + 8, :], axis=0, keepdims=True)


VMEM_LIMIT = 60 * 1024 * 1024


def forward_mix(turn, proj, aux, seg_rows, inner_p, inner_b, shared_p, shared_b, heads_p):
    length = proj.shape[0]
    width = inner_p.shape[1]
    chunks = length // Q

    def rows(n, at=0):
        return pl.BlockSpec((Q, n), lambda c, turn: (lax.rem(c + turn[0], chunks), at))

    def plain(n):
        return pl.BlockSpec((Q, n), lambda c, turn: (c, 0))

    def whole(n, rows=8):
        return pl.BlockSpec((rows, n), lambda c, turn: (0, 0))

    line = pl.BlockSpec((1, 1, Q), lambda c, turn: (c, 0, 0))
    kept = pl.BlockSpec((1, NS, width), lambda c, turn: (c, 0, 0))
    return pl.pallas_call(
        forward_kernel,
        grid_spec=pltpu.PrefetchScalarGridSpec(
            num_scalar_prefetch=1,
            grid=(chunks,),
            in_specs=[
                rows(width), rows(2 * NS, width // (2 * NS)), rows(128, (width + 2 * NS) // 128),
                plain(16), line, whole(width, 4), whole(width, 1), whole(2 * NS, 4),
                whole(2 * NS, 1), whole(128),
            ],
            out_specs=[
                rows(width), plain(width), plain(2 * NS), kept,
                pl.BlockSpec((1, 3, Q, 128), lambda c, turn: (c, 0, 0, 0)),
            ],
            scratch_shapes=[
                pltpu.VMEM((Q + 8, width), F32),
                pltpu.VMEM((Q + 8, 2 * NS), F32),
                pltpu.VMEM((NS, width), F32),
                pltpu.VMEM((Q, width), BF16),
            ],
        ),
        out_shape=[
            jax.ShapeDtypeStruct((length, width), BF16),
            jax.ShapeDtypeStruct((length, width), F32),
            jax.ShapeDtypeStruct((length, 2 * NS), F32),
            jax.ShapeDtypeStruct((chunks, NS, width), BF16),
            jax.ShapeDtypeStruct((chunks, 3, Q, 128), F32),
        ],
        compiler_params=pltpu.CompilerParams(vmem_limit_bytes=VMEM_LIMIT),
        cost_estimate=pl.CostEstimate(
            flops=32 * length * 128 * width, bytes_accessed=12 * length * width, transcendentals=0
        ),
        name="mix_forward",
    )(turn, proj, proj, proj, aux, seg_rows, inner_p, inner_b, shared_p, shared_b, heads_p)


def backward_mix(turn, proj, conv, convs, steps, aux, seg_rows, grad, states, inner_p, shared_p, heads_p):
    length = proj.shape[0]
    width = inner_p.shape[1]
    chunks = length // Q

    def rows(n, at=0):
        return pl.BlockSpec(
            (Q, n), lambda c, turn: (lax.rem(chunks - 1 - c + turn[0], chunks), at)
        )

    def plain(n):
        return pl.BlockSpec((Q, n), lambda c, turn: (chunks - 1 - c, 0))

    def whole(n, rows=8):
        return pl.BlockSpec((rows, n), lambda c, turn: (0, 0))

    line = pl.BlockSpec((1, 1, Q), lambda c, turn: (chunks - 1 - c, 0, 0))
    kept = pl.BlockSpec((1, NS, width), lambda c, turn: (chunks - 1 - c, 0, 0))
    return pl.pallas_call(
        backward_kernel,
        grid_spec=pltpu.PrefetchScalarGridSpec(
            num_scalar_prefetch=1,
            grid=(chunks,),
            in_specs=[
                rows(width), rows(2 * NS, width // (2 * NS)), plain(width), plain(2 * NS),
                rows(128, (width + 2 * NS) // 128),
                pl.BlockSpec((1, 3, Q, 128), lambda c, turn: (chunks - 1 - c, 0, 0, 0)),
                plain(16), line, rows(width), kept,
                whole(width, 4), whole(2 * NS, 4), whole(128),
            ],
            out_specs=[rows(width + 2 * NS + 128), whole(width), whole(2 * NS), whole(128)],
            scratch_shapes=[
                pltpu.VMEM((Q + 8, width), F32),
                pltpu.VMEM((Q + 8, 2 * NS), F32),
                pltpu.VMEM((NS, width), F32),
                pltpu.VMEM((128, Q), F32),
                pltpu.VMEM((3 * Q + 16, width), BF16),
                pltpu.VMEM((Q, width), BF16),
                pltpu.VMEM((Q, width), BF16),
                pltpu.VMEM((width, 128), BF16),
                pltpu.VMEM((2 * Q, 2 * Q), BF16),
                pltpu.VMEM((48, width), F32),
                pltpu.VMEM((48, 2 * NS), F32),
            ],
        ),
        out_shape=[
            jax.ShapeDtypeStruct((length, width + 2 * NS + 128), BF16),
            jax.ShapeDtypeStruct((8, width), F32),
            jax.ShapeDtypeStruct((8, 2 * NS), F32),
            jax.ShapeDtypeStruct((8, 128), F32),
        ],
        compiler_params=pltpu.CompilerParams(vmem_limit_bytes=VMEM_LIMIT),
        cost_estimate=pl.CostEstimate(
            flops=70 * length * 128 * width, bytes_accessed=20 * length * width, transcendentals=0
        ),
        name="mix_backward",
    )(turn, proj, proj, conv, convs, proj, steps, aux, seg_rows, grad, states, inner_p, shared_p, heads_p)


def aux_of(seg_line):
    length = seg_line.shape[0]
    ends = seg_line.reshape(-1, Q)[:, Q - 1]
    prior = jnp.concatenate([jnp.full((1,), -1, seg_line.dtype), ends[:-1]])
    place = jnp.arange(length)
    columns = []
    for shift in range(1, 4):
        columns.append((jnp.roll(seg_line, shift) == seg_line) & (place >= shift))
    for shift in range(1, 4):
        columns.append((jnp.roll(seg_line, -shift) == seg_line) & (place < length - shift))
    columns.append(seg_line == jnp.repeat(prior, Q))
    columns.append(seg_line == jnp.repeat(ends, Q))
    columns = [column.astype(F32) for column in columns] + [seg_line.astype(F32)]
    columns += [jnp.zeros((length,), F32)] * (16 - len(columns))
    rows = seg_line.astype(F32).reshape(-1, 1, Q)
    return jnp.stack(columns, axis=1), rows


def program(sizes, args):
    (
        hidden, norm_gain, weight_gate, weight_inner, weight_shared, weight_step,
        filter_inner, bias_inner, filter_shared, bias_shared, step_bias, log_rate, skip_gain,
        gate_gain, weight_out, segments, cotangent,
    ) = args
    n_fsdp, n_tp = sizes
    width = weight_gate.shape[1]
    heads = weight_step.shape[1]
    own_rows = hidden.shape[0]
    length = segments.shape[1]
    tp_place = lax.axis_index("tp")
    paired = n_tp == 2

    def tp_rows(own):
        if paired:
            return jnp.concatenate([own, lax.ppermute(own, "tp", [(0, 1), (1, 0)])], axis=0)
        return lax.all_gather(own, "tp", axis=0, tiled=True)

    def tp_scatter(make):
        if paired:
            away = make(slice(own_rows, 2 * own_rows)).astype(BF16)
            got = lax.ppermute(away, "tp", [(0, 1), (1, 0)])
            return make(slice(0, own_rows)), got.astype(F32)
        return lax.psum_scatter(make(slice(None)), "tp", scatter_dimension=0, tiled=True), 0.0

    def gather(shard):
        return lax.all_gather(shard, "fsdp", axis=0, tiled=True)

    fsdp_place = lax.axis_index("fsdp")
    outer = n_fsdp // 2
    digits = [(4, n_fsdp // 4), (outer // 4, 2), (2, 1)] if outer % 4 == 0 else [(outer, 2), (2, 1)]

    def line_gather(shard):
        blocks = shard
        for axis, (size, stride) in enumerate(digits):
            place = lax.rem(fsdp_place // stride, size)
            parts = [blocks]
            for step in range(1, size):
                moves = []
                for i in range(n_fsdp):
                    at = (i // stride) % size
                    moves.append((i, i + ((at + step) % size - at) * stride))
                parts.append(lax.ppermute(blocks, "fsdp", moves))
            if size == 2:
                own, away = parts
                blocks = jnp.where(
                    place == 0,
                    jnp.stack([own, away], axis=axis),
                    jnp.stack([away, own], axis=axis),
                )
            elif size > 2:
                ring = jnp.stack(parts[::-1] + parts[::-1], axis=axis)
                blocks = lax.dynamic_slice_in_dim(ring, size - 1 - place, size, axis)
            else:
                blocks = jnp.expand_dims(blocks, axis)
        return blocks.reshape(n_fsdp * shard.shape[0], shard.shape[1])

    even = lax.rem(fsdp_place, 2) == 0

    def core_halves(total):
        blocks = total.reshape(outer, 2, total.shape[0] // n_fsdp, total.shape[1])
        away = jnp.where(even, blocks[:, 1], blocks[:, 0])
        return away, jnp.where(even, blocks[:, 0], blocks[:, 1])

    def core_sum(total):
        away, mine = core_halves(total)
        got = lax.ppermute(away, "fsdp", other_core)
        return (mine.astype(F32) + got.astype(F32)).astype(BF16).reshape(-1, total.shape[1])

    other_core = [(i, i ^ 1) for i in range(n_fsdp)]

    def chip_swap(half):
        groups = [[i for i in range(n_fsdp) if i % 2 == core] for core in range(2)]
        return lax.all_to_all(half, "fsdp", 0, 0, axis_index_groups=groups, tiled=True)

    def chip_sum(swapped):
        return jnp.sum(swapped.reshape(outer, -1, swapped.shape[1]).astype(F32), axis=0)

    pad = jnp.zeros((weight_step.shape[0], 128 - heads - 1), BF16)
    shard_a = jnp.concatenate(
        [weight_inner, weight_shared, weight_step, norm_gain[:, None], pad], axis=1
    )
    hidden_all = tp_rows(hidden)
    weights_a = line_gather(shard_a)
    weights_b = gather(jnp.concatenate([weight_gate, weight_out], axis=1))
    gate_all, out_all = weights_b[:, :width], weights_b[:, width:]
    cot_all = tp_rows(cotangent)
    gain_row = weights_a[:, width + 2 * NS + heads].astype(F32)[None, :]

    hidden_f = hidden_all.astype(F32)
    inv_rms = lax.rsqrt(jnp.mean(hidden_f * hidden_f, axis=1, keepdims=True) + EPSILON)
    normed = (hidden_f * inv_rms * gain_row).astype(BF16)
    normed = lax.optimization_barrier(normed)
    proj = mm(normed, weights_a).astype(BF16)

    turn = (tp_place * (own_rows // Q) if paired else jnp.zeros((), jnp.int32)).reshape(1)
    turn = turn.astype(jnp.int32)
    aux, seg_rows = aux_of(segments[0])
    heads_p = jnp.pad(
        jnp.stack(
            [step_bias.astype(F32), -jnp.exp(log_rate.astype(F32)), skip_gain.astype(F32)]
        ),
        ((0, 5), (0, 128 - heads)),
    )
    y, conv, convs, states, steps = forward_mix(
        turn, proj, aux, seg_rows, filter_inner, bias_inner[None], filter_shared,
        bias_shared[None], heads_p,
    )

    y, gate_all, out_all, cot_all = lax.optimization_barrier((y, gate_all, out_all, cot_all))
    gate_z = mm(normed, gate_all).astype(BF16).astype(F32)
    grad_gated = mm(cot_all, out_all).astype(BF16).astype(F32)
    y = y.astype(F32)
    gain_gate = gate_gain.astype(F32)[None, :]
    sig = jax.nn.sigmoid(gate_z)
    act = gate_z * sig
    mixed = y * act
    scaled = grad_gated * gain_gate
    sums = jnp.stack([jnp.sum(mixed * mixed, axis=1), jnp.sum(mixed * scaled, axis=1)], axis=1)
    if paired:
        half = jnp.concatenate([sums[own_rows:], sums[:own_rows]], axis=0)
        sums = sums + lax.ppermute(half, "tp", [(0, 1), (1, 0)])
    else:
        sums = lax.psum(sums, "tp")
    inv_gate = lax.rsqrt(sums[:, 0:1] / INNER + EPSILON)
    gated = (mixed * inv_gate * gain_gate).astype(BF16)
    grad_mixed = inv_gate * scaled - mixed * (inv_gate * inv_gate * inv_gate) * (
        sums[:, 1:2] / INNER
    )
    grad_y = grad_mixed * act
    low_z = (grad_mixed * y * (sig + act * (1.0 - sig))).astype(BF16)
    grad_gain_gate = jnp.sum(grad_gated * mixed * inv_gate, axis=0)
    grad_y, low_z, gated = lax.optimization_barrier((grad_y.astype(BF16), low_z, gated))
    half_b = jnp.concatenate(
        [core_sum(weight_grad(normed, low_z).astype(BF16)),
         core_sum(weight_grad(cot_all, gated).astype(BF16))], axis=1)
    out_own, out_got = tp_scatter(lambda at: mm_t(gated[at], out_all))
    half_b, grad_y, out_own = lax.optimization_barrier((half_b, grad_y, out_own))
    swap_b = chip_swap(half_b)
    low, inner_sum, shared_sum, heads_sum = backward_mix(
        turn, proj, conv, convs, steps, aux, seg_rows, grad_y, states, filter_inner,
        filter_shared, heads_p
    )
    small = jnp.concatenate(
        [jnp.concatenate([inner_sum[:6], grad_gain_gate[None], inner_sum[7:]], axis=0),
         shared_sum, heads_sum], axis=1)
    reach = 1
    while reach < n_fsdp:
        small = small + lax.ppermute(small, "fsdp", [(i, i ^ reach) for i in range(n_fsdp)])
        reach *= 2
    low, late_hidden = lax.optimization_barrier((low, hidden))
    layer_out = (late_hidden.astype(F32) + out_own + out_got).astype(BF16)
    low, layer_out = lax.optimization_barrier((low, layer_out))
    grads_a = weight_grad(normed, low).astype(BF16)
    def input_rows(at):
        return mm_t(low_z[at], gate_all) + mm_t(low[at], weights_a)

    away_a, mine_a = core_halves(grads_a)
    away_a, mine_a, swap_b = lax.optimization_barrier((away_a, mine_a, swap_b))
    away_a = lax.ppermute(away_a, "fsdp", other_core)
    if paired:
        away_part = input_rows(slice(own_rows, 2 * own_rows)).astype(BF16)
    else:
        away_part = input_rows(slice(None))
    if paired:
        part_got = lax.ppermute(away_part, "tp", [(0, 1), (1, 0)]).astype(F32)
        part_own = input_rows(slice(0, own_rows))
    else:
        part_own = lax.psum_scatter(away_part, "tp", scatter_dimension=0, tiled=True)
        part_got = 0.0
    half_a = (mine_a.astype(F32) + away_a.astype(F32)).astype(BF16).reshape(-1, low.shape[1])
    swap_a = chip_swap(half_a)
    grad_normed = part_own + part_got
    x_hat = hidden.astype(F32) * inv_rms[:own_rows] if paired else None
    inv_own = inv_rms[:own_rows]
    if not paired:
        inv_own = lax.dynamic_slice_in_dim(inv_rms, tp_place * own_rows, own_rows, 0)
        x_hat = hidden.astype(F32) * inv_own
    scaled_in = grad_normed * gain_row
    grad_hidden = cotangent.astype(F32) + inv_own * (
        scaled_in - x_hat * jnp.mean(scaled_in * x_hat, axis=1, keepdims=True)
    )

    def tp_sum(value):
        if paired:
            return value + lax.ppermute(value, "tp", [(0, 1), (1, 0)])
        return lax.psum(value, "tp")

    shared_part = tp_sum(small[:, width : width + 2 * NS])
    early = (
        grad_hidden,
        layer_out,
        small[0:4, :width],
        small[4, :width],
        shared_part[0:4],
        shared_part[4],
        small[0, width + 2 * NS : width + 2 * NS + heads],
        small[1, width + 2 * NS : width + 2 * NS + heads],
        jnp.sum(small[5, :width].reshape(heads, HEAD), axis=1),
        small[6, :width],
    )
    swap_a, early = lax.optimization_barrier((swap_a, early))
    owned_a, owned_b = chip_sum(swap_a), chip_sum(swap_b)
    grad_gate, grad_out = owned_b[:, :width], owned_b[:, width:]
    grad_inner = owned_a[:, :width]
    grad_shared = owned_a[:, width : width + 2 * NS]
    grad_step = owned_a[:, width + 2 * NS : width + 2 * NS + heads]
    gain_own = (
        jnp.sum(weight_gate.astype(F32) * grad_gate, axis=1)
        + jnp.sum(weight_inner.astype(F32) * grad_inner, axis=1)
        + jnp.sum(weight_shared.astype(F32) * grad_shared, axis=1)
        + jnp.sum(weight_step.astype(F32) * grad_step, axis=1)
    )
    packed = jnp.concatenate(
        [grad_shared, jnp.pad(gain_own[None], ((0, 7), (0, 2 * NS - gain_own.shape[0])))], axis=0
    )
    packed = tp_sum(packed)
    owned = grad_shared.shape[0]
    grad_norm_gain = packed[owned, : gain_own.shape[0]] / norm_gain.astype(F32)
    return (
        early[1],
        early[0],
        grad_norm_gain,
        grad_gate,
        grad_inner,
        packed[:owned],
        grad_step,
        *early[2:],
        grad_out,
    )


def solution(mesh):
    sizes = (mesh.shape["fsdp"], mesh.shape["tp"])

    def per_device(*args):
        return program(sizes, args)

    return jax.shard_map(
        per_device,
        mesh=mesh,
        in_specs=(
            P(("fsdp", "tp"), None),
            P("fsdp"),
            P("fsdp", "tp"),
            P("fsdp", "tp"),
            P("fsdp", None),
            P("fsdp", "tp"),
            P(None, "tp"),
            P("tp"),
            P(),
            P(),
            P("tp"),
            P("tp"),
            P("tp"),
            P("tp"),
            P("fsdp", "tp"),
            P("fsdp", None),
            P(("fsdp", "tp"), None),
        ),
        out_specs=(
            P(("fsdp", "tp"), None),
            P(("fsdp", "tp"), None),
            P("fsdp"),
            P("fsdp", "tp"),
            P("fsdp", "tp"),
            P("fsdp", None),
            P("fsdp", "tp"),
            P(None, "tp"),
            P("tp"),
            P(),
            P(),
            P("tp"),
            P("tp"),
            P("tp"),
            P("tp"),
            P("fsdp", "tp"),
        ),
        check_vma=False,
    )
```

```python
import jax
import jax.numpy as jnp
from jax import lax
from jax.experimental import pallas as pl
from jax.experimental.pallas import tpu as pltpu
from jax.sharding import PartitionSpec as P

INNER = 2048
NS = 128
HEAD = 64
Q = 128
LOG2E = 1.4426950408889634
FAR = -1e30
EPSILON = 1e-05

F32 = jnp.float32
BF16 = jnp.bfloat16
HIGH = lax.Precision.HIGHEST


def mm(a, b):
    return jnp.dot(a, b, preferred_element_type=F32)


def mm_t(a, b):
    return lax.dot_general(a, b, (((1,), (1,)), ((), ())), preferred_element_type=F32)


def weight_grad(a, b):
    return lax.dot_general(a, b, (((0,), (0,)), ((), ())), preferred_element_type=F32)


def iota(shape, dim):
    return lax.broadcasted_iota(jnp.int32, shape, dim)


def softplus(v):
    return jnp.maximum(v, 0.0) + jnp.log1p(jnp.exp(-jnp.abs(v)))


def wide(column):
    return jnp.broadcast_to(column, (Q, 128))


def pair_of(first, array, pair):
    return jnp.where(
        first, wide(array[:, 2 * pair : 2 * pair + 1]), wide(array[:, 2 * pair + 1 : 2 * pair + 2])
    )


def skip_of(first, heads_ref, pair):
    line = heads_ref[2:3, :]
    return jnp.where(
        first,
        jnp.broadcast_to(line[:, 2 * pair : 2 * pair + 1], (1, 128)),
        jnp.broadcast_to(line[:, 2 * pair + 1 : 2 * pair + 2], (1, 128)),
    )


def folded(block):
    return jnp.sum(block.reshape(Q // 8, 8, 128), axis=0)


def stacked(first, block):
    nil = jnp.zeros_like(block)
    return jnp.concatenate([jnp.where(first, block, nil), jnp.where(first, nil, block)], axis=0)


def forward_kernel(
    turn_ref, u_ref, s_ref, step_ref, aux_ref, seg_ref,
    inner_ref, inner_bias_ref, shared_ref, shared_bias_ref, heads_ref,
    y_ref, conv_ref, convs_ref, states_ref, steps_ref,
    ubuf, sbuf, state, xtail,
):
    width = u_ref.shape[1]
    chunk = pl.program_id(0)

    @pl.when(chunk == 0)
    def _():
        ubuf[0:8, :] = jnp.zeros((8, width), F32)
        sbuf[0:8, :] = jnp.zeros((8, 2 * NS), F32)
        state[...] = jnp.zeros_like(state)

    @pl.when(chunk > 0)
    def _():
        ubuf[0:8, :] = ubuf[Q : Q + 8, :]
        sbuf[0:8, :] = sbuf[Q : Q + 8, :]

    ubuf[8 : Q + 8, :] = u_ref[...].astype(F32)
    sbuf[8 : Q + 8, :] = s_ref[...].astype(F32)
    aux = aux_ref[...]
    same = [wide(aux[:, k : k + 1]) for k in range(3)]
    keep = wide(aux[:, 6:7])
    tail_in = wide(aux[:, 7:8])

    def conv_of(buf, taps_ref, bias_ref, cols):
        weights = taps_ref[:, cols].astype(F32)
        total = bias_ref[:, cols].astype(F32) + weights[3:4] * buf[8 : Q + 8, cols]
        for shift in range(1, 4):
            total = total + weights[3 - shift : 4 - shift] * (
                buf[8 - shift : Q + 8 - shift, cols] * same[shift - 1]
            )
        return total

    def silu(v):
        return v * (0.5 + 0.5 * jnp.tanh(0.5 * v))

    conv_b = conv_of(sbuf, shared_ref, shared_bias_ref, slice(0, NS))
    conv_c = conv_of(sbuf, shared_ref, shared_bias_ref, slice(NS, 2 * NS))
    convs_ref[:, 0:NS] = conv_b
    convs_ref[:, NS : 2 * NS] = conv_c
    b_f = silu(conv_b)
    b_low = b_f.astype(BF16)
    b_turn = b_f.T.astype(BF16)
    c_low = silu(conv_c).astype(BF16)
    inner_cb = mm_t(c_low, b_low)
    visible = (wide(aux[:, 8:9]) == seg_ref[0]) & (iota((Q, Q), 0) >= iota((Q, Q), 1))
    bias = jnp.where(visible, 0.0, FAR)
    dt = softplus(step_ref[...].astype(F32) + heads_ref[0:1, :])
    lower = (iota((Q, Q), 0) >= iota((Q, Q), 1)).astype(BF16)
    rest = dt * (heads_ref[1:2, :] * LOG2E)
    cum = jnp.zeros((Q, 128), F32)
    for _ in range(3):
        piece = rest.astype(BF16)
        cum = cum + mm(lower, piece)
        rest = rest - piece.astype(F32)
    cum_t = cum.T
    steps_ref[0, 0] = dt
    steps_ref[0, 1] = cum
    steps_ref[0, 2] = cum_t
    first = iota((Q, 128), 1) < HEAD
    state_low = state[...].astype(BF16)
    states_ref[0] = state_low
    carried = mm(c_low, state_low)
    for pair in range(width // 128):
        cols = slice(128 * pair, 128 * pair + 128)
        conv = conv_of(ubuf, inner_ref, inner_bias_ref, cols)
        conv_ref[:, cols] = conv
        x = silu(conv)
        cum_1 = wide(cum[:, 2 * pair : 2 * pair + 1])
        cum_2 = wide(cum[:, 2 * pair + 1 : 2 * pair + 2])
        m_1 = inner_cb * jnp.exp2(cum_1 - cum_t[2 * pair : 2 * pair + 1, :] + bias)
        m_2 = inner_cb * jnp.exp2(cum_2 - cum_t[2 * pair + 1 : 2 * pair + 2, :] + bias)
        xd = x * pair_of(first, dt, pair)
        mixers = jnp.concatenate([m_1.astype(BF16), m_2.astype(BF16)], axis=1)
        y = mm(mixers, stacked(first, xd.astype(BF16)))
        cum_p = jnp.where(first, cum_1, cum_2)
        last = cum_p[Q - 1 : Q, :]
        y = y + carried[:, cols] * (jnp.exp2(cum_p) * keep)
        y_ref[:, cols] = (y + skip_of(first[0:1], heads_ref, pair) * x).astype(BF16)
        tail = jnp.exp2(last - cum_p) * tail_in
        xtail[:, cols] = (xd * tail).astype(BF16)
        state[:, cols] = state[:, cols] * (jnp.exp2(last) * keep[Q - 1 : Q, :])
    state[...] += mm(b_turn, xtail[...])


def backward_kernel(
    turn_ref, u_ref, s_ref, conv_ref, convs_ref, step_ref, steps_ref, aux_ref, seg_ref, grad_ref, states_ref,
    inner_ref, shared_ref, heads_ref,
    low_ref, inner_sum, shared_sum, heads_sum,
    dbuf, dsbuf, dstate, dcum_t, red, wgrad, xtail, to_head, lower_low, inner_acc, shared_acc,
):
    width = u_ref.shape[1]
    chunk = pl.program_id(0)

    @pl.when(chunk == 0)
    def _():
        dbuf[Q : Q + 8, :] = jnp.zeros((8, width), F32)
        dsbuf[Q : Q + 8, :] = jnp.zeros((8, 2 * NS), F32)
        dstate[...] = jnp.zeros_like(dstate)
        dcum_t[...] = jnp.zeros_like(dcum_t)
        inner_acc[...] = jnp.zeros_like(inner_acc)
        shared_acc[...] = jnp.zeros_like(shared_acc)
        heads_sum[...] = jnp.zeros_like(heads_sum)
        to_head[...] = (
            iota((width, 128), 0) // HEAD == iota((width, 128), 1)
        ).astype(BF16)
        row_2, column_2 = iota((2 * Q, 2 * Q), 0), iota((2 * Q, 2 * Q), 1)
        lower_low[...] = ((row_2 // Q == column_2 // Q) & (row_2 >= column_2)).astype(BF16)

    @pl.when(chunk > 0)
    def _():
        dbuf[Q : Q + 8, :] = dbuf[0:8, :]
        dsbuf[Q : Q + 8, :] = dsbuf[0:8, :]

    aux = aux_ref[...]
    same = [wide(aux[:, 3 + k : 4 + k]) for k in range(3)]
    keep = wide(aux[:, 6:7])
    tail_in = wide(aux[:, 7:8])

    def silu_and_slope(v):
        sig = 0.5 + 0.5 * jnp.tanh(0.5 * v)
        act = v * sig
        return act, sig + act * (1.0 - sig)

    b_f, b_slope = silu_and_slope(convs_ref[:, 0:NS])
    c_f, c_slope = silu_and_slope(convs_ref[:, NS : 2 * NS])
    b_low = b_f.astype(BF16)
    c_low = c_f.astype(BF16)
    c_turn = c_f.T.astype(BF16)
    inner_bc = mm_t(b_low, c_low)
    row, column = iota((Q, Q), 0), iota((Q, Q), 1)
    visible = (wide(aux[:, 8:9]) == seg_ref[0]) & (row <= column)
    bias = jnp.where(visible, 0.0, FAR)
    strict = jnp.concatenate([row < column, row < column], axis=1)
    inner_2 = jnp.concatenate([inner_bc, inner_bc], axis=1)
    bias_2 = jnp.concatenate([bias, bias], axis=1)
    raw = step_ref[...].astype(F32) + heads_ref[0:1, :]
    dt, cum, cum_t = steps_ref[0, 0], steps_ref[0, 1], steps_ref[0, 2]
    first = iota((Q, 128), 1) < HEAD
    dinner = jnp.zeros((Q, 2 * Q), F32)
    later_low = dstate[...].astype(BF16)
    end_all = mm(b_low, later_low)
    start_all = mm(c_low, states_ref[0])
    for pair in range(width // 128):
        cols = slice(128 * pair, 128 * pair + 128)
        cum_1 = wide(cum[:, 2 * pair : 2 * pair + 1])
        cum_2 = wide(cum[:, 2 * pair + 1 : 2 * pair + 2])
        ahead = jnp.concatenate(
            [cum_t[2 * pair : 2 * pair + 1, :], cum_t[2 * pair + 1 : 2 * pair + 2, :]], axis=1
        )
        decay = jnp.exp2(ahead - jnp.concatenate([cum_1, cum_2], axis=1) + bias_2)
        m = inner_2 * decay
        x, slope = silu_and_slope(conv_ref[:, cols])
        dt_p = pair_of(first, dt, pair)
        xd = x * dt_p
        grad = grad_ref[:, cols].astype(F32)
        grad_two = stacked(first, grad_ref[:, cols].astype(BF16))
        dm = mm_t(xd.astype(BF16), grad_two)
        dinner = dinner + dm * decay
        spans = mm((dm * m).astype(BF16), lower_low[...])
        gaps = jnp.sum(jnp.where(strict, spans, 0.0), axis=0, keepdims=True)
        dcum_t[2 * pair : 2 * pair + 1, :] = gaps[:, 0:Q]
        dcum_t[2 * pair + 1 : 2 * pair + 2, :] = gaps[:, Q : 2 * Q]
        dxd = mm(m.astype(BF16), grad_two)
        cum_p = jnp.where(first, cum_1, cum_2)
        last = cum_p[Q - 1 : Q, :]
        tail = jnp.exp2(last - cum_p) * tail_in
        later = dstate[:, cols]
        old_low = states_ref[0, :, cols]
        xt = xd * tail
        from_end = end_all[:, cols]
        dxd = dxd + tail * from_end
        weight = jnp.exp2(cum_p) * keep
        wg = grad * weight
        from_start = start_all[:, cols]
        carry = jnp.exp2(last) * keep[Q - 1 : Q, :]
        carried = jnp.sum(later * old_low.astype(F32), axis=0, keepdims=True) * carry
        red[0:Q, cols] = (dxd * x).astype(BF16)
        red[Q : 2 * Q, cols] = (xt * from_end).astype(BF16)
        red[2 * Q : 3 * Q, cols] = (wg * from_start).astype(BF16)
        red[3 * Q : 3 * Q + 16, cols] = jnp.broadcast_to(carried, (16, 128)).astype(BF16)
        wg_low = wg.astype(BF16)
        wgrad[:, cols] = wg_low
        xtail[:, cols] = xt.astype(BF16)
        dx = dxd * dt_p + skip_of(first[0:1], heads_ref, pair) * grad
        dbuf[0:Q, cols] = dx * slope
        inner_acc[40:48, cols] += folded(grad * x)

    sums = mm(red[...], to_head[...])
    spread = jnp.concatenate([(row > column).astype(BF16), (row <= column).astype(BF16)], axis=1)
    dla = dcum_t[...].T + mm(spread, sums[Q : 3 * Q, :].astype(BF16)) + sums[3 * Q : 3 * Q + 1, :]
    rate = heads_ref[1:2, :]
    ddt = sums[0:Q, :] + rate * dla
    dstep = ddt * (0.5 + 0.5 * jnp.tanh(0.5 * raw))
    low_ref[:, width + 2 * NS : width + 2 * NS + 128] = dstep.astype(BF16)
    heads_sum[0:1, :] += jnp.sum(dstep, axis=0, keepdims=True)
    heads_sum[1:2, :] += jnp.sum(dla * dt * rate, axis=0, keepdims=True)

    dinner = dinner[:, 0:Q] + dinner[:, Q : 2 * Q]
    dinner_low = dinner.astype(BF16)
    db = mm(dinner_low, c_low) + mm_t(xtail[...], later_low)
    dc = mm(dinner.T.astype(BF16), b_low) + mm_t(wgrad[...], states_ref[0])
    dsbuf[0:Q, 0:NS] = db * b_slope
    dsbuf[0:Q, NS : 2 * NS] = dc * c_slope

    def conv_back(u, buf, taps_ref, acc, cols):
        weights = taps_ref[:, cols].astype(F32)
        d = buf[0:Q, cols]
        du = weights[3:4] * d
        acc[24:32, cols] += folded(d * u)
        acc[32:40, cols] += folded(d)
        for shift in range(1, 4):
            d = buf[shift : Q + shift, cols] * same[shift - 1]
            du = du + weights[3 - shift : 4 - shift] * d
            acc[24 - 8 * shift : 32 - 8 * shift, cols] += folded(d * u)
        return du

    for part in range(2):
        cols = slice(NS * part, NS * part + NS)
        low_ref[:, width + NS * part : width + NS * part + NS] = conv_back(
            s_ref[:, cols].astype(F32), dsbuf, shared_ref, shared_acc, cols
        ).astype(BF16)
    new = mm(c_turn, wgrad[...])
    for pair in range(width // 128):
        cols = slice(128 * pair, 128 * pair + 128)
        low_ref[:, cols] = conv_back(
            u_ref[:, cols].astype(F32), dbuf, inner_ref, inner_acc, cols
        ).astype(BF16)
        cum_p = jnp.where(
            first[0:1, :],
            jnp.broadcast_to(cum[Q - 1 : Q, 2 * pair : 2 * pair + 1], (1, 128)),
            jnp.broadcast_to(cum[Q - 1 : Q, 2 * pair + 1 : 2 * pair + 2], (1, 128)),
        )
        carry = jnp.exp2(cum_p) * keep[Q - 1 : Q, :]
        dstate[:, cols] = dstate[:, cols] * carry + new[:, cols]

    @pl.when(chunk == pl.num_programs(0) - 1)
    def _():
        for out, acc, count in ((inner_sum, inner_acc, 6), (shared_sum, shared_acc, 5)):
            out[...] = jnp.zeros_like(out)
            for k in range(count):
                out[k : k + 1, :] = jnp.sum(acc[8 * k : 8 * k + 8, :], axis=0, keepdims=True)


VMEM_LIMIT = 60 * 1024 * 1024


def forward_mix(turn, proj, aux, seg_rows, inner_p, inner_b, shared_p, shared_b, heads_p):
    length = proj.shape[0]
    width = inner_p.shape[1]
    chunks = length // Q

    def rows(n, at=0):
        return pl.BlockSpec((Q, n), lambda c, turn: (lax.rem(c + turn[0], chunks), at))

    def plain(n):
        return pl.BlockSpec((Q, n), lambda c, turn: (c, 0))

    def whole(n, rows=8):
        return pl.BlockSpec((rows, n), lambda c, turn: (0, 0))

    line = pl.BlockSpec((1, 1, Q), lambda c, turn: (c, 0, 0))
    kept = pl.BlockSpec((1, NS, width), lambda c, turn: (c, 0, 0))
    return pl.pallas_call(
        forward_kernel,
        grid_spec=pltpu.PrefetchScalarGridSpec(
            num_scalar_prefetch=1,
            grid=(chunks,),
            in_specs=[
                rows(width), rows(2 * NS, width // (2 * NS)), rows(128, (width + 2 * NS) // 128),
                plain(16), line, whole(width, 4), whole(width, 1), whole(2 * NS, 4),
                whole(2 * NS, 1), whole(128),
            ],
            out_specs=[
                rows(width), plain(width), plain(2 * NS), kept,
                pl.BlockSpec((1, 3, Q, 128), lambda c, turn: (c, 0, 0, 0)),
            ],
            scratch_shapes=[
                pltpu.VMEM((Q + 8, width), F32),
                pltpu.VMEM((Q + 8, 2 * NS), F32),
                pltpu.VMEM((NS, width), F32),
                pltpu.VMEM((Q, width), BF16),
            ],
        ),
        out_shape=[
            jax.ShapeDtypeStruct((length, width), BF16),
            jax.ShapeDtypeStruct((length, width), F32),
            jax.ShapeDtypeStruct((length, 2 * NS), F32),
            jax.ShapeDtypeStruct((chunks, NS, width), BF16),
            jax.ShapeDtypeStruct((chunks, 3, Q, 128), F32),
        ],
        compiler_params=pltpu.CompilerParams(vmem_limit_bytes=VMEM_LIMIT),
        cost_estimate=pl.CostEstimate(
            flops=32 * length * 128 * width, bytes_accessed=12 * length * width, transcendentals=0
        ),
        name="mix_forward",
    )(turn, proj, proj, proj, aux, seg_rows, inner_p, inner_b, shared_p, shared_b, heads_p)


def backward_mix(turn, proj, conv, convs, steps, aux, seg_rows, grad, states, inner_p, shared_p, heads_p):
    length = proj.shape[0]
    width = inner_p.shape[1]
    chunks = length // Q

    def rows(n, at=0):
        return pl.BlockSpec(
            (Q, n), lambda c, turn: (lax.rem(chunks - 1 - c + turn[0], chunks), at)
        )

    def plain(n):
        return pl.BlockSpec((Q, n), lambda c, turn: (chunks - 1 - c, 0))

    def whole(n, rows=8):
        return pl.BlockSpec((rows, n), lambda c, turn: (0, 0))

    line = pl.BlockSpec((1, 1, Q), lambda c, turn: (chunks - 1 - c, 0, 0))
    kept = pl.BlockSpec((1, NS, width), lambda c, turn: (chunks - 1 - c, 0, 0))
    return pl.pallas_call(
        backward_kernel,
        grid_spec=pltpu.PrefetchScalarGridSpec(
            num_scalar_prefetch=1,
            grid=(chunks,),
            in_specs=[
                rows(width), rows(2 * NS, width // (2 * NS)), plain(width), plain(2 * NS),
                rows(128, (width + 2 * NS) // 128),
                pl.BlockSpec((1, 3, Q, 128), lambda c, turn: (chunks - 1 - c, 0, 0, 0)),
                plain(16), line, rows(width), kept,
                whole(width, 4), whole(2 * NS, 4), whole(128),
            ],
            out_specs=[rows(width + 2 * NS + 128), whole(width), whole(2 * NS), whole(128)],
            scratch_shapes=[
                pltpu.VMEM((Q + 8, width), F32),
                pltpu.VMEM((Q + 8, 2 * NS), F32),
                pltpu.VMEM((NS, width), F32),
                pltpu.VMEM((128, Q), F32),
                pltpu.VMEM((3 * Q + 16, width), BF16),
                pltpu.VMEM((Q, width), BF16),
                pltpu.VMEM((Q, width), BF16),
                pltpu.VMEM((width, 128), BF16),
                pltpu.VMEM((2 * Q, 2 * Q), BF16),
                pltpu.VMEM((48, width), F32),
                pltpu.VMEM((48, 2 * NS), F32),
            ],
        ),
        out_shape=[
            jax.ShapeDtypeStruct((length, width + 2 * NS + 128), BF16),
            jax.ShapeDtypeStruct((8, width), F32),
            jax.ShapeDtypeStruct((8, 2 * NS), F32),
            jax.ShapeDtypeStruct((8, 128), F32),
        ],
        compiler_params=pltpu.CompilerParams(vmem_limit_bytes=VMEM_LIMIT),
        cost_estimate=pl.CostEstimate(
            flops=70 * length * 128 * width, bytes_accessed=20 * length * width, transcendentals=0
        ),
        name="mix_backward",
    )(turn, proj, proj, conv, convs, proj, steps, aux, seg_rows, grad, states, inner_p, shared_p, heads_p)


def aux_of(seg_line):
    length = seg_line.shape[0]
    ends = seg_line.reshape(-1, Q)[:, Q - 1]
    prior = jnp.concatenate([jnp.full((1,), -1, seg_line.dtype), ends[:-1]])
    place = jnp.arange(length)
    columns = []
    for shift in range(1, 4):
        columns.append((jnp.roll(seg_line, shift) == seg_line) & (place >= shift))
    for shift in range(1, 4):
        columns.append((jnp.roll(seg_line, -shift) == seg_line) & (place < length - shift))
    columns.append(seg_line == jnp.repeat(prior, Q))
    columns.append(seg_line == jnp.repeat(ends, Q))
    columns = [column.astype(F32) for column in columns] + [seg_line.astype(F32)]
    columns += [jnp.zeros((length,), F32)] * (16 - len(columns))
    rows = seg_line.astype(F32).reshape(-1, 1, Q)
    return jnp.stack(columns, axis=1), rows


def program(sizes, args):
    (
        hidden, norm_gain, weight_gate, weight_inner, weight_shared, weight_step,
        filter_inner, bias_inner, filter_shared, bias_shared, step_bias, log_rate, skip_gain,
        gate_gain, weight_out, segments, cotangent,
    ) = args
    n_fsdp, n_tp = sizes
    width = weight_gate.shape[1]
    heads = weight_step.shape[1]
    own_rows = hidden.shape[0]
    length = segments.shape[1]
    tp_place = lax.axis_index("tp")
    paired = n_tp == 2

    def tp_rows(own):
        if paired:
            return jnp.concatenate([own, lax.ppermute(own, "tp", [(0, 1), (1, 0)])], axis=0)
        return lax.all_gather(own, "tp", axis=0, tiled=True)

    def tp_scatter(make):
        if paired:
            away = make(slice(own_rows, 2 * own_rows)).astype(BF16)
            got = lax.ppermute(away, "tp", [(0, 1), (1, 0)])
            return make(slice(0, own_rows)), got
        return lax.psum_scatter(make(slice(None)), "tp", scatter_dimension=0, tiled=True), 0.0

    fsdp_place = lax.axis_index("fsdp")
    outer = n_fsdp // 2
    digits = [(4, n_fsdp // 4), (outer // 4, 2), (2, 1)] if outer % 4 == 0 else [(outer, 2), (2, 1)]

    def stage(blocks, axis):
        size, stride = digits[axis]
        place = lax.rem(fsdp_place // stride, size)
        parts = [blocks]
        for step in range(1, size):
            moves = []
            for i in range(n_fsdp):
                at = (i // stride) % size
                moves.append((i, i + ((at + step) % size - at) * stride))
            parts.append(lax.ppermute(blocks, "fsdp", moves))
        if size == 2:
            own, away = parts
            return jnp.where(
                place == 0,
                jnp.stack([own, away], axis=axis),
                jnp.stack([away, own], axis=axis),
            )
        if size > 2:
            ring = jnp.stack(parts[::-1] + parts[::-1], axis=axis)
            return lax.dynamic_slice_in_dim(ring, size - 1 - place, size, axis)
        return jnp.expand_dims(blocks, axis)

    def line_gather(shard):
        blocks = shard
        for axis in range(len(digits)):
            blocks = stage(blocks, axis)
        return blocks.reshape(n_fsdp * shard.shape[0], shard.shape[1])

    even = lax.rem(fsdp_place, 2) == 0

    def core_halves(total):
        blocks = total.reshape(outer, 2, total.shape[0] // n_fsdp, total.shape[1])
        away = jnp.where(even, blocks[:, 1], blocks[:, 0])
        return away, jnp.where(even, blocks[:, 0], blocks[:, 1])

    def core_sum(total):
        away, mine = core_halves(total)
        got = lax.ppermute(away, "fsdp", other_core)
        return (mine.astype(F32) + got.astype(F32)).astype(BF16).reshape(-1, total.shape[1])

    other_core = [(i, i ^ 1) for i in range(n_fsdp)]

    def chip_swap(half):
        groups = [[i for i in range(n_fsdp) if i % 2 == core] for core in range(2)]
        return lax.all_to_all(half, "fsdp", 0, 0, axis_index_groups=groups, tiled=True)

    def chip_sum(swapped):
        return jnp.sum(swapped.reshape(outer, -1, swapped.shape[1]).astype(F32), axis=0)

    pad = jnp.zeros((weight_step.shape[0], 128 - heads - 1), BF16)
    shard_a = jnp.concatenate(
        [weight_inner, weight_shared, weight_step, norm_gain[:, None], pad], axis=1
    )
    hidden_all = tp_rows(hidden)
    weights_a = line_gather(shard_a)
    woven = len(digits) == 3 and digits[1][0] == 2
    if woven:
        shard_b = jnp.concatenate([weight_gate, weight_out], axis=1)
        size, span = digits[0]
        circles = [[i + span * step for step in range(size)] for i in range(span)]
        line = lax.all_to_all(
            jnp.broadcast_to(shard_b[None], (size,) + shard_b.shape), "fsdp", 0, 0,
            axis_index_groups=circles, tiled=True)
        line_core = lax.ppermute(line, "fsdp", other_core)
        next_line = lax.ppermute(line, "fsdp", [(i, i ^ 2) for i in range(n_fsdp)])
    else:
        gate_all, out_all = line_gather(weight_gate), line_gather(weight_out)
    if paired:
        late_cot, hidden_all = lax.optimization_barrier((cotangent, hidden_all))
        cot_got = lax.ppermute(late_cot, "tp", [(0, 1), (1, 0)])
    else:
        cot_got = lax.all_gather(cotangent, "tp", axis=0, tiled=True)
    gain_row = weights_a[:, width + 2 * NS + heads].astype(F32)[None, :]

    hidden_f = hidden_all.astype(F32)
    inv_rms = lax.rsqrt(jnp.mean(hidden_f * hidden_f, axis=1, keepdims=True) + EPSILON)
    normed = (hidden_f * inv_rms * gain_row).astype(BF16)
    normed = lax.optimization_barrier(normed)
    proj = mm(normed, weights_a).astype(BF16)

    turn = (tp_place * (own_rows // Q) if paired else jnp.zeros((), jnp.int32)).reshape(1)
    turn = turn.astype(jnp.int32)
    aux, seg_rows = aux_of(segments[0])
    heads_p = jnp.pad(
        jnp.stack(
            [step_bias.astype(F32), -jnp.exp(log_rate.astype(F32)), skip_gain.astype(F32)]
        ),
        ((0, 5), (0, 128 - heads)),
    )
    y, conv, convs, states, steps = forward_mix(
        turn, proj, aux, seg_rows, filter_inner, bias_inner[None], filter_shared,
        bias_shared[None], heads_p,
    )

    if woven:
        y, next_line, cot_got = lax.optimization_barrier((y, next_line, cot_got))
        next_core = lax.ppermute(next_line, "fsdp", other_core)
        lower_line = lax.rem(fsdp_place // 2, 2) == 0

        def swapped(flag, one, two):
            return jnp.where(flag, jnp.stack([one, two], axis=1), jnp.stack([two, one], axis=1))

        def weave(cols):
            near = swapped(even, line[:, :, cols], line_core[:, :, cols])
            far = swapped(even, next_line[:, :, cols], next_core[:, :, cols])
            return swapped(lower_line, near, far).reshape(-1, width)

        gate_all, out_all = weave(slice(0, width)), weave(slice(width, 2 * width))
    else:
        y, gate_all, out_all, cot_got = lax.optimization_barrier((y, gate_all, out_all, cot_got))
    cot_all = jnp.concatenate([cotangent, cot_got], axis=0) if paired else cot_got
    gate_z = mm(normed, gate_all).astype(BF16).astype(F32)
    grad_gated = mm(cot_all, out_all).astype(BF16).astype(F32)
    y = y.astype(F32)
    gain_gate = gate_gain.astype(F32)[None, :]
    sig = jax.nn.sigmoid(gate_z)
    act = gate_z * sig
    mixed = y * act
    scaled = grad_gated * gain_gate
    sums = jnp.stack([jnp.sum(mixed * mixed, axis=1), jnp.sum(mixed * scaled, axis=1)], axis=1)
    if paired:
        half = jnp.concatenate([sums[own_rows:], sums[:own_rows]], axis=0)
        sums = sums + lax.ppermute(half, "tp", [(0, 1), (1, 0)])
    else:
        sums = lax.psum(sums, "tp")
    inv_gate = lax.rsqrt(sums[:, 0:1] / INNER + EPSILON)
    gated = (mixed * inv_gate * gain_gate).astype(BF16)
    grad_mixed = inv_gate * scaled - mixed * (inv_gate * inv_gate * inv_gate) * (
        sums[:, 1:2] / INNER
    )
    grad_y = grad_mixed * act
    low_z = (grad_mixed * y * (sig + act * (1.0 - sig))).astype(BF16)
    grad_gain_gate = jnp.sum(grad_gated * mixed * inv_gate, axis=0)
    grad_y, low_z, gated = lax.optimization_barrier((grad_y.astype(BF16), low_z, gated))
    half_b = jnp.concatenate(
        [core_sum(weight_grad(normed, low_z).astype(BF16)),
         core_sum(weight_grad(cot_all, gated).astype(BF16))], axis=1)
    out_own, out_got = tp_scatter(lambda at: mm_t(gated[at], out_all))
    half_b, grad_y, out_own = lax.optimization_barrier((half_b, grad_y, out_own))
    swap_b = chip_swap(half_b)
    low, inner_sum, shared_sum, heads_sum = backward_mix(
        turn, proj, conv, convs, steps, aux, seg_rows, grad_y, states, filter_inner,
        filter_shared, heads_p
    )
    small = jnp.concatenate(
        [jnp.concatenate([inner_sum[:6], grad_gain_gate[None], inner_sum[7:]], axis=0),
         shared_sum, heads_sum], axis=1)
    reach = 1
    while reach < n_fsdp:
        small = small + lax.ppermute(small, "fsdp", [(i, i ^ reach) for i in range(n_fsdp)])
        reach *= 2
    low, out_got = lax.optimization_barrier((low, out_got))
    grads_a = weight_grad(normed, low).astype(BF16)
    def input_rows(at):
        return mm_t(low_z[at], gate_all) + mm_t(low[at], weights_a)

    away_a, mine_a = core_halves(grads_a)
    away_a, mine_a, swap_b = lax.optimization_barrier((away_a, mine_a, swap_b))
    away_a = lax.ppermute(away_a, "fsdp", other_core)
    if paired:
        away_part = input_rows(slice(own_rows, 2 * own_rows)).astype(BF16)
    else:
        away_part = input_rows(slice(None))
    if paired:
        part_got = lax.ppermute(away_part, "tp", [(0, 1), (1, 0)]).astype(F32)
        part_own = input_rows(slice(0, own_rows))
    else:
        part_own = lax.psum_scatter(away_part, "tp", scatter_dimension=0, tiled=True)
        part_got = 0.0
    half_a = (mine_a.astype(F32) + away_a.astype(F32)).astype(BF16).reshape(-1, low.shape[1])
    swap_a = chip_swap(half_a)
    layer_out = (hidden.astype(F32) + out_own + out_got).astype(BF16)
    grad_normed = part_own + part_got
    x_hat = hidden.astype(F32) * inv_rms[:own_rows] if paired else None
    inv_own = inv_rms[:own_rows]
    if not paired:
        inv_own = lax.dynamic_slice_in_dim(inv_rms, tp_place * own_rows, own_rows, 0)
        x_hat = hidden.astype(F32) * inv_own
    scaled_in = grad_normed * gain_row
    grad_hidden = cotangent.astype(F32) + inv_own * (
        scaled_in - x_hat * jnp.mean(scaled_in * x_hat, axis=1, keepdims=True)
    )

    def tp_sum(value):
        if paired:
            return value + lax.ppermute(value, "tp", [(0, 1), (1, 0)])
        return lax.psum(value, "tp")

    shared_part = tp_sum(small[:, width : width + 2 * NS])
    early = (
        grad_hidden,
        layer_out,
        small[0:4, :width],
        small[4, :width],
        shared_part[0:4],
        shared_part[4],
        small[0, width + 2 * NS : width + 2 * NS + heads],
        small[1, width + 2 * NS : width + 2 * NS + heads],
        jnp.sum(small[5, :width].reshape(heads, HEAD), axis=1),
        small[6, :width],
    )
    swap_a, early = lax.optimization_barrier((swap_a, early))
    owned_a, owned_b = chip_sum(swap_a), chip_sum(swap_b)
    grad_gate, grad_out = owned_b[:, :width], owned_b[:, width:]
    grad_inner = owned_a[:, :width]
    grad_shared = owned_a[:, width : width + 2 * NS]
    grad_step = owned_a[:, width + 2 * NS : width + 2 * NS + heads]
    gain_own = (
        jnp.sum(weight_gate.astype(F32) * grad_gate, axis=1)
        + jnp.sum(weight_inner.astype(F32) * grad_inner, axis=1)
        + jnp.sum(weight_shared.astype(F32) * grad_shared, axis=1)
        + jnp.sum(weight_step.astype(F32) * grad_step, axis=1)
    )
    packed = jnp.concatenate(
        [grad_shared, jnp.pad(gain_own[None], ((0, 7), (0, 2 * NS - gain_own.shape[0])))], axis=0
    )
    packed = tp_sum(packed)
    owned = grad_shared.shape[0]
    grad_norm_gain = packed[owned, : gain_own.shape[0]] / norm_gain.astype(F32)
    return (
        early[1],
        early[0],
        grad_norm_gain,
        grad_gate,
        grad_inner,
        packed[:owned],
        grad_step,
        *early[2:],
        grad_out,
    )


def solution(mesh):
    sizes = (mesh.shape["fsdp"], mesh.shape["tp"])

    def per_device(*args):
        return program(sizes, args)

    return jax.shard_map(
        per_device,
        mesh=mesh,
        in_specs=(
            P(("fsdp", "tp"), None),
            P("fsdp"),
            P("fsdp", "tp"),
            P("fsdp", "tp"),
            P("fsdp", None),
            P("fsdp", "tp"),
            P(None, "tp"),
            P("tp"),
            P(),
            P(),
            P("tp"),
            P("tp"),
            P("tp"),
            P("tp"),
            P("fsdp", "tp"),
            P("fsdp", None),
            P(("fsdp", "tp"), None),
        ),
        out_specs=(
            P(("fsdp", "tp"), None),
            P(("fsdp", "tp"), None),
            P("fsdp"),
            P("fsdp", "tp"),
            P("fsdp", "tp"),
            P("fsdp", None),
            P("fsdp", "tp"),
            P(None, "tp"),
            P("tp"),
            P(),
            P(),
            P("tp"),
            P("tp"),
            P("tp"),
            P("tp"),
            P("fsdp", "tp"),
        ),
        check_vma=False,
    )
```

```python
import jax
import jax.numpy as jnp
from jax import lax
from jax.experimental import pallas as pl
from jax.experimental.pallas import tpu as pltpu
from jax.sharding import PartitionSpec as P

INNER = 2048
NS = 128
HEAD = 64
Q = 128
LOG2E = 1.4426950408889634
FAR = -1e30
EPSILON = 1e-05

F32 = jnp.float32
BF16 = jnp.bfloat16
HIGH = lax.Precision.HIGHEST


def mm(a, b):
    return jnp.dot(a, b, preferred_element_type=F32)


def mm_t(a, b):
    return lax.dot_general(a, b, (((1,), (1,)), ((), ())), preferred_element_type=F32)


def weight_grad(a, b):
    return lax.dot_general(a, b, (((0,), (0,)), ((), ())), preferred_element_type=F32)


def iota(shape, dim):
    return lax.broadcasted_iota(jnp.int32, shape, dim)


def softplus(v):
    return jnp.maximum(v, 0.0) + jnp.log1p(jnp.exp(-jnp.abs(v)))


def wide(column):
    return jnp.broadcast_to(column, (Q, 128))


def pair_of(first, array, pair):
    return jnp.where(
        first, wide(array[:, 2 * pair : 2 * pair + 1]), wide(array[:, 2 * pair + 1 : 2 * pair + 2])
    )


def skip_of(first, heads_ref, pair):
    line = heads_ref[2:3, :]
    return jnp.where(
        first,
        jnp.broadcast_to(line[:, 2 * pair : 2 * pair + 1], (1, 128)),
        jnp.broadcast_to(line[:, 2 * pair + 1 : 2 * pair + 2], (1, 128)),
    )


def folded(block):
    return jnp.sum(block.reshape(Q // 8, 8, 128), axis=0)


def stacked(first, block):
    nil = jnp.zeros_like(block)
    return jnp.concatenate([jnp.where(first, block, nil), jnp.where(first, nil, block)], axis=0)


def forward_kernel(
    turn_ref, u_ref, s_ref, step_ref, aux_ref, seg_ref,
    inner_ref, inner_bias_ref, shared_ref, shared_bias_ref, heads_ref,
    y_ref, conv_ref, convs_ref, states_ref, steps_ref,
    ubuf, sbuf, state, xtail,
):
    width = u_ref.shape[1]
    chunk = pl.program_id(0)

    @pl.when(chunk == 0)
    def _():
        ubuf[0:8, :] = jnp.zeros((8, width), F32)
        sbuf[0:8, :] = jnp.zeros((8, 2 * NS), F32)
        state[...] = jnp.zeros_like(state)

    @pl.when(chunk > 0)
    def _():
        ubuf[0:8, :] = ubuf[Q : Q + 8, :]
        sbuf[0:8, :] = sbuf[Q : Q + 8, :]

    ubuf[8 : Q + 8, :] = u_ref[...].astype(F32)
    sbuf[8 : Q + 8, :] = s_ref[...].astype(F32)
    aux = aux_ref[...]
    same = [wide(aux[:, k : k + 1]) for k in range(3)]
    keep = wide(aux[:, 6:7])
    tail_in = wide(aux[:, 7:8])

    def conv_of(buf, taps_ref, bias_ref, cols):
        weights = taps_ref[:, cols].astype(F32)
        total = bias_ref[:, cols].astype(F32) + weights[3:4] * buf[8 : Q + 8, cols]
        for shift in range(1, 4):
            total = total + weights[3 - shift : 4 - shift] * (
                buf[8 - shift : Q + 8 - shift, cols] * same[shift - 1]
            )
        return total

    def silu(v):
        return v * (0.5 + 0.5 * jnp.tanh(0.5 * v))

    conv_b = conv_of(sbuf, shared_ref, shared_bias_ref, slice(0, NS))
    conv_c = conv_of(sbuf, shared_ref, shared_bias_ref, slice(NS, 2 * NS))
    convs_ref[:, 0:NS] = conv_b
    convs_ref[:, NS : 2 * NS] = conv_c
    b_f = silu(conv_b)
    b_low = b_f.astype(BF16)
    b_turn = b_f.T.astype(BF16)
    c_low = silu(conv_c).astype(BF16)
    inner_cb = mm_t(c_low, b_low)
    visible = (wide(aux[:, 8:9]) == seg_ref[0]) & (iota((Q, Q), 0) >= iota((Q, Q), 1))
    bias = jnp.where(visible, 0.0, FAR)
    dt = softplus(step_ref[...].astype(F32) + heads_ref[0:1, :])
    lower = (iota((Q, Q), 0) >= iota((Q, Q), 1)).astype(BF16)
    rest = dt * (heads_ref[1:2, :] * LOG2E)
    cum = jnp.zeros((Q, 128), F32)
    for _ in range(3):
        piece = rest.astype(BF16)
        cum = cum + mm(lower, piece)
        rest = rest - piece.astype(F32)
    cum_t = cum.T
    steps_ref[0, 0] = dt
    steps_ref[0, 1] = cum
    steps_ref[0, 2] = cum_t
    first = iota((Q, 128), 1) < HEAD
    state_low = state[...].astype(BF16)
    states_ref[0] = state_low
    carried = mm(c_low, state_low)
    for pair in range(width // 128):
        cols = slice(128 * pair, 128 * pair + 128)
        conv = conv_of(ubuf, inner_ref, inner_bias_ref, cols)
        conv_ref[:, cols] = conv
        x = silu(conv)
        cum_1 = wide(cum[:, 2 * pair : 2 * pair + 1])
        cum_2 = wide(cum[:, 2 * pair + 1 : 2 * pair + 2])
        m_1 = inner_cb * jnp.exp2(cum_1 - cum_t[2 * pair : 2 * pair + 1, :] + bias)
        m_2 = inner_cb * jnp.exp2(cum_2 - cum_t[2 * pair + 1 : 2 * pair + 2, :] + bias)
        xd = x * pair_of(first, dt, pair)
        mixers = jnp.concatenate([m_1.astype(BF16), m_2.astype(BF16)], axis=1)
        y = mm(mixers, stacked(first, xd.astype(BF16)))
        cum_p = jnp.where(first, cum_1, cum_2)
        last = cum_p[Q - 1 : Q, :]
        y = y + carried[:, cols] * (jnp.exp2(cum_p) * keep)
        y_ref[:, cols] = (y + skip_of(first[0:1], heads_ref, pair) * x).astype(BF16)
        tail = jnp.exp2(last - cum_p) * tail_in
        xtail[:, cols] = (xd * tail).astype(BF16)
        state[:, cols] = state[:, cols] * (jnp.exp2(last) * keep[Q - 1 : Q, :])
    state[...] += mm(b_turn, xtail[...])


def backward_kernel(
    turn_ref, u_ref, s_ref, conv_ref, convs_ref, step_ref, steps_ref, aux_ref, seg_ref, grad_ref, states_ref,
    inner_ref, shared_ref, heads_ref,
    low_ref, inner_sum, shared_sum, heads_sum,
    dbuf, dsbuf, dstate, dcum_t, red, wgrad, xtail, to_head, lower_low, inner_acc, shared_acc,
):
    width = u_ref.shape[1]
    chunk = pl.program_id(0)

    @pl.when(chunk == 0)
    def _():
        dbuf[Q : Q + 8, :] = jnp.zeros((8, width), F32)
        dsbuf[Q : Q + 8, :] = jnp.zeros((8, 2 * NS), F32)
        dstate[...] = jnp.zeros_like(dstate)
        dcum_t[...] = jnp.zeros_like(dcum_t)
        inner_acc[...] = jnp.zeros_like(inner_acc)
        shared_acc[...] = jnp.zeros_like(shared_acc)
        heads_sum[...] = jnp.zeros_like(heads_sum)
        to_head[...] = (
            iota((width, 128), 0) // HEAD == iota((width, 128), 1)
        ).astype(BF16)
        row_2, column_2 = iota((2 * Q, 2 * Q), 0), iota((2 * Q, 2 * Q), 1)
        lower_low[...] = ((row_2 // Q == column_2 // Q) & (row_2 >= column_2)).astype(BF16)

    @pl.when(chunk > 0)
    def _():
        dbuf[Q : Q + 8, :] = dbuf[0:8, :]
        dsbuf[Q : Q + 8, :] = dsbuf[0:8, :]

    aux = aux_ref[...]
    same = [wide(aux[:, 3 + k : 4 + k]) for k in range(3)]
    keep = wide(aux[:, 6:7])
    tail_in = wide(aux[:, 7:8])

    def silu_and_slope(v):
        sig = 0.5 + 0.5 * jnp.tanh(0.5 * v)
        act = v * sig
        return act, sig + act * (1.0 - sig)

    b_f, b_slope = silu_and_slope(convs_ref[:, 0:NS])
    c_f, c_slope = silu_and_slope(convs_ref[:, NS : 2 * NS])
    b_low = b_f.astype(BF16)
    c_low = c_f.astype(BF16)
    c_turn = c_f.T.astype(BF16)
    inner_bc = mm_t(b_low, c_low)
    row, column = iota((Q, Q), 0), iota((Q, Q), 1)
    visible = (wide(aux[:, 8:9]) == seg_ref[0]) & (row <= column)
    bias = jnp.where(visible, 0.0, FAR)
    strict = jnp.concatenate([row < column, row < column], axis=1)
    inner_2 = jnp.concatenate([inner_bc, inner_bc], axis=1)
    bias_2 = jnp.concatenate([bias, bias], axis=1)
    raw = step_ref[...].astype(F32) + heads_ref[0:1, :]
    dt, cum, cum_t = steps_ref[0, 0], steps_ref[0, 1], steps_ref[0, 2]
    first = iota((Q, 128), 1) < HEAD
    dinner = jnp.zeros((Q, 2 * Q), F32)
    later_low = dstate[...].astype(BF16)
    end_all = mm(b_low, later_low)
    start_all = mm(c_low, states_ref[0])
    for pair in range(width // 128):
        cols = slice(128 * pair, 128 * pair + 128)
        cum_1 = wide(cum[:, 2 * pair : 2 * pair + 1])
        cum_2 = wide(cum[:, 2 * pair + 1 : 2 * pair + 2])
        ahead = jnp.concatenate(
            [cum_t[2 * pair : 2 * pair + 1, :], cum_t[2 * pair + 1 : 2 * pair + 2, :]], axis=1
        )
        decay = jnp.exp2(ahead - jnp.concatenate([cum_1, cum_2], axis=1) + bias_2)
        m = inner_2 * decay
        x, slope = silu_and_slope(conv_ref[:, cols])
        dt_p = pair_of(first, dt, pair)
        xd = x * dt_p
        grad = grad_ref[:, cols].astype(F32)
        grad_two = stacked(first, grad_ref[:, cols].astype(BF16))
        dm = mm_t(xd.astype(BF16), grad_two)
        dinner = dinner + dm * decay
        spans = mm((dm * m).astype(BF16), lower_low[...])
        gaps = jnp.sum(jnp.where(strict, spans, 0.0), axis=0, keepdims=True)
        dcum_t[2 * pair : 2 * pair + 1, :] = gaps[:, 0:Q]
        dcum_t[2 * pair + 1 : 2 * pair + 2, :] = gaps[:, Q : 2 * Q]
        dxd = mm(m.astype(BF16), grad_two)
        cum_p = jnp.where(first, cum_1, cum_2)
        last = cum_p[Q - 1 : Q, :]
        tail = jnp.exp2(last - cum_p) * tail_in
        later = dstate[:, cols]
        old_low = states_ref[0, :, cols]
        xt = xd * tail
        from_end = end_all[:, cols]
        dxd = dxd + tail * from_end
        weight = jnp.exp2(cum_p) * keep
        wg = grad * weight
        from_start = start_all[:, cols]
        carry = jnp.exp2(last) * keep[Q - 1 : Q, :]
        carried = jnp.sum(later * old_low.astype(F32), axis=0, keepdims=True) * carry
        red[0:Q, cols] = (dxd * x).astype(BF16)
        red[Q : 2 * Q, cols] = (xt * from_end).astype(BF16)
        red[2 * Q : 3 * Q, cols] = (wg * from_start).astype(BF16)
        red[3 * Q : 3 * Q + 16, cols] = jnp.broadcast_to(carried, (16, 128)).astype(BF16)
        wg_low = wg.astype(BF16)
        wgrad[:, cols] = wg_low
        xtail[:, cols] = xt.astype(BF16)
        dx = dxd * dt_p + skip_of(first[0:1], heads_ref, pair) * grad
        dbuf[0:Q, cols] = dx * slope
        inner_acc[40:48, cols] += folded(grad * x)

    sums = mm(red[...], to_head[...])
    spread = jnp.concatenate([(row > column).astype(BF16), (row <= column).astype(BF16)], axis=1)
    dla = dcum_t[...].T + mm(spread, sums[Q : 3 * Q, :].astype(BF16)) + sums[3 * Q : 3 * Q + 1, :]
    rate = heads_ref[1:2, :]
    ddt = sums[0:Q, :] + rate * dla
    dstep = ddt * (0.5 + 0.5 * jnp.tanh(0.5 * raw))
    low_ref[:, width + 2 * NS : width + 2 * NS + 128] = dstep.astype(BF16)
    heads_sum[0:1, :] += jnp.sum(dstep, axis=0, keepdims=True)
    heads_sum[1:2, :] += jnp.sum(dla * dt * rate, axis=0, keepdims=True)

    dinner = dinner[:, 0:Q] + dinner[:, Q : 2 * Q]
    dinner_low = dinner.astype(BF16)
    db = mm(dinner_low, c_low) + mm_t(xtail[...], later_low)
    dc = mm(dinner.T.astype(BF16), b_low) + mm_t(wgrad[...], states_ref[0])
    dsbuf[0:Q, 0:NS] = db * b_slope
    dsbuf[0:Q, NS : 2 * NS] = dc * c_slope

    def conv_back(u, buf, taps_ref, acc, cols):
        weights = taps_ref[:, cols].astype(F32)
        d = buf[0:Q, cols]
        du = weights[3:4] * d
        acc[24:32, cols] += folded(d * u)
        acc[32:40, cols] += folded(d)
        for shift in range(1, 4):
            d = buf[shift : Q + shift, cols] * same[shift - 1]
            du = du + weights[3 - shift : 4 - shift] * d
            acc[24 - 8 * shift : 32 - 8 * shift, cols] += folded(d * u)
        return du

    for part in range(2):
        cols = slice(NS * part, NS * part + NS)
        low_ref[:, width + NS * part : width + NS * part + NS] = conv_back(
            s_ref[:, cols].astype(F32), dsbuf, shared_ref, shared_acc, cols
        ).astype(BF16)
    new = mm(c_turn, wgrad[...])
    for pair in range(width // 128):
        cols = slice(128 * pair, 128 * pair + 128)
        low_ref[:, cols] = conv_back(
            u_ref[:, cols].astype(F32), dbuf, inner_ref, inner_acc, cols
        ).astype(BF16)
        cum_p = jnp.where(
            first[0:1, :],
            jnp.broadcast_to(cum[Q - 1 : Q, 2 * pair : 2 * pair + 1], (1, 128)),
            jnp.broadcast_to(cum[Q - 1 : Q, 2 * pair + 1 : 2 * pair + 2], (1, 128)),
        )
        carry = jnp.exp2(cum_p) * keep[Q - 1 : Q, :]
        dstate[:, cols] = dstate[:, cols] * carry + new[:, cols]

    @pl.when(chunk == pl.num_programs(0) - 1)
    def _():
        for out, acc, count in ((inner_sum, inner_acc, 6), (shared_sum, shared_acc, 5)):
            out[...] = jnp.zeros_like(out)
            for k in range(count):
                out[k : k + 1, :] = jnp.sum(acc[8 * k : 8 * k + 8, :], axis=0, keepdims=True)


VMEM_LIMIT = 32 * 1024 * 1024


def forward_mix(turn, proj, aux, seg_rows, inner_p, inner_b, shared_p, shared_b, heads_p):
    length = proj.shape[0]
    width = inner_p.shape[1]
    chunks = length // Q

    def rows(n, at=0):
        return pl.BlockSpec((Q, n), lambda c, turn: (lax.rem(c + turn[0], chunks), at))

    def plain(n):
        return pl.BlockSpec((Q, n), lambda c, turn: (c, 0))

    def whole(n, rows=8):
        return pl.BlockSpec((rows, n), lambda c, turn: (0, 0))

    line = pl.BlockSpec((1, 1, Q), lambda c, turn: (c, 0, 0))
    kept = pl.BlockSpec((1, NS, width), lambda c, turn: (c, 0, 0))
    return pl.pallas_call(
        forward_kernel,
        grid_spec=pltpu.PrefetchScalarGridSpec(
            num_scalar_prefetch=1,
            grid=(chunks,),
            in_specs=[
                rows(width), rows(2 * NS, width // (2 * NS)), rows(128, (width + 2 * NS) // 128),
                plain(16), line, whole(width, 4), whole(width, 1), whole(2 * NS, 4),
                whole(2 * NS, 1), whole(128),
            ],
            out_specs=[
                rows(width), plain(width), plain(2 * NS), kept,
                pl.BlockSpec((1, 3, Q, 128), lambda c, turn: (c, 0, 0, 0)),
            ],
            scratch_shapes=[
                pltpu.VMEM((Q + 8, width), F32),
                pltpu.VMEM((Q + 8, 2 * NS), F32),
                pltpu.VMEM((NS, width), F32),
                pltpu.VMEM((Q, width), BF16),
            ],
        ),
        out_shape=[
            jax.ShapeDtypeStruct((length, width), BF16),
            jax.ShapeDtypeStruct((length, width), F32),
            jax.ShapeDtypeStruct((length, 2 * NS), F32),
            jax.ShapeDtypeStruct((chunks, NS, width), BF16),
            jax.ShapeDtypeStruct((chunks, 3, Q, 128), F32),
        ],
        compiler_params=pltpu.CompilerParams(vmem_limit_bytes=VMEM_LIMIT),
        cost_estimate=pl.CostEstimate(
            flops=32 * length * 128 * width, bytes_accessed=12 * length * width, transcendentals=0
        ),
        name="mix_forward",
    )(turn, proj, proj, proj, aux, seg_rows, inner_p, inner_b, shared_p, shared_b, heads_p)


def backward_mix(turn, proj, conv, convs, steps, aux, seg_rows, grad, states, inner_p, shared_p, heads_p):
    length = proj.shape[0]
    width = inner_p.shape[1]
    chunks = length // Q

    def rows(n, at=0):
        return pl.BlockSpec(
            (Q, n), lambda c, turn: (lax.rem(chunks - 1 - c + turn[0], chunks), at)
        )

    def plain(n):
        return pl.BlockSpec((Q, n), lambda c, turn: (chunks - 1 - c, 0))

    def whole(n, rows=8):
        return pl.BlockSpec((rows, n), lambda c, turn: (0, 0))

    line = pl.BlockSpec((1, 1, Q), lambda c, turn: (chunks - 1 - c, 0, 0))
    kept = pl.BlockSpec((1, NS, width), lambda c, turn: (chunks - 1 - c, 0, 0))
    return pl.pallas_call(
        backward_kernel,
        grid_spec=pltpu.PrefetchScalarGridSpec(
            num_scalar_prefetch=1,
            grid=(chunks,),
            in_specs=[
                rows(width), rows(2 * NS, width // (2 * NS)), plain(width), plain(2 * NS),
                rows(128, (width + 2 * NS) // 128),
                pl.BlockSpec((1, 3, Q, 128), lambda c, turn: (chunks - 1 - c, 0, 0, 0)),
                plain(16), line, rows(width), kept,
                whole(width, 4), whole(2 * NS, 4), whole(128),
            ],
            out_specs=[rows(width + 2 * NS + 128), whole(width), whole(2 * NS), whole(128)],
            scratch_shapes=[
                pltpu.VMEM((Q + 8, width), F32),
                pltpu.VMEM((Q + 8, 2 * NS), F32),
                pltpu.VMEM((NS, width), F32),
                pltpu.VMEM((128, Q), F32),
                pltpu.VMEM((3 * Q + 16, width), BF16),
                pltpu.VMEM((Q, width), BF16),
                pltpu.VMEM((Q, width), BF16),
                pltpu.VMEM((width, 128), BF16),
                pltpu.VMEM((2 * Q, 2 * Q), BF16),
                pltpu.VMEM((48, width), F32),
                pltpu.VMEM((48, 2 * NS), F32),
            ],
        ),
        out_shape=[
            jax.ShapeDtypeStruct((length, width + 2 * NS + 128), BF16),
            jax.ShapeDtypeStruct((8, width), F32),
            jax.ShapeDtypeStruct((8, 2 * NS), F32),
            jax.ShapeDtypeStruct((8, 128), F32),
        ],
        compiler_params=pltpu.CompilerParams(vmem_limit_bytes=VMEM_LIMIT),
        cost_estimate=pl.CostEstimate(
            flops=70 * length * 128 * width, bytes_accessed=20 * length * width, transcendentals=0
        ),
        name="mix_backward",
    )(turn, proj, proj, conv, convs, proj, steps, aux, seg_rows, grad, states, inner_p, shared_p, heads_p)


def aux_of(seg_line):
    length = seg_line.shape[0]
    ends = seg_line.reshape(-1, Q)[:, Q - 1]
    prior = jnp.concatenate([jnp.full((1,), -1, seg_line.dtype), ends[:-1]])
    place = jnp.arange(length)
    columns = []
    for shift in range(1, 4):
        columns.append((jnp.roll(seg_line, shift) == seg_line) & (place >= shift))
    for shift in range(1, 4):
        columns.append((jnp.roll(seg_line, -shift) == seg_line) & (place < length - shift))
    columns.append(seg_line == jnp.repeat(prior, Q))
    columns.append(seg_line == jnp.repeat(ends, Q))
    columns = [column.astype(F32) for column in columns] + [seg_line.astype(F32)]
    columns += [jnp.zeros((length,), F32)] * (16 - len(columns))
    rows = seg_line.astype(F32).reshape(-1, 1, Q)
    return jnp.stack(columns, axis=1), rows


def program(sizes, args):
    (
        hidden, norm_gain, weight_gate, weight_inner, weight_shared, weight_step,
        filter_inner, bias_inner, filter_shared, bias_shared, step_bias, log_rate, skip_gain,
        gate_gain, weight_out, segments, cotangent,
    ) = args
    n_fsdp, n_tp = sizes
    width = weight_gate.shape[1]
    heads = weight_step.shape[1]
    own_rows = hidden.shape[0]
    length = segments.shape[1]
    tp_place = lax.axis_index("tp")
    paired = n_tp == 2

    def tp_rows(own):
        if paired:
            return jnp.concatenate([own, lax.ppermute(own, "tp", [(0, 1), (1, 0)])], axis=0)
        return lax.all_gather(own, "tp", axis=0, tiled=True)

    def tp_scatter(make):
        if paired:
            away = make(slice(own_rows, 2 * own_rows)).astype(BF16)
            got = lax.ppermute(away, "tp", [(0, 1), (1, 0)])
            return make(slice(0, own_rows)), got
        return lax.psum_scatter(make(slice(None)), "tp", scatter_dimension=0, tiled=True), 0.0

    fsdp_place = lax.axis_index("fsdp")
    outer = n_fsdp // 2
    digits = [(4, n_fsdp // 4), (outer // 4, 2), (2, 1)] if outer % 4 == 0 else [(outer, 2), (2, 1)]

    def stage(blocks, axis):
        size, stride = digits[axis]
        place = lax.rem(fsdp_place // stride, size)
        parts = [blocks]
        for step in range(1, size):
            moves = []
            for i in range(n_fsdp):
                at = (i // stride) % size
                moves.append((i, i + ((at + step) % size - at) * stride))
            parts.append(lax.ppermute(blocks, "fsdp", moves))
        if size == 2:
            own, away = parts
            return jnp.where(
                place == 0,
                jnp.stack([own, away], axis=axis),
                jnp.stack([away, own], axis=axis),
            )
        if size > 2:
            ring = jnp.stack(parts[::-1] + parts[::-1], axis=axis)
            return lax.dynamic_slice_in_dim(ring, size - 1 - place, size, axis)
        return jnp.expand_dims(blocks, axis)

    def line_gather(shard):
        blocks = shard
        for axis in range(len(digits)):
            blocks = stage(blocks, axis)
        return blocks.reshape(n_fsdp * shard.shape[0], shard.shape[1])

    even = lax.rem(fsdp_place, 2) == 0

    def core_halves(total):
        blocks = total.reshape(outer, 2, total.shape[0] // n_fsdp, total.shape[1])
        away = jnp.where(even, blocks[:, 1], blocks[:, 0])
        return away, jnp.where(even, blocks[:, 0], blocks[:, 1])

    def core_sum(total):
        away, mine = core_halves(total)
        got = lax.ppermute(away, "fsdp", other_core)
        return (mine.astype(F32) + got.astype(F32)).astype(BF16).reshape(-1, total.shape[1])

    other_core = [(i, i ^ 1) for i in range(n_fsdp)]

    def chip_swap(half):
        groups = [[i for i in range(n_fsdp) if i % 2 == core] for core in range(2)]
        return lax.all_to_all(half, "fsdp", 0, 0, axis_index_groups=groups, tiled=True)

    def chip_sum(swapped):
        return jnp.sum(swapped.reshape(outer, -1, swapped.shape[1]).astype(F32), axis=0)

    pad = jnp.zeros((weight_step.shape[0], 128 - heads - 1), BF16)
    shard_a = jnp.concatenate(
        [weight_inner, weight_shared, weight_step, norm_gain[:, None], pad], axis=1
    )
    hidden_all = tp_rows(hidden)
    next_chip = [(i, i ^ 2) for i in range(n_fsdp)]
    lower_line = lax.rem(fsdp_place // 2, 2) == 0

    def swapped(flag, one, two):
        return jnp.where(flag, jnp.stack([one, two], axis=1), jnp.stack([two, one], axis=1))

    def weave(near, near_core, far, far_core):
        both = swapped(lower_line, swapped(even, near, near_core), swapped(even, far, far_core))
        return both.reshape(-1, near.shape[-1])

    if len(digits) == 3 and digits[1][0] == 2:
        line_a = stage(shard_a, 0)
        core_a = lax.ppermute(line_a, "fsdp", other_core)
        next_a = lax.ppermute(line_a, "fsdp", next_chip)
        next_core_a = lax.ppermute(next_a, "fsdp", other_core)
        weights_a = weave(line_a, core_a, next_a, next_core_a)
    else:
        weights_a = line_gather(shard_a)
    woven = len(digits) == 3 and digits[1][0] == 2
    if woven:
        shard_b = jnp.concatenate([weight_gate, weight_out], axis=1)
        size, span = digits[0]
        circles = [[i + span * step for step in range(size)] for i in range(span)]
        line = lax.all_to_all(
            jnp.broadcast_to(shard_b[None], (size,) + shard_b.shape), "fsdp", 0, 0,
            axis_index_groups=circles, tiled=True)
        line_core = lax.ppermute(line, "fsdp", other_core)
        next_line = lax.ppermute(line, "fsdp", next_chip)
    else:
        gate_all, out_all = line_gather(weight_gate), line_gather(weight_out)
    if paired:
        late_cot, hidden_all = lax.optimization_barrier((cotangent, hidden_all))
        cot_got = lax.ppermute(late_cot, "tp", [(0, 1), (1, 0)])
    else:
        cot_got = lax.all_gather(cotangent, "tp", axis=0, tiled=True)
    gain_row = weights_a[:, width + 2 * NS + heads].astype(F32)[None, :]

    hidden_f = hidden_all.astype(F32)
    inv_rms = lax.rsqrt(jnp.mean(hidden_f * hidden_f, axis=1, keepdims=True) + EPSILON)
    normed = (hidden_f * inv_rms * gain_row).astype(BF16)
    normed = lax.optimization_barrier(normed)
    proj = mm(normed, weights_a).astype(BF16)

    turn = (tp_place * (own_rows // Q) if paired else jnp.zeros((), jnp.int32)).reshape(1)
    turn = turn.astype(jnp.int32)
    aux, seg_rows = aux_of(segments[0])
    heads_p = jnp.pad(
        jnp.stack(
            [step_bias.astype(F32), -jnp.exp(log_rate.astype(F32)), skip_gain.astype(F32)]
        ),
        ((0, 5), (0, 128 - heads)),
    )
    y, conv, convs, states, steps = forward_mix(
        turn, proj, aux, seg_rows, filter_inner, bias_inner[None], filter_shared,
        bias_shared[None], heads_p,
    )

    if woven:
        y, next_line, cot_got, line, line_core = lax.optimization_barrier(
            (y, next_line, cot_got, line, line_core)
        )
        next_core = lax.ppermute(next_line, "fsdp", other_core)
        pieces = (line, line_core, next_line, next_core)
        gate_all, out_all = (
            weave(*[piece[:, :, at : at + width] for piece in pieces]) for at in (0, width)
        )
    else:
        y, gate_all, out_all, cot_got = lax.optimization_barrier((y, gate_all, out_all, cot_got))
    cot_all = jnp.concatenate([cotangent, cot_got], axis=0) if paired else cot_got
    gate_z = mm(normed, gate_all).astype(BF16).astype(F32)
    grad_gated = mm(cot_all, out_all).astype(BF16).astype(F32)
    y = y.astype(F32)
    gain_gate = gate_gain.astype(F32)[None, :]
    sig = jax.nn.sigmoid(gate_z)
    act = gate_z * sig
    mixed = y * act
    scaled = grad_gated * gain_gate
    sums = jnp.stack([jnp.sum(mixed * mixed, axis=1), jnp.sum(mixed * scaled, axis=1)], axis=1)
    if paired:
        half = jnp.concatenate([sums[own_rows:], sums[:own_rows]], axis=0)
        sums = sums + lax.ppermute(half, "tp", [(0, 1), (1, 0)])
    else:
        sums = lax.psum(sums, "tp")
    inv_gate = lax.rsqrt(sums[:, 0:1] / INNER + EPSILON)
    gated = (mixed * inv_gate * gain_gate).astype(BF16)
    grad_mixed = inv_gate * scaled - mixed * (inv_gate * inv_gate * inv_gate) * (
        sums[:, 1:2] / INNER
    )
    grad_y = grad_mixed * act
    low_z = (grad_mixed * y * (sig + act * (1.0 - sig))).astype(BF16)
    grad_gain_gate = jnp.sum(grad_gated * mixed * inv_gate, axis=0)
    grad_y, low_z, gated = lax.optimization_barrier((grad_y.astype(BF16), low_z, gated))
    half_b = jnp.concatenate(
        [core_sum(weight_grad(normed, low_z).astype(BF16)),
         core_sum(weight_grad(cot_all, gated).astype(BF16))], axis=1)
    out_own, out_got = tp_scatter(lambda at: mm_t(gated[at], out_all))
    half_b, grad_y, out_own = lax.optimization_barrier((half_b, grad_y, out_own))
    swap_b = chip_swap(half_b)
    low, inner_sum, shared_sum, heads_sum = backward_mix(
        turn, proj, conv, convs, steps, aux, seg_rows, grad_y, states, filter_inner,
        filter_shared, heads_p
    )
    small = jnp.concatenate(
        [jnp.concatenate([inner_sum[:6], grad_gain_gate[None], inner_sum[7:]], axis=0),
         shared_sum, heads_sum], axis=1)
    reach = 1
    while reach < n_fsdp:
        small = small + lax.ppermute(small, "fsdp", [(i, i ^ reach) for i in range(n_fsdp)])
        reach *= 2
    low, out_got = lax.optimization_barrier((low, out_got))
    grads_a = weight_grad(normed, low).astype(BF16)
    def input_rows(at):
        return mm_t(low_z[at], gate_all) + mm_t(low[at], weights_a)

    away_a, mine_a = core_halves(grads_a)
    away_a, mine_a, swap_b = lax.optimization_barrier((away_a, mine_a, swap_b))
    away_a = lax.ppermute(away_a, "fsdp", other_core)
    if paired:
        away_part = input_rows(slice(own_rows, 2 * own_rows)).astype(BF16)
    else:
        away_part = input_rows(slice(None))
    if paired:
        part_got = lax.ppermute(away_part, "tp", [(0, 1), (1, 0)]).astype(F32)
        part_own = input_rows(slice(0, own_rows))
    else:
        part_own = lax.psum_scatter(away_part, "tp", scatter_dimension=0, tiled=True)
        part_got = 0.0
    half_a = (mine_a.astype(F32) + away_a.astype(F32)).astype(BF16).reshape(-1, low.shape[1])
    swap_a = chip_swap(half_a)
    layer_out = (hidden.astype(F32) + out_own + out_got).astype(BF16)
    grad_normed = part_own + part_got
    x_hat = hidden.astype(F32) * inv_rms[:own_rows] if paired else None
    inv_own = inv_rms[:own_rows]
    if not paired:
        inv_own = lax.dynamic_slice_in_dim(inv_rms, tp_place * own_rows, own_rows, 0)
        x_hat = hidden.astype(F32) * inv_own
    scaled_in = grad_normed * gain_row
    grad_hidden = cotangent.astype(F32) + inv_own * (
        scaled_in - x_hat * jnp.mean(scaled_in * x_hat, axis=1, keepdims=True)
    )

    def tp_sum(value):
        if paired:
            return value + lax.ppermute(value, "tp", [(0, 1), (1, 0)])
        return lax.psum(value, "tp")

    shared_part = tp_sum(small[:, width : width + 2 * NS])
    early = (
        grad_hidden,
        layer_out,
        small[0:4, :width],
        small[4, :width],
        shared_part[0:4],
        shared_part[4],
        small[0, width + 2 * NS : width + 2 * NS + heads],
        small[1, width + 2 * NS : width + 2 * NS + heads],
        jnp.sum(small[5, :width].reshape(heads, HEAD), axis=1),
        small[6, :width],
    )
    swap_a, early = lax.optimization_barrier((swap_a, early))
    owned_a, owned_b = chip_sum(swap_a), chip_sum(swap_b)
    grad_gate, grad_out = owned_b[:, :width], owned_b[:, width:]
    grad_inner = owned_a[:, :width]
    grad_shared = owned_a[:, width : width + 2 * NS]
    grad_step = owned_a[:, width + 2 * NS : width + 2 * NS + heads]
    gain_own = (
        jnp.sum(weight_gate.astype(F32) * grad_gate, axis=1)
        + jnp.sum(weight_inner.astype(F32) * grad_inner, axis=1)
        + jnp.sum(weight_shared.astype(F32) * grad_shared, axis=1)
        + jnp.sum(weight_step.astype(F32) * grad_step, axis=1)
    )
    packed = jnp.concatenate(
        [grad_shared, jnp.pad(gain_own[None], ((0, 7), (0, 2 * NS - gain_own.shape[0])))], axis=0
    )
    packed = tp_sum(packed)
    owned = grad_shared.shape[0]
    grad_norm_gain = packed[owned, : gain_own.shape[0]] / norm_gain.astype(F32)
    return (
        early[1],
        early[0],
        grad_norm_gain,
        grad_gate,
        grad_inner,
        packed[:owned],
        grad_step,
        *early[2:],
        grad_out,
    )


def solution(mesh):
    sizes = (mesh.shape["fsdp"], mesh.shape["tp"])

    def per_device(*args):
        return program(sizes, args)

    return jax.shard_map(
        per_device,
        mesh=mesh,
        in_specs=(
            P(("fsdp", "tp"), None),
            P("fsdp"),
            P("fsdp", "tp"),
            P("fsdp", "tp"),
            P("fsdp", None),
            P("fsdp", "tp"),
            P(None, "tp"),
            P("tp"),
            P(),
            P(),
            P("tp"),
            P("tp"),
            P("tp"),
            P("tp"),
            P("fsdp", "tp"),
            P("fsdp", None),
            P(("fsdp", "tp"), None),
        ),
        out_specs=(
            P(("fsdp", "tp"), None),
            P(("fsdp", "tp"), None),
            P("fsdp"),
            P("fsdp", "tp"),
            P("fsdp", "tp"),
            P("fsdp", None),
            P("fsdp", "tp"),
            P(None, "tp"),
            P("tp"),
            P(),
            P(),
            P("tp"),
            P("tp"),
            P("tp"),
            P("tp"),
            P("fsdp", "tp"),
        ),
        check_vma=False,
    )
```

```python
import jax
import jax.numpy as jnp
from jax import lax
from jax.experimental import pallas as pl
from jax.experimental.pallas import tpu as pltpu
from jax.sharding import PartitionSpec as P

INNER = 2048
NS = 128
HEAD = 64
Q = 128
LOG2E = 1.4426950408889634
FAR = -1e30
EPSILON = 1e-05

F32 = jnp.float32
BF16 = jnp.bfloat16
HIGH = lax.Precision.HIGHEST


def mm(a, b):
    return jnp.dot(a, b, preferred_element_type=F32)


def mm_t(a, b):
    return lax.dot_general(a, b, (((1,), (1,)), ((), ())), preferred_element_type=F32)


def weight_grad(a, b):
    return lax.dot_general(a, b, (((0,), (0,)), ((), ())), preferred_element_type=F32)


def iota(shape, dim):
    return lax.broadcasted_iota(jnp.int32, shape, dim)


def softplus(v):
    return jnp.maximum(v, 0.0) + jnp.log1p(jnp.exp(-jnp.abs(v)))


def wide(column):
    return jnp.broadcast_to(column, (Q, 128))


def pair_of(first, array, pair):
    return jnp.where(
        first, wide(array[:, 2 * pair : 2 * pair + 1]), wide(array[:, 2 * pair + 1 : 2 * pair + 2])
    )


def skip_of(first, heads_ref, pair):
    line = heads_ref[2:3, :]
    return jnp.where(
        first,
        jnp.broadcast_to(line[:, 2 * pair : 2 * pair + 1], (1, 128)),
        jnp.broadcast_to(line[:, 2 * pair + 1 : 2 * pair + 2], (1, 128)),
    )


def folded(block):
    return jnp.sum(block.reshape(Q // 8, 8, 128), axis=0)


def stacked(first, block):
    nil = jnp.zeros_like(block)
    return jnp.concatenate([jnp.where(first, block, nil), jnp.where(first, nil, block)], axis=0)


def forward_kernel(
    turn_ref, u_ref, s_ref, step_ref, aux_ref, seg_ref,
    inner_ref, inner_bias_ref, shared_ref, shared_bias_ref, heads_ref,
    y_ref, conv_ref, convs_ref, states_ref, steps_ref,
    ubuf, sbuf, state, xtail,
):
    width = u_ref.shape[1]
    chunk = pl.program_id(0)

    @pl.when(chunk == 0)
    def _():
        ubuf[0:8, :] = jnp.zeros((8, width), F32)
        sbuf[0:8, :] = jnp.zeros((8, 2 * NS), F32)
        state[...] = jnp.zeros_like(state)

    @pl.when(chunk > 0)
    def _():
        ubuf[0:8, :] = ubuf[Q : Q + 8, :]
        sbuf[0:8, :] = sbuf[Q : Q + 8, :]

    ubuf[8 : Q + 8, :] = u_ref[...].astype(F32)
    sbuf[8 : Q + 8, :] = s_ref[...].astype(F32)
    aux = aux_ref[...]
    same = [wide(aux[:, k : k + 1]) for k in range(3)]
    keep = wide(aux[:, 6:7])
    tail_in = wide(aux[:, 7:8])

    def conv_of(buf, taps_ref, bias_ref, cols):
        weights = taps_ref[:, cols].astype(F32)
        total = bias_ref[:, cols].astype(F32) + weights[3:4] * buf[8 : Q + 8, cols]
        for shift in range(1, 4):
            total = total + weights[3 - shift : 4 - shift] * (
                buf[8 - shift : Q + 8 - shift, cols] * same[shift - 1]
            )
        return total

    def silu(v):
        return v * (0.5 + 0.5 * jnp.tanh(0.5 * v))

    conv_b = conv_of(sbuf, shared_ref, shared_bias_ref, slice(0, NS))
    conv_c = conv_of(sbuf, shared_ref, shared_bias_ref, slice(NS, 2 * NS))
    convs_ref[:, 0:NS] = conv_b
    convs_ref[:, NS : 2 * NS] = conv_c
    b_f = silu(conv_b)
    b_low = b_f.astype(BF16)
    b_turn = b_f.T.astype(BF16)
    c_low = silu(conv_c).astype(BF16)
    inner_cb = mm_t(c_low, b_low)
    visible = (wide(aux[:, 8:9]) == seg_ref[0]) & (iota((Q, Q), 0) >= iota((Q, Q), 1))
    bias = jnp.where(visible, 0.0, FAR)
    dt = softplus(step_ref[...].astype(F32) + heads_ref[0:1, :])
    lower = (iota((Q, Q), 0) >= iota((Q, Q), 1)).astype(BF16)
    rest = dt * (heads_ref[1:2, :] * LOG2E)
    cum = jnp.zeros((Q, 128), F32)
    for _ in range(3):
        piece = rest.astype(BF16)
        cum = cum + mm(lower, piece)
        rest = rest - piece.astype(F32)
    cum_t = cum.T
    steps_ref[0, 0] = dt
    steps_ref[0, 1] = cum
    steps_ref[0, 2] = cum_t
    first = iota((Q, 128), 1) < HEAD
    state_low = state[...].astype(BF16)
    states_ref[0] = state_low
    carried = mm(c_low, state_low)
    for pair in range(width // 128):
        cols = slice(128 * pair, 128 * pair + 128)
        conv = conv_of(ubuf, inner_ref, inner_bias_ref, cols)
        conv_ref[:, cols] = conv.astype(BF16)
        x = silu(conv)
        cum_1 = wide(cum[:, 2 * pair : 2 * pair + 1])
        cum_2 = wide(cum[:, 2 * pair + 1 : 2 * pair + 2])
        m_1 = inner_cb * jnp.exp2(cum_1 - cum_t[2 * pair : 2 * pair + 1, :] + bias)
        m_2 = inner_cb * jnp.exp2(cum_2 - cum_t[2 * pair + 1 : 2 * pair + 2, :] + bias)
        xd = x * pair_of(first, dt, pair)
        mixers = jnp.concatenate([m_1.astype(BF16), m_2.astype(BF16)], axis=1)
        y = mm(mixers, stacked(first, xd.astype(BF16)))
        cum_p = jnp.where(first, cum_1, cum_2)
        last = cum_p[Q - 1 : Q, :]
        y = y + carried[:, cols] * (jnp.exp2(cum_p) * keep)
        y_ref[:, cols] = (y + skip_of(first[0:1], heads_ref, pair) * x).astype(BF16)
        tail = jnp.exp2(last - cum_p) * tail_in
        xtail[:, cols] = (xd * tail).astype(BF16)
        state[:, cols] = state[:, cols] * (jnp.exp2(last) * keep[Q - 1 : Q, :])
    state[...] += mm(b_turn, xtail[...])


def backward_kernel(
    turn_ref, u_ref, s_ref, conv_ref, convs_ref, step_ref, steps_ref, aux_ref, seg_ref, grad_ref, states_ref,
    inner_ref, shared_ref, heads_ref,
    low_ref, inner_sum, shared_sum, heads_sum,
    dbuf, dsbuf, dstate, dcum_t, red, wgrad, xtail, to_head, lower_low, inner_acc, shared_acc,
):
    width = u_ref.shape[1]
    chunk = pl.program_id(0)

    @pl.when(chunk == 0)
    def _():
        dbuf[Q : Q + 8, :] = jnp.zeros((8, width), F32)
        dsbuf[Q : Q + 8, :] = jnp.zeros((8, 2 * NS), F32)
        dstate[...] = jnp.zeros_like(dstate)
        dcum_t[...] = jnp.zeros_like(dcum_t)
        inner_acc[...] = jnp.zeros_like(inner_acc)
        shared_acc[...] = jnp.zeros_like(shared_acc)
        heads_sum[...] = jnp.zeros_like(heads_sum)
        to_head[...] = (
            iota((width, 128), 0) // HEAD == iota((width, 128), 1)
        ).astype(BF16)
        row_2, column_2 = iota((2 * Q, 2 * Q), 0), iota((2 * Q, 2 * Q), 1)
        lower_low[...] = ((row_2 // Q == column_2 // Q) & (row_2 >= column_2)).astype(BF16)

    @pl.when(chunk > 0)
    def _():
        dbuf[Q : Q + 8, :] = dbuf[0:8, :]
        dsbuf[Q : Q + 8, :] = dsbuf[0:8, :]

    aux = aux_ref[...]
    same = [wide(aux[:, 3 + k : 4 + k]) for k in range(3)]
    keep = wide(aux[:, 6:7])
    tail_in = wide(aux[:, 7:8])

    def silu_and_slope(v):
        sig = 0.5 + 0.5 * jnp.tanh(0.5 * v)
        act = v * sig
        return act, sig + act * (1.0 - sig)

    b_f, b_slope = silu_and_slope(convs_ref[:, 0:NS])
    c_f, c_slope = silu_and_slope(convs_ref[:, NS : 2 * NS])
    b_low = b_f.astype(BF16)
    c_low = c_f.astype(BF16)
    c_turn = c_f.T.astype(BF16)
    inner_bc = mm_t(b_low, c_low)
    row, column = iota((Q, Q), 0), iota((Q, Q), 1)
    visible = (wide(aux[:, 8:9]) == seg_ref[0]) & (row <= column)
    bias = jnp.where(visible, 0.0, FAR)
    strict = jnp.concatenate([row < column, row < column], axis=1)
    inner_2 = jnp.concatenate([inner_bc, inner_bc], axis=1)
    bias_2 = jnp.concatenate([bias, bias], axis=1)
    raw = step_ref[...].astype(F32) + heads_ref[0:1, :]
    dt, cum, cum_t = steps_ref[0, 0], steps_ref[0, 1], steps_ref[0, 2]
    first = iota((Q, 128), 1) < HEAD
    dinner = jnp.zeros((Q, 2 * Q), F32)
    later_low = dstate[...].astype(BF16)
    end_all = mm(b_low, later_low)
    start_all = mm(c_low, states_ref[0])
    for pair in range(width // 128):
        cols = slice(128 * pair, 128 * pair + 128)
        cum_1 = wide(cum[:, 2 * pair : 2 * pair + 1])
        cum_2 = wide(cum[:, 2 * pair + 1 : 2 * pair + 2])
        ahead = jnp.concatenate(
            [cum_t[2 * pair : 2 * pair + 1, :], cum_t[2 * pair + 1 : 2 * pair + 2, :]], axis=1
        )
        decay = jnp.exp2(ahead - jnp.concatenate([cum_1, cum_2], axis=1) + bias_2)
        m = inner_2 * decay
        x, slope = silu_and_slope(conv_ref[:, cols].astype(F32))
        dt_p = pair_of(first, dt, pair)
        xd = x * dt_p
        grad = grad_ref[:, cols].astype(F32)
        grad_two = stacked(first, grad_ref[:, cols].astype(BF16))
        dm = mm_t(xd.astype(BF16), grad_two)
        dinner = dinner + dm * decay
        spans = mm((dm * m).astype(BF16), lower_low[...])
        gaps = jnp.sum(jnp.where(strict, spans, 0.0), axis=0, keepdims=True)
        dcum_t[2 * pair : 2 * pair + 1, :] = gaps[:, 0:Q]
        dcum_t[2 * pair + 1 : 2 * pair + 2, :] = gaps[:, Q : 2 * Q]
        dxd = mm(m.astype(BF16), grad_two)
        cum_p = jnp.where(first, cum_1, cum_2)
        last = cum_p[Q - 1 : Q, :]
        tail = jnp.exp2(last - cum_p) * tail_in
        later = dstate[:, cols]
        old_low = states_ref[0, :, cols]
        xt = xd * tail
        from_end = end_all[:, cols]
        dxd = dxd + tail * from_end
        weight = jnp.exp2(cum_p) * keep
        wg = grad * weight
        from_start = start_all[:, cols]
        carry = jnp.exp2(last) * keep[Q - 1 : Q, :]
        carried = jnp.sum(later * old_low.astype(F32), axis=0, keepdims=True) * carry
        red[0:Q, cols] = (dxd * x).astype(BF16)
        red[Q : 2 * Q, cols] = (xt * from_end).astype(BF16)
        red[2 * Q : 3 * Q, cols] = (wg * from_start).astype(BF16)
        red[3 * Q : 3 * Q + 16, cols] = jnp.broadcast_to(carried, (16, 128)).astype(BF16)
        wg_low = wg.astype(BF16)
        wgrad[:, cols] = wg_low
        xtail[:, cols] = xt.astype(BF16)
        dx = dxd * dt_p + skip_of(first[0:1], heads_ref, pair) * grad
        dbuf[0:Q, cols] = dx * slope
        inner_acc[40:48, cols] += folded(grad * x)

    sums = mm(red[...], to_head[...])
    spread = jnp.concatenate([(row > column).astype(BF16), (row <= column).astype(BF16)], axis=1)
    dla = dcum_t[...].T + mm(spread, sums[Q : 3 * Q, :].astype(BF16)) + sums[3 * Q : 3 * Q + 1, :]
    rate = heads_ref[1:2, :]
    ddt = sums[0:Q, :] + rate * dla
    dstep = ddt * (0.5 + 0.5 * jnp.tanh(0.5 * raw))
    low_ref[:, width + 2 * NS : width + 2 * NS + 128] = dstep.astype(BF16)
    heads_sum[0:1, :] += jnp.sum(dstep, axis=0, keepdims=True)
    heads_sum[1:2, :] += jnp.sum(dla * dt * rate, axis=0, keepdims=True)

    dinner = dinner[:, 0:Q] + dinner[:, Q : 2 * Q]
    dinner_low = dinner.astype(BF16)
    db = mm(dinner_low, c_low) + mm_t(xtail[...], later_low)
    dc = mm(dinner.T.astype(BF16), b_low) + mm_t(wgrad[...], states_ref[0])
    dsbuf[0:Q, 0:NS] = db * b_slope
    dsbuf[0:Q, NS : 2 * NS] = dc * c_slope

    def conv_back(u, buf, taps_ref, acc, cols):
        weights = taps_ref[:, cols].astype(F32)
        d = buf[0:Q, cols]
        du = weights[3:4] * d
        acc[24:32, cols] += folded(d * u)
        acc[32:40, cols] += folded(d)
        for shift in range(1, 4):
            d = buf[shift : Q + shift, cols] * same[shift - 1]
            du = du + weights[3 - shift : 4 - shift] * d
            acc[24 - 8 * shift : 32 - 8 * shift, cols] += folded(d * u)
        return du

    for part in range(2):
        cols = slice(NS * part, NS * part + NS)
        low_ref[:, width + NS * part : width + NS * part + NS] = conv_back(
            s_ref[:, cols].astype(F32), dsbuf, shared_ref, shared_acc, cols
        ).astype(BF16)
    new = mm(c_turn, wgrad[...])
    for pair in range(width // 128):
        cols = slice(128 * pair, 128 * pair + 128)
        low_ref[:, cols] = conv_back(
            u_ref[:, cols].astype(F32), dbuf, inner_ref, inner_acc, cols
        ).astype(BF16)
        cum_p = jnp.where(
            first[0:1, :],
            jnp.broadcast_to(cum[Q - 1 : Q, 2 * pair : 2 * pair + 1], (1, 128)),
            jnp.broadcast_to(cum[Q - 1 : Q, 2 * pair + 1 : 2 * pair + 2], (1, 128)),
        )
        carry = jnp.exp2(cum_p) * keep[Q - 1 : Q, :]
        dstate[:, cols] = dstate[:, cols] * carry + new[:, cols]

    @pl.when(chunk == pl.num_programs(0) - 1)
    def _():
        for out, acc, count in ((inner_sum, inner_acc, 6), (shared_sum, shared_acc, 5)):
            out[...] = jnp.zeros_like(out)
            for k in range(count):
                out[k : k + 1, :] = jnp.sum(acc[8 * k : 8 * k + 8, :], axis=0, keepdims=True)


VMEM_LIMIT = 32 * 1024 * 1024


def forward_mix(turn, proj, aux, seg_rows, inner_p, inner_b, shared_p, shared_b, heads_p):
    length = proj.shape[0]
    width = inner_p.shape[1]
    chunks = length // Q

    def rows(n, at=0):
        return pl.BlockSpec((Q, n), lambda c, turn: (lax.rem(c + turn[0], chunks), at))

    def plain(n):
        return pl.BlockSpec((Q, n), lambda c, turn: (c, 0))

    def whole(n, rows=8):
        return pl.BlockSpec((rows, n), lambda c, turn: (0, 0))

    line = pl.BlockSpec((1, 1, Q), lambda c, turn: (c, 0, 0))
    kept = pl.BlockSpec((1, NS, width), lambda c, turn: (c, 0, 0))
    return pl.pallas_call(
        forward_kernel,
        grid_spec=pltpu.PrefetchScalarGridSpec(
            num_scalar_prefetch=1,
            grid=(chunks,),
            in_specs=[
                rows(width), rows(2 * NS, width // (2 * NS)), rows(128, (width + 2 * NS) // 128),
                plain(16), line, whole(width, 4), whole(width, 1), whole(2 * NS, 4),
                whole(2 * NS, 1), whole(128),
            ],
            out_specs=[
                rows(width), plain(width), plain(2 * NS), kept,
                pl.BlockSpec((1, 3, Q, 128), lambda c, turn: (c, 0, 0, 0)),
            ],
            scratch_shapes=[
                pltpu.VMEM((Q + 8, width), F32),
                pltpu.VMEM((Q + 8, 2 * NS), F32),
                pltpu.VMEM((NS, width), F32),
                pltpu.VMEM((Q, width), BF16),
            ],
        ),
        out_shape=[
            jax.ShapeDtypeStruct((length, width), BF16),
            pltpu.HBM((length, width), BF16),
            pltpu.HBM((length, 2 * NS), F32),
            pltpu.HBM((chunks, NS, width), BF16),
            pltpu.HBM((chunks, 3, Q, 128), F32),
        ],
        compiler_params=pltpu.CompilerParams(vmem_limit_bytes=VMEM_LIMIT),
        cost_estimate=pl.CostEstimate(
            flops=32 * length * 128 * width, bytes_accessed=12 * length * width, transcendentals=0
        ),
        name="mix_forward",
    )(turn, proj, proj, proj, aux, seg_rows, inner_p, inner_b, shared_p, shared_b, heads_p)


def backward_mix(turn, proj, conv, convs, steps, aux, seg_rows, grad, states, inner_p, shared_p, heads_p):
    length = proj.shape[0]
    width = inner_p.shape[1]
    chunks = length // Q

    def rows(n, at=0):
        return pl.BlockSpec(
            (Q, n), lambda c, turn: (lax.rem(chunks - 1 - c + turn[0], chunks), at)
        )

    def plain(n):
        return pl.BlockSpec((Q, n), lambda c, turn: (chunks - 1 - c, 0))

    def whole(n, rows=8):
        return pl.BlockSpec((rows, n), lambda c, turn: (0, 0))

    line = pl.BlockSpec((1, 1, Q), lambda c, turn: (chunks - 1 - c, 0, 0))
    kept = pl.BlockSpec((1, NS, width), lambda c, turn: (chunks - 1 - c, 0, 0))
    return pl.pallas_call(
        backward_kernel,
        grid_spec=pltpu.PrefetchScalarGridSpec(
            num_scalar_prefetch=1,
            grid=(chunks,),
            in_specs=[
                rows(width), rows(2 * NS, width // (2 * NS)), plain(width), plain(2 * NS),
                rows(128, (width + 2 * NS) // 128),
                pl.BlockSpec((1, 3, Q, 128), lambda c, turn: (chunks - 1 - c, 0, 0, 0)),
                plain(16), line, rows(width), kept,
                whole(width, 4), whole(2 * NS, 4), whole(128),
            ],
            out_specs=[rows(width + 2 * NS + 128), whole(width), whole(2 * NS), whole(128)],
            scratch_shapes=[
                pltpu.VMEM((Q + 8, width), F32),
                pltpu.VMEM((Q + 8, 2 * NS), F32),
                pltpu.VMEM((NS, width), F32),
                pltpu.VMEM((128, Q), F32),
                pltpu.VMEM((3 * Q + 16, width), BF16),
                pltpu.VMEM((Q, width), BF16),
                pltpu.VMEM((Q, width), BF16),
                pltpu.VMEM((width, 128), BF16),
                pltpu.VMEM((2 * Q, 2 * Q), BF16),
                pltpu.VMEM((48, width), F32),
                pltpu.VMEM((48, 2 * NS), F32),
            ],
        ),
        out_shape=[
            jax.ShapeDtypeStruct((length, width + 2 * NS + 128), BF16),
            jax.ShapeDtypeStruct((8, width), F32),
            jax.ShapeDtypeStruct((8, 2 * NS), F32),
            jax.ShapeDtypeStruct((8, 128), F32),
        ],
        compiler_params=pltpu.CompilerParams(vmem_limit_bytes=VMEM_LIMIT),
        cost_estimate=pl.CostEstimate(
            flops=70 * length * 128 * width, bytes_accessed=20 * length * width, transcendentals=0
        ),
        name="mix_backward",
    )(turn, proj, proj, conv, convs, proj, steps, aux, seg_rows, grad, states, inner_p, shared_p, heads_p)


def aux_of(seg_line):
    length = seg_line.shape[0]
    ends = seg_line.reshape(-1, Q)[:, Q - 1]
    prior = jnp.concatenate([jnp.full((1,), -1, seg_line.dtype), ends[:-1]])
    place = jnp.arange(length)
    columns = []
    for shift in range(1, 4):
        columns.append((jnp.roll(seg_line, shift) == seg_line) & (place >= shift))
    for shift in range(1, 4):
        columns.append((jnp.roll(seg_line, -shift) == seg_line) & (place < length - shift))
    columns.append(seg_line == jnp.repeat(prior, Q))
    columns.append(seg_line == jnp.repeat(ends, Q))
    columns = [column.astype(F32) for column in columns] + [seg_line.astype(F32)]
    columns += [jnp.zeros((length,), F32)] * (16 - len(columns))
    rows = seg_line.astype(F32).reshape(-1, 1, Q)
    return jnp.stack(columns, axis=1), rows


def program(sizes, args):
    (
        hidden, norm_gain, weight_gate, weight_inner, weight_shared, weight_step,
        filter_inner, bias_inner, filter_shared, bias_shared, step_bias, log_rate, skip_gain,
        gate_gain, weight_out, segments, cotangent,
    ) = args
    n_fsdp, n_tp = sizes
    width = weight_gate.shape[1]
    heads = weight_step.shape[1]
    own_rows = hidden.shape[0]
    length = segments.shape[1]
    tp_place = lax.axis_index("tp")
    paired = n_tp == 2

    def tp_rows(own):
        if paired:
            return jnp.concatenate([own, lax.ppermute(own, "tp", [(0, 1), (1, 0)])], axis=0)
        return lax.all_gather(own, "tp", axis=0, tiled=True)

    def tp_scatter(make):
        if paired:
            away = make(slice(own_rows, 2 * own_rows)).astype(BF16)
            got = lax.ppermute(away, "tp", [(0, 1), (1, 0)])
            return make(slice(0, own_rows)), got
        return lax.psum_scatter(make(slice(None)), "tp", scatter_dimension=0, tiled=True), 0.0

    fsdp_place = lax.axis_index("fsdp")
    outer = n_fsdp // 2
    digits = [(4, n_fsdp // 4), (outer // 4, 2), (2, 1)] if outer % 4 == 0 else [(outer, 2), (2, 1)]

    def stage(blocks, axis):
        size, stride = digits[axis]
        place = lax.rem(fsdp_place // stride, size)
        parts = [blocks]
        for step in range(1, size):
            moves = []
            for i in range(n_fsdp):
                at = (i // stride) % size
                moves.append((i, i + ((at + step) % size - at) * stride))
            parts.append(lax.ppermute(blocks, "fsdp", moves))
        if size == 2:
            own, away = parts
            return jnp.where(
                place == 0,
                jnp.stack([own, away], axis=axis),
                jnp.stack([away, own], axis=axis),
            )
        if size > 2:
            ring = jnp.stack(parts[::-1] + parts[::-1], axis=axis)
            return lax.dynamic_slice_in_dim(ring, size - 1 - place, size, axis)
        return jnp.expand_dims(blocks, axis)

    def line_gather(shard):
        blocks = shard
        for axis in range(len(digits)):
            blocks = stage(blocks, axis)
        return blocks.reshape(n_fsdp * shard.shape[0], shard.shape[1])

    even = lax.rem(fsdp_place, 2) == 0

    def core_halves(total):
        blocks = total.reshape(outer, 2, total.shape[0] // n_fsdp, total.shape[1])
        away = jnp.where(even, blocks[:, 1], blocks[:, 0])
        return away, jnp.where(even, blocks[:, 0], blocks[:, 1])

    def core_sum(total):
        away, mine = core_halves(total)
        got = lax.ppermute(away, "fsdp", other_core)
        return (mine.astype(F32) + got.astype(F32)).astype(BF16).reshape(-1, total.shape[1])

    other_core = [(i, i ^ 1) for i in range(n_fsdp)]

    def chip_swap(half):
        groups = [[i for i in range(n_fsdp) if i % 2 == core] for core in range(2)]
        return lax.all_to_all(half, "fsdp", 0, 0, axis_index_groups=groups, tiled=True)

    def chip_sum(swapped):
        return jnp.sum(swapped.reshape(outer, -1, swapped.shape[1]).astype(F32), axis=0)

    pad = jnp.zeros((weight_step.shape[0], 128 - heads - 1), BF16)
    shard_a = jnp.concatenate(
        [weight_inner, weight_shared, weight_step, norm_gain[:, None], pad], axis=1
    )
    hidden_all = tp_rows(hidden)
    next_chip = [(i, i ^ 2) for i in range(n_fsdp)]
    lower_line = lax.rem(fsdp_place // 2, 2) == 0

    def swapped(flag, one, two):
        return jnp.where(flag, jnp.stack([one, two], axis=1), jnp.stack([two, one], axis=1))

    def weave(near, near_core, far, far_core):
        both = swapped(lower_line, swapped(even, near, near_core), swapped(even, far, far_core))
        return both.reshape(-1, near.shape[-1])

    if len(digits) == 3 and digits[1][0] == 2:
        line_a = stage(shard_a, 0)
        core_a = lax.ppermute(line_a, "fsdp", other_core)
        next_a = lax.ppermute(line_a, "fsdp", next_chip)
        next_core_a = lax.ppermute(next_a, "fsdp", other_core)
        weights_a = weave(line_a, core_a, next_a, next_core_a)
    else:
        weights_a = line_gather(shard_a)
    woven = len(digits) == 3 and digits[1][0] == 2
    if woven:
        shard_b = jnp.concatenate([weight_gate, weight_out], axis=1)
        size, span = digits[0]
        circles = [[i + span * step for step in range(size)] for i in range(span)]
        line = lax.all_to_all(
            jnp.broadcast_to(shard_b[None], (size,) + shard_b.shape), "fsdp", 0, 0,
            axis_index_groups=circles, tiled=True)
        line_core = lax.ppermute(line, "fsdp", other_core)
        next_line = lax.ppermute(line, "fsdp", next_chip)
    else:
        gate_all, out_all = line_gather(weight_gate), line_gather(weight_out)
    if paired:
        late_cot, hidden_all = lax.optimization_barrier((cotangent, hidden_all))
        cot_got = lax.ppermute(late_cot, "tp", [(0, 1), (1, 0)])
    else:
        cot_got = lax.all_gather(cotangent, "tp", axis=0, tiled=True)
    gain_row = weights_a[:, width + 2 * NS + heads].astype(F32)[None, :]

    hidden_f = hidden_all.astype(F32)
    inv_rms = lax.rsqrt(jnp.mean(hidden_f * hidden_f, axis=1, keepdims=True) + EPSILON)
    normed = (hidden_f * inv_rms * gain_row).astype(BF16)
    normed = lax.optimization_barrier(normed)
    proj = mm(normed, weights_a).astype(BF16)

    turn = (tp_place * (own_rows // Q) if paired else jnp.zeros((), jnp.int32)).reshape(1)
    turn = turn.astype(jnp.int32)
    aux, seg_rows = aux_of(segments[0])
    heads_p = jnp.pad(
        jnp.stack(
            [step_bias.astype(F32), -jnp.exp(log_rate.astype(F32)), skip_gain.astype(F32)]
        ),
        ((0, 5), (0, 128 - heads)),
    )
    y, conv, convs, states, steps = forward_mix(
        turn, proj, aux, seg_rows, filter_inner, bias_inner[None], filter_shared,
        bias_shared[None], heads_p,
    )

    if woven:
        y, next_line, cot_got, line, line_core = lax.optimization_barrier(
            (y, next_line, cot_got, line, line_core)
        )
        next_core = lax.ppermute(next_line, "fsdp", other_core)
        pieces = (line, line_core, next_line, next_core)
        gate_all, out_all = (
            weave(*[piece[:, :, at : at + width] for piece in pieces]) for at in (0, width)
        )
    else:
        y, gate_all, out_all, cot_got = lax.optimization_barrier((y, gate_all, out_all, cot_got))
    cot_all = jnp.concatenate([cotangent, cot_got], axis=0) if paired else cot_got
    gate_z = mm(normed, gate_all).astype(BF16).astype(F32)
    grad_gated = mm(cot_all, out_all).astype(BF16).astype(F32)
    y = y.astype(F32)
    gain_gate = gate_gain.astype(F32)[None, :]
    sig = jax.nn.sigmoid(gate_z)
    act = gate_z * sig
    mixed = y * act
    scaled = grad_gated * gain_gate
    sums = jnp.stack([jnp.sum(mixed * mixed, axis=1), jnp.sum(mixed * scaled, axis=1)], axis=1)
    if paired:
        half = jnp.concatenate([sums[own_rows:], sums[:own_rows]], axis=0)
        sums = sums + lax.ppermute(half, "tp", [(0, 1), (1, 0)])
    else:
        sums = lax.psum(sums, "tp")
    inv_gate = lax.rsqrt(sums[:, 0:1] / INNER + EPSILON)
    gated = (mixed * inv_gate * gain_gate).astype(BF16)
    grad_mixed = inv_gate * scaled - mixed * (inv_gate * inv_gate * inv_gate) * (
        sums[:, 1:2] / INNER
    )
    grad_y = grad_mixed * act
    low_z = (grad_mixed * y * (sig + act * (1.0 - sig))).astype(BF16)
    grad_gain_gate = jnp.sum(grad_gated * mixed * inv_gate, axis=0)
    grad_y, low_z, gated = lax.optimization_barrier((grad_y.astype(BF16), low_z, gated))
    half_b = jnp.concatenate(
        [core_sum(weight_grad(normed, low_z).astype(BF16)),
         core_sum(weight_grad(cot_all, gated).astype(BF16))], axis=1)
    out_own, out_got = tp_scatter(lambda at: mm_t(gated[at], out_all))
    half_b, grad_y, out_own = lax.optimization_barrier((half_b, grad_y, out_own))
    swap_b = chip_swap(half_b)
    low, inner_sum, shared_sum, heads_sum = backward_mix(
        turn, proj, conv, convs, steps, aux, seg_rows, grad_y, states, filter_inner,
        filter_shared, heads_p
    )
    small = jnp.concatenate(
        [jnp.concatenate([inner_sum[:6], grad_gain_gate[None], inner_sum[7:]], axis=0),
         shared_sum, heads_sum], axis=1)
    reach = 1
    while reach < n_fsdp:
        small = small + lax.ppermute(small, "fsdp", [(i, i ^ reach) for i in range(n_fsdp)])
        reach *= 2
    low, out_got = lax.optimization_barrier((low, out_got))
    grads_a = weight_grad(normed, low).astype(BF16)
    def input_rows(at):
        return mm_t(low_z[at], gate_all) + mm_t(low[at], weights_a)

    away_a, mine_a = core_halves(grads_a)
    away_a, mine_a, swap_b = lax.optimization_barrier((away_a, mine_a, swap_b))
    away_a = lax.ppermute(away_a, "fsdp", other_core)
    if paired:
        away_part = input_rows(slice(own_rows, 2 * own_rows)).astype(BF16)
    else:
        away_part = input_rows(slice(None))
    if paired:
        part_got = lax.ppermute(away_part, "tp", [(0, 1), (1, 0)]).astype(F32)
        part_own = input_rows(slice(0, own_rows))
    else:
        part_own = lax.psum_scatter(away_part, "tp", scatter_dimension=0, tiled=True)
        part_got = 0.0
    half_a = (mine_a.astype(F32) + away_a.astype(F32)).astype(BF16).reshape(-1, low.shape[1])
    swap_a = chip_swap(half_a)
    layer_out = (hidden.astype(F32) + out_own + out_got).astype(BF16)
    grad_normed = part_own + part_got
    x_hat = hidden.astype(F32) * inv_rms[:own_rows] if paired else None
    inv_own = inv_rms[:own_rows]
    if not paired:
        inv_own = lax.dynamic_slice_in_dim(inv_rms, tp_place * own_rows, own_rows, 0)
        x_hat = hidden.astype(F32) * inv_own
    scaled_in = grad_normed * gain_row
    grad_hidden = cotangent.astype(F32) + inv_own * (
        scaled_in - x_hat * jnp.mean(scaled_in * x_hat, axis=1, keepdims=True)
    )

    def tp_sum(value):
        if paired:
            return value + lax.ppermute(value, "tp", [(0, 1), (1, 0)])
        return lax.psum(value, "tp")

    shared_part = tp_sum(small[:, width : width + 2 * NS])
    early = (
        grad_hidden,
        layer_out,
        small[0:4, :width],
        small[4, :width],
        shared_part[0:4],
        shared_part[4],
        small[0, width + 2 * NS : width + 2 * NS + heads],
        small[1, width + 2 * NS : width + 2 * NS + heads],
        jnp.sum(small[5, :width].reshape(heads, HEAD), axis=1),
        small[6, :width],
    )
    swap_a, early = lax.optimization_barrier((swap_a, early))
    owned_a, owned_b = chip_sum(swap_a), chip_sum(swap_b)
    grad_gate, grad_out = owned_b[:, :width], owned_b[:, width:]
    grad_inner = owned_a[:, :width]
    grad_shared = owned_a[:, width : width + 2 * NS]
    grad_step = owned_a[:, width + 2 * NS : width + 2 * NS + heads]
    gain_own = (
        jnp.sum(weight_gate.astype(F32) * grad_gate, axis=1)
        + jnp.sum(weight_inner.astype(F32) * grad_inner, axis=1)
        + jnp.sum(weight_shared.astype(F32) * grad_shared, axis=1)
        + jnp.sum(weight_step.astype(F32) * grad_step, axis=1)
    )
    packed = jnp.concatenate(
        [grad_shared, jnp.pad(gain_own[None], ((0, 7), (0, 2 * NS - gain_own.shape[0])))], axis=0
    )
    packed = tp_sum(packed)
    owned = grad_shared.shape[0]
    grad_norm_gain = packed[owned, : gain_own.shape[0]] / norm_gain.astype(F32)
    return (
        early[1],
        early[0],
        grad_norm_gain,
        grad_gate,
        grad_inner,
        packed[:owned],
        grad_step,
        *early[2:],
        grad_out,
    )


def solution(mesh):
    sizes = (mesh.shape["fsdp"], mesh.shape["tp"])

    def per_device(*args):
        return program(sizes, args)

    return jax.shard_map(
        per_device,
        mesh=mesh,
        in_specs=(
            P(("fsdp", "tp"), None),
            P("fsdp"),
            P("fsdp", "tp"),
            P("fsdp", "tp"),
            P("fsdp", None),
            P("fsdp", "tp"),
            P(None, "tp"),
            P("tp"),
            P(),
            P(),
            P("tp"),
            P("tp"),
            P("tp"),
            P("tp"),
            P("fsdp", "tp"),
            P("fsdp", None),
            P(("fsdp", "tp"), None),
        ),
        out_specs=(
            P(("fsdp", "tp"), None),
            P(("fsdp", "tp"), None),
            P("fsdp"),
            P("fsdp", "tp"),
            P("fsdp", "tp"),
            P("fsdp", None),
            P("fsdp", "tp"),
            P(None, "tp"),
            P("tp"),
            P(),
            P(),
            P("tp"),
            P("tp"),
            P("tp"),
            P("tp"),
            P("fsdp", "tp"),
        ),
        check_vma=False,
    )
```
